32 devices in a mesh: expert: 16 (over z, y, x), tensor: 2 (over core).
Axes of the slice: x: 2, y: 2, z: 4, core: 2. Of those that a mesh axis runs over, the one named last changes fastest.
Arguments:
- batch_one: bfloat16 [2048, 1536], P(('expert', 'tensor')), may hold values from -6 to 6
- batch_two: bfloat16 [2048, 1536], P(('expert', 'tensor')), may hold values from -6 to 6
- norm_gain: bfloat16 [1536], replicated, may hold values from 0.25 to 1.75
- slots_one: int32 [2048, 8], P(('expert', 'tensor')), may hold values from 0 to 15, all different within a row; in each aligned block of 64 rows (0 to 63, 64 to 127, ...) at most 36 rows name the same one
- slots_two: int32 [2048, 8], P(('expert', 'tensor')), may hold values from 0 to 15, all different within a row; in each aligned block of 64 rows (0 to 63, 64 to 127, ...) at most 36 rows name the same one
- gates_one: float32 [2048, 8], P(('expert', 'tensor')), may hold values from 0.2 to 1
- gates_two: float32 [2048, 8], P(('expert', 'tensor')), may hold values from 0.2 to 1
- table_old: int32 [16], replicated, may hold values from 0 to 39, as said below
- table_new: int32 [16], replicated, may hold values from 0 to 39, as said below
- gate_old: bfloat16 [16, 1536, 512], P('expert', 'tensor'), as said below
- up_old: bfloat16 [16, 1536, 512], P('expert', 'tensor'), as said below
- down_old: bfloat16 [16, 512, 1536], P('expert', None, 'tensor'), as said below
Outputs:
- mixed_one: bfloat16 [2048, 1536], P(('expert', 'tensor'))
- mixed_two: bfloat16 [2048, 1536], P(('expert', 'tensor'))
The draws below stay inside these ranges and needn't reach their ends.
Inputs may be any that keep to these rules, and one draw needn't show every extreme that they name: `slots_one`: the 8 routes of a token name different slots; among the 64 tokens of one device no slot is named by more than 36 routes, a bound that some block reaches. `slots_two`: the 8 routes of a token name different slots; among the 64 tokens of one device no slot is named by more than 36 routes, a bound that some block reaches. `table_old`: when 16 >= 40 every expert is held by at least one slot; several slots may hold the same expert. table_new[s] equals table_old at slot s, s - 1 or s + 1 (modulo 16), and each of the three cases occurs. `gate_old`: slots that hold the same expert under table_old hold equal weights. `up_old`: slots that hold the same expert under table_old hold equal weights. `down_old`: slots that hold the same expert under table_old hold equal weights.
All inputs are finite; a program needn't handle non-finite values.
Results may differ from the reference program's by a relative error of at most 0.0071.
Values may be sent and summed in bfloat16 or wider, within the bound.
No kernel may reach another device: no remote copies, remote signals or barrier semaphores. Data moves between devices by JAX's collectives and lax.ppermute only.
A program may use at most 128 MiB of HBM per device.

```python
import math
import jax
import jax.numpy as jnp
import numpy as np
from jax import lax

D = 1536
FF = 512
EXPERTS = 40
TOPK = 8
TOK = 64
SLOTS = 16
CAP = 36
TOKENS = 2048
N_EXPERT = 16
N_TENSOR = 2


def place_table(key):
    others = jax.random.permutation(jax.random.fold_in(key, 101), EXPERTS - 1).astype(jnp.int32)
    base = jnp.concatenate([jnp.full((1,), EXPERTS - 1, jnp.int32), others])
    if SLOTS > EXPERTS:
        extra = jax.random.randint(jax.random.fold_in(key, 102), (SLOTS - EXPERTS,), 0, EXPERTS - 1).astype(jnp.int32)
        base = jnp.concatenate([base, extra])
    held = base[:SLOTS]
    rest = jax.random.permutation(jax.random.fold_in(key, 103), SLOTS - 1).astype(jnp.int32) + 1
    order = jnp.concatenate([jnp.zeros((1,), jnp.int32), rest])
    return held[order].astype(jnp.int32)


def draw_table_old(key, part):
    return place_table(key)


def draw_table_new(key, part):
    table = place_table(key)
    offset = jax.random.randint(jax.random.fold_in(key, 104), (SLOTS,), -1, 2).astype(jnp.int32)
    offset = offset.at[0].set(-1).at[1].set(1).at[2].set(0)
    where_from = (jnp.arange(SLOTS, dtype=jnp.int32) + offset) % SLOTS
    return table[where_from].astype(jnp.int32)


def expert_weights(key, salt, shape, fan_in):
    table = place_table(key)
    values = jax.random.normal(jax.random.fold_in(key, salt), (EXPERTS,) + shape, jnp.float32) * fan_in ** (-0.5)
    return values[table].astype(jnp.bfloat16)


def draw_gate_old(key, part):
    return expert_weights(key, 201, (D, FF), D)


def draw_up_old(key, part):
    return expert_weights(key, 202, (D, FF), D)


def draw_down_old(key, part):
    return expert_weights(key, 203, (FF, D), FF)


def block_levels(own_key, dims, shards, smallest, top_value):
    factor_of, own = 1.0, jax.random.fold_in(own_key, 6)
    for position, blocks in shards:
        heights = jnp.exp(jax.random.uniform(jax.random.fold_in(own, position), (blocks,), jnp.float32, smallest / len(shards), top_value / len(shards)))
        factor_of = factor_of * jnp.repeat(heights, dims[position] // blocks).reshape([-1 if axis == position else 1 for axis in range(len(dims))])
    return factor_of


def assign_block(stream_key, own, number, rows, count, top, limit, skew):
    sequence = jax.random.permutation(stream_key, count)
    crowded, ordinary = portions_of(count, rows * top, limit, skew, True), portions_of(count, rows * top, limit, skew, False)
    places = jnp.arange(count)

    def named(lengths, rotation):
        used = int((lengths > 0).sum())
        fixed = max(1, used // 4)
        shifted = fixed + (places - fixed + rotation * (used - fixed)) % max(1, count - fixed)
        return jnp.zeros((count,), jnp.int32).at[sequence[jnp.where(places < fixed, places, shifted)]].set(jnp.asarray(lengths, jnp.int32))

    lengths = jnp.where(number % 4 == 0, named(crowded, number // 4), named(ordinary, number - number // 4 - 1))
    mixed = jax.random.permutation(jax.random.fold_in(own, 3), count)
    source_of, receiver = mixed[0:count // 2 * 2:2], mixed[1:count // 2 * 2:2]
    slack = jnp.minimum(lengths[source_of] - 1, limit - lengths[receiver]) // 2
    slack = jnp.where((source_of == sequence[0]) | (receiver == sequence[0]) | (lengths[receiver] == 0), 0, jnp.maximum(slack, 0))
    shifted = jax.random.randint(jax.random.fold_in(own, 4), (count // 2,), 0, 1 << 20) % (slack + 1)
    lengths = lengths.at[source_of].add(-shifted).at[receiver].add(shifted)
    items = jnp.searchsorted(jnp.cumsum(lengths), jnp.arange(rows * top), side="right").astype(jnp.int32)
    grid = items.reshape(top, rows).T
    grid = grid[jax.random.permutation(jax.random.fold_in(own, 1), rows)]
    rotation = jax.random.randint(jax.random.fold_in(own, 2), (rows, 1), 0, top)
    return jnp.take_along_axis(grid, (jnp.arange(top)[None, :] + rotation) % top, axis=1)


def portions_of(count, total, limit, lean, full):
    loads = [(1 << 20) // math.isqrt(rank ** lean) + 1 for rank in range(1, count + 1)]
    largest = limit if full else min(limit, max(-(-total // count), total * loads[0] // sum(loads)))
    least = 1 if total - largest >= count - 1 else 0
    given, spare = [largest] + [least] * (count - 1), total - largest - least * (count - 1)
    while spare > 0:
        candidates = [i for i in range(1, count) if given[i] < largest] or [i for i in range(1, count) if given[i] < limit]
        whole, left = sum([loads[i] for i in candidates]), spare
        for i in candidates:
            addition = min(limit - given[i], max(1, left * loads[i] // whole), spare)
            given[i] = given[i] + addition
            spare = spare - addition
    return np.array(given)


def noise(key, dims, deviation, most, pieces=(), held_as=jnp.bfloat16):
    level = block_levels(key, dims, pieces, -0.22, 0.18) if pieces else 1.0
    values = jax.random.normal(key, dims, jnp.float32) * deviation * level
    return jnp.minimum(jnp.maximum(values, -most), most).astype(held_as)


def setup_inputs(seed: int = 0) -> dict:
    keys = jax.random.split(jax.random.key(seed), 13)
    batch_one = noise(keys[0], (TOKENS, D), 1.0, 6.0, ((0, 32),))
    batch_two = noise(keys[1], (TOKENS, D), 1.0, 6.0, ((0, 32),))
    norm_gain = jnp.clip(1.0 + 0.15 * jax.random.normal(keys[2], (D,), jnp.float32), 0.25, 1.75).astype(jnp.bfloat16)
    slots_one_keys = jax.random.split(jax.random.fold_in(keys[3], 1), TOKENS // TOK)
    slots_one_turns = jax.random.permutation(jax.random.fold_in(keys[3], 3), TOKENS // TOK)
    slots_one = jax.vmap(lambda own, number: assign_block(jax.random.fold_in(keys[3], 2), own, number, TOK, SLOTS, TOPK, CAP, 2))(slots_one_keys, slots_one_turns).reshape((TOKENS, TOPK))
    slots_two_keys = jax.random.split(jax.random.fold_in(keys[4], 1), TOKENS // TOK)
    slots_two_turns = jax.random.permutation(jax.random.fold_in(keys[4], 3), TOKENS // TOK)
    slots_two = jax.vmap(lambda own, number: assign_block(jax.random.fold_in(keys[4], 2), own, number, TOK, SLOTS, TOPK, CAP, 2))(slots_two_keys, slots_two_turns).reshape((TOKENS, TOPK))
    gates_one = jnp.clip(0.2 + 0.8 * jax.random.uniform(keys[5], (TOKENS, TOPK), jnp.float32) ** block_levels(keys[5], (TOKENS, TOPK), ((0, 32),), -0.2, 0.2), 0.2, 1.0)
    gates_two = jnp.clip(0.2 + 0.8 * jax.random.uniform(keys[6], (TOKENS, TOPK), jnp.float32) ** block_levels(keys[6], (TOKENS, TOPK), ((0, 32),), -0.2, 0.2), 0.2, 1.0)
    table_old = draw_table_old(jax.random.fold_in(keys[12], 71), 0)
    table_new = draw_table_new(jax.random.fold_in(keys[12], 71), 0)
    gate_old = draw_gate_old(jax.random.fold_in(keys[12], 71), 0)
    up_old = draw_up_old(jax.random.fold_in(keys[12], 71), 0)
    down_old = draw_down_old(jax.random.fold_in(keys[12], 71), 0)
    return {"batch_one": batch_one, "batch_two": batch_two, "norm_gain": norm_gain, "slots_one": slots_one, "slots_two": slots_two, "gates_one": gates_one, "gates_two": gates_two, "table_old": table_old, "table_new": table_new, "gate_old": gate_old, "up_old": up_old, "down_old": down_old}


EPS = 1e-05

def rms_rows(tokens, norm_gain):
    values = tokens.astype(jnp.float32)
    square = lax.optimization_barrier(jnp.mean(values * values, axis=-1, keepdims=True))
    return (values * lax.rsqrt(square + EPS) * norm_gain.astype(jnp.float32)).astype(jnp.bfloat16)

def source_slots(table_old, table_new):
    group = table_old.shape[0]
    slot_index = jnp.arange(group, dtype=jnp.int32)
    left_table = jnp.roll(table_old, 1)
    picked = jnp.where(table_new == left_table, (slot_index - 1) % group, (slot_index + 1) % group)
    return jnp.where(table_new == table_old, slot_index, picked).astype(jnp.int32)

def expert_mix(normed, route_slots, route_gates, gate_weights, up_weights, down_weights):
    tok_total = normed.shape[0]
    flat_slot = route_slots.reshape(-1)
    flat_gate = route_gates.reshape(-1)
    flat_token = (jnp.arange(flat_slot.shape[0], dtype=jnp.int32) // TOPK).astype(jnp.int32)
    bound = N_EXPERT * N_TENSOR * CAP

    def visit(total, inputs):
        slot_index, gate_slot, up_slot, down_slot = inputs
        chosen = flat_slot == slot_index
        found = jnp.sum(chosen.astype(jnp.int32))
        entry = jnp.nonzero(chosen, size=bound, fill_value=0)[0].astype(jnp.int32)
        valid = jnp.arange(bound, dtype=jnp.int32) < found
        token_ids = flat_token[entry]
        weight = jnp.where(valid, flat_gate[entry], jnp.zeros_like(flat_gate[entry]))
        row_block = normed[token_ids]
        gate_act = jnp.dot(row_block, gate_slot, preferred_element_type=jnp.float32)
        up_act = jnp.dot(row_block, up_slot, preferred_element_type=jnp.float32)
        hidden = (jax.nn.silu(gate_act) * up_act).astype(jnp.bfloat16)
        result = jnp.dot(hidden, down_slot, preferred_element_type=jnp.float32).astype(jnp.bfloat16)
        total = total.at[token_ids].add(weight[:, None] * result.astype(jnp.float32))
        return (total, valid)
    start = jnp.zeros((tok_total, normed.shape[1]), jnp.float32)
    slot_ids = jnp.arange(gate_weights.shape[0], dtype=jnp.int32)
    total, ignored = lax.scan(visit, start, (slot_ids, gate_weights, up_weights, down_weights))
    return total.astype(jnp.bfloat16)

def reference(batch_one, batch_two, norm_gain, slots_one, slots_two, gates_one, gates_two, table_old, table_new, gate_old, up_old, down_old):
    mixed_one = expert_mix(rms_rows(batch_one, norm_gain), slots_one, gates_one, gate_old, up_old, down_old)
    source = source_slots(table_old, table_new)
    mixed_two = expert_mix(rms_rows(batch_two, norm_gain), slots_two, gates_two, gate_old[source], up_old[source], down_old[source])
    return (mixed_one, mixed_two)
```

```python
import jax
import jax.numpy as jnp
from jax import lax
from jax.sharding import PartitionSpec as P

EPS = 1e-05


def rms_rows(tokens, norm_gain):
    values = tokens.astype(jnp.float32)
    square = jnp.mean(values * values, axis=-1, keepdims=True)
    return (values * lax.rsqrt(square + EPS) * norm_gain.astype(jnp.float32)).astype(jnp.bfloat16)


def gather_tensor(shard, axis):
    if lax.axis_size("tensor") != 2:
        return lax.all_gather(shard, "tensor", axis=axis, tiled=True)
    other = lax.ppermute(shard, "tensor", [(0, 1), (1, 0)])
    first = lax.axis_index("tensor") == 0
    return jnp.concatenate(
        [jnp.where(first, shard, other), jnp.where(first, other, shard)], axis=axis
    )


def source_slots(table_old, table_new):
    group = table_old.shape[0]
    slot_index = jnp.arange(group, dtype=jnp.int32)
    picked = jnp.where(
        table_new == jnp.roll(table_old, 1), (slot_index - 1) % group, (slot_index + 1) % group
    )
    return jnp.where(table_new == table_old, slot_index, picked).astype(jnp.int32)


def slot_weights(route_slots, route_gates, held_by):
    group = held_by.shape[0]
    hit = route_slots[:, :, None] == jnp.arange(group, dtype=jnp.int32)
    by_slot = jnp.sum(jnp.where(hit, route_gates[:, :, None], 0.0), axis=1)
    moved = held_by[:, None] == jnp.arange(group, dtype=jnp.int32)
    return jnp.sum(jnp.where(moved[None], by_slot[:, :, None], 0.0), axis=1)


def expert_part(rows, weight, gate_full, up_full, down_full):
    gate_act = jnp.dot(rows, gate_full, preferred_element_type=jnp.float32)
    up_act = jnp.dot(rows, up_full, preferred_element_type=jnp.float32)
    hidden = (jax.nn.silu(gate_act) * up_act).astype(jnp.bfloat16)
    result = jnp.dot(hidden, down_full, preferred_element_type=jnp.float32).astype(jnp.bfloat16)
    return (result.astype(jnp.float32) * weight[:, None]).astype(jnp.bfloat16)


def local(
    batch_one,
    batch_two,
    norm_gain,
    slots_one,
    slots_two,
    gates_one,
    gates_two,
    table_old,
    table_new,
    gate_old,
    up_old,
    down_old,
):
    group = table_old.shape[0]
    me = lax.axis_index("expert")
    gate_full = gather_tensor(gate_old[0], 0)
    up_full = gather_tensor(up_old[0], 0)
    down_full = gather_tensor(down_old[0], 1)
    rows_one = lax.all_gather(rms_rows(batch_one, norm_gain), "expert", axis=0, tiled=True)
    rows_two = lax.all_gather(rms_rows(batch_two, norm_gain), "expert", axis=0, tiled=True)
    own = jnp.arange(group, dtype=jnp.int32)
    weights = jnp.stack(
        [
            slot_weights(slots_one, gates_one, own),
            slot_weights(slots_two, gates_two, source_slots(table_old, table_new)),
        ]
    )
    all_weights = lax.all_gather(weights, "expert", axis=1, tiled=True)
    mine = lax.dynamic_index_in_dim(all_weights, me, axis=2, keepdims=False)
    outs = []
    for rows, weight in ((rows_one, mine[0]), (rows_two, mine[1])):
        part = expert_part(rows, weight, gate_full, up_full, down_full)
        outs.append(lax.psum_scatter(part, "expert", scatter_dimension=0, tiled=True))
    return tuple(outs)


def solution(mesh):
    in_specs = (
        P(("expert", "tensor"), None),
        P(("expert", "tensor"), None),
        P(),
        P(("expert", "tensor"), None),
        P(("expert", "tensor"), None),
        P(("expert", "tensor"), None),
        P(("expert", "tensor"), None),
        P(),
        P(),
        P("expert", "tensor", None),
        P("expert", "tensor", None),
        P("expert", None, "tensor"),
    )
    out_specs = (P(("expert", "tensor"), None), P(("expert", "tensor"), None))
    return jax.shard_map(local, mesh=mesh, in_specs=in_specs, out_specs=out_specs, check_vma=False)
```

```python
import functools

import jax
import jax.numpy as jnp
from jax import lax
from jax.experimental import pallas as pl
from jax.experimental.pallas import tpu as pltpu
from jax.sharding import PartitionSpec as P

EPS = 1e-05
PACK = 128
VMEM_LIMIT = 48 * 1024 * 1024
X, Y, Z_LOW, Z_HIGH = 1, 2, 4, 8


def rms_rows(tokens, norm_gain):
    values = tokens.astype(jnp.float32)
    square = jnp.mean(values * values, axis=-1, keepdims=True)
    return (values * lax.rsqrt(square + EPS) * norm_gain.astype(jnp.float32)).astype(jnp.bfloat16)


def source_slots(table_old, table_new):
    group = table_old.shape[0]
    slot_index = jnp.arange(group, dtype=jnp.int32)
    picked = jnp.where(
        table_new == jnp.roll(table_old, 1), (slot_index - 1) % group, (slot_index + 1) % group
    )
    return jnp.where(table_new == table_old, slot_index, picked).astype(jnp.int32)


def slot_weights(route_slots, route_gates, held_by):
    group = held_by.shape[0]
    hit = route_slots[:, :, None] == jnp.arange(group, dtype=jnp.int32)
    by_slot = jnp.sum(jnp.where(hit, route_gates[:, :, None], 0.0), axis=1)
    moved = held_by[:, None] == jnp.arange(group, dtype=jnp.int32)
    return jnp.sum(jnp.where(moved[None], by_slot[:, :, None], 0.0), axis=1)


def expert_part(rows, weight, gate_full, up_full, down_full):
    gate_act = jnp.dot(rows, gate_full, preferred_element_type=jnp.float32)
    up_act = jnp.dot(rows, up_full, preferred_element_type=jnp.float32)
    hidden = (jax.nn.silu(gate_act) * up_act).astype(jnp.bfloat16)
    result = jnp.dot(hidden, down_full, preferred_element_type=jnp.float32)
    return (result * weight[:, None]).astype(jnp.bfloat16)


def local_any(
    batch_one,
    batch_two,
    norm_gain,
    slots_one,
    slots_two,
    gates_one,
    gates_two,
    table_old,
    table_new,
    gate_old,
    up_old,
    down_old,
):
    group = table_old.shape[0]
    me = lax.axis_index("expert")
    gate_full = lax.all_gather(gate_old[0], "tensor", axis=0, tiled=True)
    up_full = lax.all_gather(up_old[0], "tensor", axis=0, tiled=True)
    down_full = lax.all_gather(down_old[0], "tensor", axis=1, tiled=True)
    rows_one = lax.all_gather(rms_rows(batch_one, norm_gain), "expert", axis=0, tiled=True)
    rows_two = lax.all_gather(rms_rows(batch_two, norm_gain), "expert", axis=0, tiled=True)
    own = jnp.arange(group, dtype=jnp.int32)
    weights = jnp.stack(
        [
            slot_weights(slots_one, gates_one, own),
            slot_weights(slots_two, gates_two, source_slots(table_old, table_new)),
        ]
    )
    all_weights = lax.all_gather(weights, "expert", axis=1, tiled=True)
    mine = lax.dynamic_index_in_dim(all_weights, me, axis=2, keepdims=False)
    outs = []
    for rows, weight in ((rows_one, mine[0]), (rows_two, mine[1])):
        part = expert_part(rows, weight, gate_full, up_full, down_full)
        outs.append(lax.psum_scatter(part, "expert", scatter_dimension=0, tiled=True))
    return tuple(outs)


def call(body, outs, ins, flops=0, moved=0, scratch=()):
    smem = pl.BlockSpec(memory_space=pltpu.SMEM)
    vmem = pl.BlockSpec(memory_space=pltpu.VMEM)
    return pl.pallas_call(
        body,
        out_shape=outs,
        in_specs=[smem if x.ndim == 1 and x.dtype == jnp.int32 else vmem for x in ins],
        out_specs=jax.tree.map(lambda _: vmem, outs),
        scratch_shapes=list(scratch),
        compiler_params=pltpu.CompilerParams(vmem_limit_bytes=VMEM_LIMIT),
        cost_estimate=pl.CostEstimate(flops=flops, bytes_accessed=moved, transcendentals=0),
    )(*ins)


def prepare_kernel(
    source_ref, one_ref, two_ref, gain_ref, slots_one_ref, slots_two_ref, gates_one_ref, gates_two_ref,
    out_one_ref, out_two_ref,
):
    group = source_ref.shape[0]
    gain = gain_ref[...].astype(jnp.float32)
    width = one_ref.shape[1]
    for tokens_ref, slots_ref, gates_ref, out_ref, moved in (
        (one_ref, slots_one_ref, gates_one_ref, out_one_ref, False),
        (two_ref, slots_two_ref, gates_two_ref, out_two_ref, True),
    ):
        values = tokens_ref[...].astype(jnp.float32)
        square = jnp.mean(values * values, axis=-1, keepdims=True)
        out_ref[:, :width] = (values * lax.rsqrt(square + EPS) * gain).astype(jnp.bfloat16)
        slots = slots_ref[...]
        if moved:
            holder = jnp.zeros_like(slots)
            for s in range(group):
                holder = jnp.where(slots == s, source_ref[s], holder)
            slots = holder
        gates = gates_ref[...]
        lane = lax.broadcasted_iota(jnp.int32, (slots.shape[0], PACK), 1)
        expert = lane & (group - 1)
        total = jnp.zeros((slots.shape[0], PACK), jnp.float32)
        for k in range(slots.shape[1]):
            total += jnp.where(expert == slots[:, k : k + 1], gates[:, k : k + 1], 0.0)
        high = total.astype(jnp.bfloat16).astype(jnp.float32)
        rest = total - high
        middle = rest.astype(jnp.bfloat16).astype(jnp.float32)
        low = rest - middle
        piece = lane // group
        packed = jnp.where(
            piece == 0, high, jnp.where(piece == 1, middle, jnp.where(piece == 2, low, 0.0))
        )
        out_ref[:, width:] = packed.astype(jnp.bfloat16)


def hidden_of(place, rows_ref, gate_refs, up_refs, begin, count):
    depth = gate_refs[0].shape[0]
    acts = []
    for refs in (gate_refs, up_refs):
        act = None
        for which, ref in enumerate(refs):
            half = place if which == 0 else 1 - place
            columns = pl.ds(pl.multiple_of(half * depth, depth), depth)
            term = jnp.dot(
                rows_ref[pl.ds(begin, count), columns], ref[...], preferred_element_type=jnp.float32
            )
            act = term if act is None else act + term
        acts.append(act)
    gate_act, up_act = acts
    return (gate_act / (1.0 + jnp.exp(-gate_act)) * up_act).astype(jnp.bfloat16)


def weight_of(expert, group, packed):
    lane = lax.broadcasted_iota(jnp.int32, packed.shape, 1)
    chosen = (lane & (group - 1)) == expert
    return jnp.sum(jnp.where(chosen, packed.astype(jnp.float32), 0.0), axis=1, keepdims=True)


def own_kernel(pieces, group, place_ref, *refs):
    piece_refs, refs = refs[:pieces], refs[pieces:]
    gate_a, gate_b, up_a, up_b, down_a, down_b, total_ref, rows_ref = refs
    tok = piece_refs[0].shape[0]
    width = total_ref.shape[1]
    for i, ref in enumerate(piece_refs):
        rows_ref[i * tok : (i + 1) * tok, :] = ref[...]
    place = place_ref[0]
    block = 256

    @pl.loop(0, rows_ref.shape[0] // block)
    def _(step):
        begin = pl.multiple_of(step * block, block)
        hidden = hidden_of(place, rows_ref, (gate_a, gate_b), (up_a, up_b), begin, block)
        weight = weight_of(place_ref[1], group, rows_ref[pl.ds(begin, block), width:])
        for which, ref in enumerate((down_a, down_b)):
            half = place if which == 0 else 1 - place
            columns = pl.ds(pl.multiple_of(half * ref.shape[1], ref.shape[1]), ref.shape[1])
            part = jnp.dot(hidden, ref[...], preferred_element_type=jnp.float32)
            total_ref[pl.ds(begin, block), columns] = part * weight


def beside_kernel(pieces, group, place_ref, *refs):
    piece_refs, refs = refs[:pieces], refs[pieces:]
    gate_a, gate_b, up_a, up_b, hidden_ref, weight_ref, rows_ref = refs
    tok = piece_refs[0].shape[0]
    width = rows_ref.shape[1] - PACK
    for i, ref in enumerate(piece_refs):
        rows_ref[i * tok : (i + 1) * tok, :] = ref[...]
    block = 256

    @pl.loop(0, rows_ref.shape[0] // block)
    def _(step):
        begin = pl.multiple_of(step * block, block)
        hidden_ref[pl.ds(begin, block), :] = hidden_of(
            place_ref[0], rows_ref, (gate_a, gate_b), (up_a, up_b), begin, block
        )
        weight = weight_of(place_ref[1] ^ Z_LOW, group, rows_ref[pl.ds(begin, block), width:])
        weight_ref[pl.ds(begin, block), :] = jnp.broadcast_to(weight, (block, PACK))


def join_kernel(place_ref, hidden_ref, weight_ref, total_ref, down_a, down_b, send_a, send_b, keep_a, keep_b):
    place = place_ref[0]
    count = send_a.shape[0]
    for pair, outs in ((0, (send_a, send_b)), (1, (keep_a, keep_b))):
        rows = slice(pair * 2 * count, (pair + 1) * 2 * count)
        weight = weight_ref[rows, :1]
        for which, ref in enumerate((down_a, down_b)):
            half = place if which == 0 else 1 - place
            columns = pl.ds(pl.multiple_of(half * ref.shape[1], ref.shape[1]), ref.shape[1])
            part = jnp.dot(hidden_ref[rows, :], ref[...], preferred_element_type=jnp.float32)
            part = part * weight + total_ref[rows, columns]
            outs[0][:, columns] = part[:count].astype(outs[0].dtype)
            outs[1][:, columns] = part[count:].astype(outs[1].dtype)


def first_sum_kernel(keep_ref, got_ref, send_ref, held_ref):
    half = held_ref.shape[0]
    held_ref[...] = keep_ref[:half] + got_ref[:half].astype(jnp.float32)
    send_ref[...] = (keep_ref[half:] + got_ref[half:].astype(jnp.float32)).astype(jnp.bfloat16)


def second_sum_kernel(keep_a, got_a, keep_b, got_b, send_ref, held_ref):
    half = keep_a.shape[0] // 2
    for i, (keep, got) in enumerate(((keep_a, got_a), (keep_b, got_b))):
        rows = slice(i * half, (i + 1) * half)
        held_ref[rows, :] = keep[:half] + got[:half].astype(jnp.float32)
        send_ref[rows, :] = (keep[half:] + got[half:].astype(jnp.float32)).astype(jnp.bfloat16)


def last_sum_kernel(keep_ref, got_ref, out_ref):
    out_ref[...] = (keep_ref[...] + got_ref[...].astype(jnp.float32)).astype(jnp.bfloat16)


def swap(block, distance):
    count = lax.axis_size("expert")
    return lax.ppermute(block, "expert", [(i, i ^ distance) for i in range(count)])


def swap_core(block):
    return lax.ppermute(block, "tensor", [(0, 1), (1, 0)])


def spread(own):
    half = own.shape[0] // 2
    far = swap(own, Z_HIGH)
    a1 = jnp.concatenate([own[:half], far[:half]])
    b1 = jnp.concatenate([own[half:], far[half:]])
    a2, b2 = swap(a1, X), swap(b1, Y)
    a3, b3 = swap(a1, Y), swap(b1, X)
    a4, b4 = swap(a2, Y), swap(b2, X)
    return [a3, a4, b3, b4, a1, a2, b1, b2]


def send_back(send_a, send_b, keep_a, keep_b):
    quarter, width = keep_a.shape[0] // 2, keep_a.shape[1]
    bf = jax.ShapeDtypeStruct((quarter, width), jnp.bfloat16)
    f32 = jax.ShapeDtypeStruct((quarter, width), jnp.float32)
    size = quarter * width
    got_a, got_b = swap(send_a, Y), swap(send_b, X)
    next_a, held_a = call(first_sum_kernel, (bf, f32), (keep_a, got_a), size, 18 * size)
    next_b, held_b = call(first_sum_kernel, (bf, f32), (keep_b, got_b), size, 18 * size)
    got_a, got_b = swap(next_a, X), swap(next_b, Y)
    next_z, held_z = call(
        second_sum_kernel, (bf, f32), (held_a, got_a, held_b, got_b), size, 18 * size
    )
    got_z = swap(next_z, Z_HIGH)
    return call(last_sum_kernel, bf, (held_z, got_z), size, 8 * size)


def local_pairs(
    batch_one,
    batch_two,
    norm_gain,
    slots_one,
    slots_two,
    gates_one,
    gates_two,
    table_old,
    table_new,
    gate_old,
    up_old,
    down_old,
):
    group = table_old.shape[0]
    tok, width = batch_one.shape
    place = jnp.stack([lax.axis_index("tensor"), lax.axis_index("expert")]).astype(jnp.int32)
    mine = (gate_old[0], up_old[0], down_old[0])
    own = call(
        prepare_kernel,
        (jax.ShapeDtypeStruct((tok, width + PACK), jnp.bfloat16),) * 2,
        (
            source_slots(table_old, table_new),
            batch_one,
            batch_two,
            norm_gain.reshape(1, width),
            slots_one,
            slots_two,
            gates_one,
            gates_two,
        ),
        10 * tok * width,
        8 * tok * width,
    )
    twins = tuple(swap_core(w) for w in mine)
    beside = tuple(swap(w, Z_LOW) for w in mine)
    beside_twins = tuple(swap_core(w) for w in beside)
    ff = gate_old.shape[2]
    rows = 8 * tok
    pieces = [spread(x) for x in own]
    scratch = (pltpu.VMEM((rows, width + PACK), jnp.bfloat16),)
    totals = [
        call(
            functools.partial(own_kernel, 8, group),
            jax.ShapeDtypeStruct((rows, width), jnp.float32),
            (place, *p, mine[0], twins[0], mine[1], twins[1], mine[2], twins[2]),
            6 * rows * width * ff,
            6 * width * ff + 6 * rows * width,
            scratch,
        )
        for p in pieces
    ]
    hidden = [
        call(
            functools.partial(beside_kernel, 8, group),
            (
                jax.ShapeDtypeStruct((rows, ff), jnp.bfloat16),
                jax.ShapeDtypeStruct((rows, PACK), jnp.float32),
            ),
            (place, *p, beside[0], beside_twins[0], beside[1], beside_twins[1]),
            4 * rows * width * ff,
            4 * width * ff + 2 * rows * width,
            scratch,
        )
        for p in pieces
    ]
    outs = []
    for total, (hid, weight) in zip(totals, hidden):
        parts = call(
            join_kernel,
            (jax.ShapeDtypeStruct((2 * tok, width), jnp.bfloat16),) * 2
            + (jax.ShapeDtypeStruct((2 * tok, width), jnp.float32),) * 2,
            (place, hid, weight, total, beside[2], beside_twins[2]),
            2 * rows * width * ff,
            2 * width * ff + 8 * rows * width,
        )
        outs.append(send_back(*parts))
    return tuple(outs)


def solution(mesh):
    in_specs = (
        P(("expert", "tensor"), None),
        P(("expert", "tensor"), None),
        P(),
        P(("expert", "tensor"), None),
        P(("expert", "tensor"), None),
        P(("expert", "tensor"), None),
        P(("expert", "tensor"), None),
        P(),
        P(),
        P("expert", "tensor", None),
        P("expert", "tensor", None),
        P("expert", None, "tensor"),
    )
    out_specs = (P(("expert", "tensor"), None), P(("expert", "tensor"), None))
    local = local_pairs if (mesh.shape["expert"], mesh.shape["tensor"]) == (16, 2) else local_any
    return jax.shard_map(local, mesh=mesh, in_specs=in_specs, out_specs=out_specs, check_vma=False)
```

```python
import functools

import jax
import jax.numpy as jnp
from jax import lax
from jax.experimental import pallas as pl
from jax.experimental.pallas import tpu as pltpu
from jax.sharding import PartitionSpec as P

EPS = 1e-05
PACK = 128
X, Y, Z_LOW, Z_HIGH = 1, 2, 4, 8


def rms_rows(tokens, norm_gain):
    values = tokens.astype(jnp.float32)
    square = jnp.mean(values * values, axis=-1, keepdims=True)
    return (values * lax.rsqrt(square + EPS) * norm_gain.astype(jnp.float32)).astype(jnp.bfloat16)


def source_slots(table_old, table_new):
    group = table_old.shape[0]
    slot_index = jnp.arange(group, dtype=jnp.int32)
    picked = jnp.where(
        table_new == jnp.roll(table_old, 1), (slot_index - 1) % group, (slot_index + 1) % group
    )
    return jnp.where(table_new == table_old, slot_index, picked).astype(jnp.int32)


def slot_weights(route_slots, route_gates, held_by):
    group = held_by.shape[0]
    hit = route_slots[:, :, None] == jnp.arange(group, dtype=jnp.int32)
    by_slot = jnp.sum(jnp.where(hit, route_gates[:, :, None], 0.0), axis=1)
    moved = held_by[:, None] == jnp.arange(group, dtype=jnp.int32)
    return jnp.sum(jnp.where(moved[None], by_slot[:, :, None], 0.0), axis=1)


def expert_part(rows, weight, gate_full, up_full, down_full):
    gate_act = jnp.dot(rows, gate_full, preferred_element_type=jnp.float32)
    up_act = jnp.dot(rows, up_full, preferred_element_type=jnp.float32)
    hidden = (jax.nn.silu(gate_act) * up_act).astype(jnp.bfloat16)
    result = jnp.dot(hidden, down_full, preferred_element_type=jnp.float32)
    return (result * weight[:, None]).astype(jnp.bfloat16)


def local_any(
    batch_one,
    batch_two,
    norm_gain,
    slots_one,
    slots_two,
    gates_one,
    gates_two,
    table_old,
    table_new,
    gate_old,
    up_old,
    down_old,
):
    group = table_old.shape[0]
    me = lax.axis_index("expert")
    gate_full = lax.all_gather(gate_old[0], "tensor", axis=0, tiled=True)
    up_full = lax.all_gather(up_old[0], "tensor", axis=0, tiled=True)
    down_full = lax.all_gather(down_old[0], "tensor", axis=1, tiled=True)
    rows_one = lax.all_gather(rms_rows(batch_one, norm_gain), "expert", axis=0, tiled=True)
    rows_two = lax.all_gather(rms_rows(batch_two, norm_gain), "expert", axis=0, tiled=True)
    own = jnp.arange(group, dtype=jnp.int32)
    weights = jnp.stack(
        [
            slot_weights(slots_one, gates_one, own),
            slot_weights(slots_two, gates_two, source_slots(table_old, table_new)),
        ]
    )
    all_weights = lax.all_gather(weights, "expert", axis=1, tiled=True)
    mine = lax.dynamic_index_in_dim(all_weights, me, axis=2, keepdims=False)
    outs = []
    for rows, weight in ((rows_one, mine[0]), (rows_two, mine[1])):
        part = expert_part(rows, weight, gate_full, up_full, down_full)
        outs.append(lax.psum_scatter(part, "expert", scatter_dimension=0, tiled=True))
    return tuple(outs)


def call(body, outs, ins, vmem_mb, flops=0, moved=0, scratch=(), specs=None):
    smem = pl.BlockSpec(memory_space=pltpu.SMEM)
    vmem = pl.BlockSpec(memory_space=pltpu.VMEM)
    return pl.pallas_call(
        body,
        out_shape=outs,
        in_specs=specs
        or [smem if x.ndim == 1 and x.dtype == jnp.int32 else vmem for x in ins],
        out_specs=jax.tree.map(lambda _: vmem, outs),
        scratch_shapes=list(scratch),
        compiler_params=pltpu.CompilerParams(vmem_limit_bytes=vmem_mb * 1024 * 1024),
        cost_estimate=pl.CostEstimate(flops=flops, bytes_accessed=moved, transcendentals=0),
    )(*ins)


def prepare_kernel(old_ref, new_ref, *refs):
    hbm, outs, held, sems = refs[:7], refs[7:9], refs[9:16], refs[16]
    copies = [pltpu.make_async_copy(a, b, sems.at[i]) for i, (a, b) in enumerate(zip(hbm, held))]
    for copy in copies:
        copy.start()
    group = old_ref.shape[0]
    sources = []
    for s in range(group):
        left, right = (s - 1) % group, (s + 1) % group
        wanted = new_ref[s]
        other = jnp.where(wanted == old_ref[left], left, right)
        sources.append(jnp.where(wanted == old_ref[s], s, other))
    for copy in copies:
        copy.wait()
    gain = held[0][...].astype(jnp.float32).reshape(1, -1)
    for b in range(2):
        tokens_ref, slots_ref, gates_ref = held[1 + b], held[3 + b], held[5 + b]
        out_ref = outs[b]
        tok, width = tokens_ref.shape
        values = tokens_ref[...].astype(jnp.float32)
        square = jnp.mean(values * values, axis=-1, keepdims=True)
        out_ref[:, :width] = (values * lax.rsqrt(square + EPS) * gain).astype(jnp.bfloat16)
        slots, gates = slots_ref[...], gates_ref[...]
        if b == 1:
            holder = jnp.zeros_like(slots)
            for s in range(group):
                holder = jnp.where(slots == s, sources[s], holder)
            slots = holder
        expert = lax.broadcasted_iota(jnp.int32, (group, tok), 0)
        total = jnp.zeros((group, tok), jnp.float32)
        for k in range(slots.shape[0]):
            total += jnp.where(expert == slots[k : k + 1, :], gates[k : k + 1, :], 0.0)
        high = total.astype(jnp.bfloat16)
        rest = total - high.astype(jnp.float32)
        middle = rest.astype(jnp.bfloat16)
        low = (rest - middle.astype(jnp.float32)).astype(jnp.bfloat16)
        packed = jnp.concatenate([high, middle, low], axis=0)
        row = lax.broadcasted_iota(jnp.int32, (3 * group, PACK), 0)
        lane = lax.broadcasted_iota(jnp.int32, (3 * group, PACK), 1)
        turned = lax.dot_general(
            packed,
            (row == lane).astype(jnp.bfloat16),
            (((0,), (0,)), ((), ())),
            preferred_element_type=jnp.float32,
        )
        out_ref[:, width:] = turned.astype(jnp.bfloat16)


def hidden_of(place, rows_ref, both_refs, begin, count):
    depth, ff = both_refs[0].shape[0], both_refs[0].shape[1] // 2
    acts = None
    for which, ref in enumerate(both_refs):
        half = place if which == 0 else 1 - place
        columns = pl.ds(pl.multiple_of(half * depth, depth), depth)
        term = jnp.dot(
            rows_ref[pl.ds(begin, count), columns], ref[...], preferred_element_type=jnp.float32
        )
        acts = term if acts is None else acts + term
    gate_act, up_act = acts[:, :ff], acts[:, ff:]
    return (gate_act / (1.0 + jnp.exp(-gate_act)) * up_act).astype(jnp.bfloat16)


def weight_of(expert, group, packed):
    lane = lax.broadcasted_iota(jnp.int32, packed.shape, 1)
    chosen = (lane & (group - 1)) == expert
    return jnp.sum(jnp.where(chosen, packed.astype(jnp.float32), 0.0), axis=1, keepdims=True)


def own_kernel(pieces, group, place_ref, *refs):
    piece_refs, refs = refs[:pieces], refs[pieces:]
    both_a, both_b, down_a, down_b, total_ref, rows_ref = refs
    tok = piece_refs[0].shape[0]
    width = total_ref.shape[1]
    for i, ref in enumerate(piece_refs):
        rows_ref[i * tok : (i + 1) * tok, :] = ref[...]
    place = place_ref[0]
    block = 256

    @pl.loop(0, rows_ref.shape[0] // block)
    def _(step):
        begin = pl.multiple_of(step * block, block)
        hidden = hidden_of(place, rows_ref, (both_a, both_b), begin, block)
        weight = weight_of(place_ref[1], group, rows_ref[pl.ds(begin, block), width:])
        for which, ref in enumerate((down_a, down_b)):
            half = place if which == 0 else 1 - place
            columns = pl.ds(pl.multiple_of(half * ref.shape[1], ref.shape[1]), ref.shape[1])
            part = jnp.dot(hidden, ref[...], preferred_element_type=jnp.float32)
            total_ref[pl.ds(begin, block), columns] = part * weight


def beside_kernel(pieces, group, place_ref, *refs):
    piece_refs, refs = refs[:pieces], refs[pieces:]
    both_a, both_b, hidden_ref, weight_ref, rows_ref = refs
    tok = piece_refs[0].shape[0]
    width = rows_ref.shape[1] - PACK
    for i, ref in enumerate(piece_refs):
        rows_ref[i * tok : (i + 1) * tok, :] = ref[...]
    block = 256

    @pl.loop(0, rows_ref.shape[0] // block)
    def _(step):
        begin = pl.multiple_of(step * block, block)
        hidden_ref[pl.ds(begin, block), :] = hidden_of(
            place_ref[0], rows_ref, (both_a, both_b), begin, block
        )
        weight = weight_of(place_ref[1] ^ Z_LOW, group, rows_ref[pl.ds(begin, block), width:])
        weight_ref[pl.ds(begin, block), :] = jnp.broadcast_to(weight, (block, PACK))


def join_kernel(place_ref, hidden_ref, weight_ref, total_ref, down_a, down_b, send_a, send_b, keep_a, keep_b):
    place = place_ref[0]
    count = send_a.shape[0]
    for pair, outs in ((0, (send_a, send_b)), (1, (keep_a, keep_b))):
        rows = slice(pair * 2 * count, (pair + 1) * 2 * count)
        weight = weight_ref[rows, :1]
        for which, ref in enumerate((down_a, down_b)):
            half = place if which == 0 else 1 - place
            columns = pl.ds(pl.multiple_of(half * ref.shape[1], ref.shape[1]), ref.shape[1])
            part = jnp.dot(hidden_ref[rows, :], ref[...], preferred_element_type=jnp.float32)
            part = part * weight + total_ref[rows, columns]
            outs[0][:, columns] = part[:count].astype(outs[0].dtype)
            outs[1][:, columns] = part[count:].astype(outs[1].dtype)


def first_sum_kernel(keep_ref, got_ref, send_ref, held_ref):
    half = held_ref.shape[0]
    held_ref[...] = keep_ref[:half] + got_ref[:half].astype(jnp.float32)
    send_ref[...] = (keep_ref[half:] + got_ref[half:].astype(jnp.float32)).astype(jnp.bfloat16)


def second_sum_kernel(keep_a, got_a, keep_b, got_b, send_ref, held_ref):
    half = keep_a.shape[0] // 2
    for i, (keep, got) in enumerate(((keep_a, got_a), (keep_b, got_b))):
        rows = slice(i * half, (i + 1) * half)
        held_ref[rows, :] = keep[:half] + got[:half].astype(jnp.float32)
        send_ref[rows, :] = (keep[half:] + got[half:].astype(jnp.float32)).astype(jnp.bfloat16)


def last_sum_kernel(keep_ref, got_ref, out_ref):
    out_ref[...] = (keep_ref[...] + got_ref[...].astype(jnp.float32)).astype(jnp.bfloat16)


def swap(block, distance):
    count = lax.axis_size("expert")
    return lax.ppermute(block, "expert", [(i, i ^ distance) for i in range(count)])


def swap_core(block):
    return lax.ppermute(block, "tensor", [(0, 1), (1, 0)])


def spread(own):
    half = own.shape[0] // 2
    far = swap(own, Z_HIGH)
    a1 = jnp.concatenate([own[:half], far[:half]])
    b1 = jnp.concatenate([own[half:], far[half:]])
    a2, b2 = swap(a1, X), swap(b1, Y)
    a3, b3 = swap(a1, Y), swap(b1, X)
    a4, b4 = swap(a2, Y), swap(b2, X)
    return [a3, a4, b3, b4, a1, a2, b1, b2]


def send_back(send_a, send_b, keep_a, keep_b):
    quarter, width = keep_a.shape[0] // 2, keep_a.shape[1]
    bf = jax.ShapeDtypeStruct((quarter, width), jnp.bfloat16)
    f32 = jax.ShapeDtypeStruct((quarter, width), jnp.float32)
    size = quarter * width
    got_a, got_b = swap(send_a, Y), swap(send_b, X)
    next_a, held_a = call(first_sum_kernel, (bf, f32), (keep_a, got_a), 8, size, 18 * size)
    next_b, held_b = call(first_sum_kernel, (bf, f32), (keep_b, got_b), 8, size, 18 * size)
    got_a, got_b = swap(next_a, X), swap(next_b, Y)
    next_z, held_z = call(
        second_sum_kernel, (bf, f32), (held_a, got_a, held_b, got_b), 8, size, 18 * size
    )
    got_z = swap(next_z, Z_HIGH)
    return call(last_sum_kernel, bf, (held_z, got_z), 8, size, 8 * size)


def local_pairs(
    batch_one,
    batch_two,
    norm_gain,
    slots_one,
    slots_two,
    gates_one,
    gates_two,
    table_old,
    table_new,
    gate_old,
    up_old,
    down_old,
):
    group = table_old.shape[0]
    tok, width = batch_one.shape
    place = jnp.stack([lax.axis_index("tensor"), lax.axis_index("expert")]).astype(jnp.int32)
    tables = [pl.BlockSpec(memory_space=pltpu.SMEM)] * 2
    ins = (
        norm_gain, batch_one, batch_two, slots_one.T, slots_two.T, gates_one.T, gates_two.T
    )
    own = call(
        prepare_kernel,
        (jax.ShapeDtypeStruct((tok, width + PACK), jnp.bfloat16),) * 2,
        (table_old, table_new, *ins),
        8,
        10 * tok * width,
        8 * tok * width,
        [pltpu.VMEM(x.shape, x.dtype) for x in ins] + [pltpu.SemaphoreType.DMA((len(ins),))],
        tables + [pl.BlockSpec(memory_space=pl.ANY)] * len(ins),
    )
    both = jnp.concatenate([gate_old[0], up_old[0]], axis=1)
    down = down_old[0]
    beside_both = swap(both, Z_LOW)
    twin_both, twin_down = swap_core(both), swap_core(down)
    pieces = [spread(x) for x in own]
    down_later, beside_both, pieces = lax.optimization_barrier((down, beside_both, pieces))
    beside_down = swap(down_later, Z_LOW)
    beside_twin_both = swap_core(beside_both)
    ff = gate_old.shape[2]
    rows = 8 * tok
    scratch = (pltpu.VMEM((rows, width + PACK), jnp.bfloat16),)
    totals = [
        call(
            functools.partial(own_kernel, 8, group),
            jax.ShapeDtypeStruct((rows, width), jnp.float32),
            (place, *p, both, twin_both, down, twin_down),
            20,
            6 * rows * width * ff,
            6 * width * ff + 6 * rows * width,
            scratch,
        )
        for p in pieces
    ]
    hidden = [
        call(
            functools.partial(beside_kernel, 8, group),
            (
                jax.ShapeDtypeStruct((rows, ff), jnp.bfloat16),
                jax.ShapeDtypeStruct((rows, PACK), jnp.float32),
            ),
            (place, *p, beside_both, beside_twin_both),
            16,
            4 * rows * width * ff,
            4 * width * ff + 2 * rows * width,
            scratch,
        )
        for p in pieces
    ]
    beside_down, totals, hidden[0] = lax.optimization_barrier((beside_down, totals, hidden[0]))
    beside_twin_down = swap_core(beside_down)
    outs = []
    for total, (hid, weight) in zip(totals, hidden):
        parts = call(
            join_kernel,
            (jax.ShapeDtypeStruct((2 * tok, width), jnp.bfloat16),) * 2
            + (jax.ShapeDtypeStruct((2 * tok, width), jnp.float32),) * 2,
            (place, hid, weight, total, beside_down, beside_twin_down),
            14,
            2 * rows * width * ff,
            2 * width * ff + 8 * rows * width,
        )
        outs.append(send_back(*parts))
    return tuple(outs)


def solution(mesh):
    in_specs = (
        P(("expert", "tensor"), None),
        P(("expert", "tensor"), None),
        P(),
        P(("expert", "tensor"), None),
        P(("expert", "tensor"), None),
        P(("expert", "tensor"), None),
        P(("expert", "tensor"), None),
        P(),
        P(),
        P("expert", "tensor", None),
        P("expert", "tensor", None),
        P("expert", None, "tensor"),
    )
    out_specs = (P(("expert", "tensor"), None), P(("expert", "tensor"), None))
    local = local_pairs if (mesh.shape["expert"], mesh.shape["tensor"]) == (16, 2) else local_any
    return jax.shard_map(local, mesh=mesh, in_specs=in_specs, out_specs=out_specs, check_vma=False)
```

```python
import functools

import jax
import jax.numpy as jnp
from jax import lax
from jax.experimental import pallas as pl
from jax.experimental.pallas import tpu as pltpu
from jax.sharding import PartitionSpec as P

EPS = 1e-05
PACK = 128
X, Y, Z_LOW, Z_HIGH = 1, 2, 4, 8


def rms_rows(tokens, norm_gain):
    values = tokens.astype(jnp.float32)
    square = jnp.mean(values * values, axis=-1, keepdims=True)
    return (values * lax.rsqrt(square + EPS) * norm_gain.astype(jnp.float32)).astype(jnp.bfloat16)


def source_slots(table_old, table_new):
    group = table_old.shape[0]
    slot_index = jnp.arange(group, dtype=jnp.int32)
    picked = jnp.where(
        table_new == jnp.roll(table_old, 1), (slot_index - 1) % group, (slot_index + 1) % group
    )
    return jnp.where(table_new == table_old, slot_index, picked).astype(jnp.int32)


def slot_weights(route_slots, route_gates, held_by):
    group = held_by.shape[0]
    hit = route_slots[:, :, None] == jnp.arange(group, dtype=jnp.int32)
    by_slot = jnp.sum(jnp.where(hit, route_gates[:, :, None], 0.0), axis=1)
    moved = held_by[:, None] == jnp.arange(group, dtype=jnp.int32)
    return jnp.sum(jnp.where(moved[None], by_slot[:, :, None], 0.0), axis=1)


def expert_part(rows, weight, gate_full, up_full, down_full):
    gate_act = jnp.dot(rows, gate_full, preferred_element_type=jnp.float32)
    up_act = jnp.dot(rows, up_full, preferred_element_type=jnp.float32)
    hidden = (jax.nn.silu(gate_act) * up_act).astype(jnp.bfloat16)
    result = jnp.dot(hidden, down_full, preferred_element_type=jnp.float32)
    return (result * weight[:, None]).astype(jnp.bfloat16)


def local_any(
    batch_one,
    batch_two,
    norm_gain,
    slots_one,
    slots_two,
    gates_one,
    gates_two,
    table_old,
    table_new,
    gate_old,
    up_old,
    down_old,
):
    group = table_old.shape[0]
    me = lax.axis_index("expert")
    gate_full = lax.all_gather(gate_old[0], "tensor", axis=0, tiled=True)
    up_full = lax.all_gather(up_old[0], "tensor", axis=0, tiled=True)
    down_full = lax.all_gather(down_old[0], "tensor", axis=1, tiled=True)
    rows_one = lax.all_gather(rms_rows(batch_one, norm_gain), "expert", axis=0, tiled=True)
    rows_two = lax.all_gather(rms_rows(batch_two, norm_gain), "expert", axis=0, tiled=True)
    own = jnp.arange(group, dtype=jnp.int32)
    weights = jnp.stack(
        [
            slot_weights(slots_one, gates_one, own),
            slot_weights(slots_two, gates_two, source_slots(table_old, table_new)),
        ]
    )
    all_weights = lax.all_gather(weights, "expert", axis=1, tiled=True)
    mine = lax.dynamic_index_in_dim(all_weights, me, axis=2, keepdims=False)
    outs = []
    for rows, weight in ((rows_one, mine[0]), (rows_two, mine[1])):
        part = expert_part(rows, weight, gate_full, up_full, down_full)
        outs.append(lax.psum_scatter(part, "expert", scatter_dimension=0, tiled=True))
    return tuple(outs)


def call(body, outs, ins, vmem_mb, flops=0, moved=0, scratch=(), specs=None):
    smem = pl.BlockSpec(memory_space=pltpu.SMEM)
    vmem = pl.BlockSpec(memory_space=pltpu.VMEM)
    return pl.pallas_call(
        body,
        out_shape=outs,
        in_specs=specs
        or [smem if x.ndim == 1 and x.dtype == jnp.int32 else vmem for x in ins],
        out_specs=jax.tree.map(lambda _: vmem, outs),
        scratch_shapes=list(scratch),
        compiler_params=pltpu.CompilerParams(vmem_limit_bytes=vmem_mb * 1024 * 1024),
        cost_estimate=pl.CostEstimate(flops=flops, bytes_accessed=moved, transcendentals=0),
    )(*ins)


def prepare_kernel(old_ref, new_ref, *refs):
    hbm, outs, both_ref, held, sems = refs[:9], refs[9:11], refs[11], refs[12:19], refs[19]
    ff = both_ref.shape[1] // 2
    places = list(held) + [both_ref.at[:, :ff], both_ref.at[:, ff:]]
    copies = [pltpu.make_async_copy(a, b, sems.at[i]) for i, (a, b) in enumerate(zip(hbm, places))]
    for copy in copies:
        copy.start()
    group = old_ref.shape[0]
    sources = []
    for s in range(group):
        left, right = (s - 1) % group, (s + 1) % group
        wanted = new_ref[s]
        other = jnp.where(wanted == old_ref[left], left, right)
        sources.append(jnp.where(wanted == old_ref[s], s, other))
    for copy in copies[: len(held)]:
        copy.wait()
    gain = held[0][...].astype(jnp.float32).reshape(1, -1)
    for b in range(2):
        tokens_ref, slots_ref, gates_ref = held[1 + b], held[3 + b], held[5 + b]
        out_ref = outs[b]
        tok, width = tokens_ref.shape
        values = tokens_ref[...].astype(jnp.float32)
        square = jnp.mean(values * values, axis=-1, keepdims=True)
        out_ref[:, :width] = (values * lax.rsqrt(square + EPS) * gain).astype(jnp.bfloat16)
        slots, gates = slots_ref[...], gates_ref[...]
        if b == 1:
            holder = jnp.zeros_like(slots)
            for s in range(group):
                holder = jnp.where(slots == s, sources[s], holder)
            slots = holder
        expert = lax.broadcasted_iota(jnp.int32, (group, tok), 0)
        total = jnp.zeros((group, tok), jnp.float32)
        for k in range(slots.shape[0]):
            total += jnp.where(expert == slots[k : k + 1, :], gates[k : k + 1, :], 0.0)
        high = total.astype(jnp.bfloat16)
        rest = total - high.astype(jnp.float32)
        middle = rest.astype(jnp.bfloat16)
        low = (rest - middle.astype(jnp.float32)).astype(jnp.bfloat16)
        packed = jnp.concatenate([high, middle, low], axis=0)
        row = lax.broadcasted_iota(jnp.int32, (3 * group, PACK), 0)
        lane = lax.broadcasted_iota(jnp.int32, (3 * group, PACK), 1)
        turned = lax.dot_general(
            packed,
            (row == lane).astype(jnp.bfloat16),
            (((0,), (0,)), ((), ())),
            preferred_element_type=jnp.float32,
        )
        out_ref[:, width:] = turned.astype(jnp.bfloat16)
    for copy in copies[len(held) :]:
        copy.wait()


def hidden_of(place, rows_ref, both_refs, begin, count):
    depth, ff = both_refs[0].shape[0], both_refs[0].shape[1] // 2
    acts = None
    for which, ref in enumerate(both_refs):
        half = place if which == 0 else 1 - place
        columns = pl.ds(pl.multiple_of(half * depth, depth), depth)
        rows = rows_ref[pl.ds(begin, count), columns]
        term = jnp.dot(rows, ref[...], preferred_element_type=jnp.float32)
        acts = term if acts is None else acts + term
    gate_act, up_act = acts[:, :ff], acts[:, ff:]
    return (gate_act / (1.0 + jnp.exp(-gate_act)) * up_act).astype(jnp.bfloat16)


def weight_of(expert, group, packed):
    lane = lax.broadcasted_iota(jnp.int32, packed.shape, 1)
    chosen = (lane & (group - 1)) == expert
    return jnp.sum(jnp.where(chosen, packed.astype(jnp.float32), 0.0), axis=1, keepdims=True)


def own_kernel(pieces, group, *refs):
    piece_refs, refs = refs[:pieces], refs[pieces:]
    both_a, both_b, down_a, down_b, total_ref, rows_ref = refs
    tok = piece_refs[0].shape[0]
    width = total_ref.shape[1]
    for i, ref in enumerate(piece_refs):
        rows_ref[i * tok : (i + 1) * tok, :] = ref[...]
    place, expert = lax.axis_index("tensor"), lax.axis_index("expert")
    block = 256

    @pl.loop(0, rows_ref.shape[0] // block)
    def _(step):
        begin = pl.multiple_of(step * block, block)
        hidden = hidden_of(place, rows_ref, (both_a, both_b), begin, block)
        weight = weight_of(expert, group, rows_ref[pl.ds(begin, block), width:])
        for which, ref in enumerate((down_a, down_b)):
            half = place if which == 0 else 1 - place
            columns = pl.ds(pl.multiple_of(half * ref.shape[1], ref.shape[1]), ref.shape[1])
            part = jnp.dot(hidden, ref[...], preferred_element_type=jnp.float32)
            total_ref[pl.ds(begin, block), columns] = part * weight


def beside_kernel(pieces, group, *refs):
    piece_refs, refs = refs[:pieces], refs[pieces:]
    both_a, both_b, hidden_ref, weight_ref, rows_ref = refs
    tok = piece_refs[0].shape[0]
    width = rows_ref.shape[1] - PACK
    for i, ref in enumerate(piece_refs):
        rows_ref[i * tok : (i + 1) * tok, :] = ref[...]
    place, expert = lax.axis_index("tensor"), lax.axis_index("expert") ^ Z_LOW
    block = 256

    @pl.loop(0, rows_ref.shape[0] // block)
    def _(step):
        begin = pl.multiple_of(step * block, block)
        hidden_ref[pl.ds(begin, block), :] = hidden_of(
            place, rows_ref, (both_a, both_b), begin, block
        )
        weight = weight_of(expert, group, rows_ref[pl.ds(begin, block), width:])
        weight_ref[pl.ds(begin, block), :] = jnp.broadcast_to(weight, (block, PACK))


def join_kernel(hidden_ref, weight_ref, total_ref, down_a, down_b, send_a, send_b, keep_a, keep_b):
    place = lax.axis_index("tensor")
    count = send_a.shape[0]
    for pair, outs in ((0, (send_a, send_b)), (1, (keep_a, keep_b))):
        rows = slice(pair * 2 * count, (pair + 1) * 2 * count)
        weight = weight_ref[rows, :1]
        for which, ref in enumerate((down_a, down_b)):
            half = place if which == 0 else 1 - place
            columns = pl.ds(pl.multiple_of(half * ref.shape[1], ref.shape[1]), ref.shape[1])
            part = jnp.dot(hidden_ref[rows, :], ref[...], preferred_element_type=jnp.float32)
            part = part * weight + total_ref[rows, columns]
            outs[0][:, columns] = part[:count].astype(outs[0].dtype)
            outs[1][:, columns] = part[count:].astype(outs[1].dtype)


def first_sum_kernel(keep_ref, got_ref, send_ref, held_ref):
    half = held_ref.shape[0]
    held_ref[...] = keep_ref[:half] + got_ref[:half].astype(jnp.float32)
    send_ref[...] = (keep_ref[half:] + got_ref[half:].astype(jnp.float32)).astype(jnp.bfloat16)


def second_sum_kernel(keep_a, got_a, keep_b, got_b, send_ref, held_ref):
    half = keep_a.shape[0] // 2
    for i, (keep, got) in enumerate(((keep_a, got_a), (keep_b, got_b))):
        rows = slice(i * half, (i + 1) * half)
        held_ref[rows, :] = keep[:half] + got[:half].astype(jnp.float32)
        send_ref[rows, :] = (keep[half:] + got[half:].astype(jnp.float32)).astype(jnp.bfloat16)


def last_sum_kernel(keep_ref, got_ref, out_ref):
    out_ref[...] = (keep_ref[...] + got_ref[...].astype(jnp.float32)).astype(jnp.bfloat16)


def swap(block, distance):
    count = lax.axis_size("expert")
    return lax.ppermute(block, "expert", [(i, i ^ distance) for i in range(count)])


def swap_core(block):
    return lax.ppermute(block, "tensor", [(0, 1), (1, 0)])


def halves(own, far):
    half = own.shape[0] // 2
    return [jnp.concatenate([own[i : i + half], far[i : i + half]]) for i in (0, half)]


def spread(a1, b1, a2, b2):
    a3, b3 = swap(a1, Y), swap(b1, X)
    a4, b4 = swap(a2, Y), swap(b2, X)
    return [a3, a4, b3, b4, a1, a2, b1, b2]


def first_return(send_a, send_b, keep_a, keep_b):
    quarter, width = keep_a.shape[0] // 2, keep_a.shape[1]
    outs = (
        jax.ShapeDtypeStruct((quarter, width), jnp.bfloat16),
        jax.ShapeDtypeStruct((quarter, width), jnp.float32),
    )
    size = quarter * width
    got_a, got_b = swap(send_a, Y), swap(send_b, X)
    next_a, held_a = call(first_sum_kernel, outs, (keep_a, got_a), 8, size, 18 * size)
    next_b, held_b = call(first_sum_kernel, outs, (keep_b, got_b), 8, size, 18 * size)
    return next_a, next_b, held_a, held_b


def last_returns(next_a, next_b, held_a, held_b):
    outs = (
        jax.ShapeDtypeStruct(held_a.shape, jnp.bfloat16),
        jax.ShapeDtypeStruct(held_a.shape, jnp.float32),
    )
    size = held_a.size
    got_a, got_b = swap(next_a, X), swap(next_b, Y)
    next_z, held_z = call(
        second_sum_kernel, outs, (held_a, got_a, held_b, got_b), 8, size, 18 * size
    )
    got_z = swap(next_z, Z_HIGH)
    return call(last_sum_kernel, outs[0], (held_z, got_z), 8, size, 8 * size)


def local_pairs(
    batch_one,
    batch_two,
    norm_gain,
    slots_one,
    slots_two,
    gates_one,
    gates_two,
    table_old,
    table_new,
    gate_old,
    up_old,
    down_old,
):
    group = table_old.shape[0]
    tok, width = batch_one.shape
    ff = gate_old.shape[2]
    gate, up, down = gate_old[0], up_old[0], down_old[0]
    held = (norm_gain, batch_one, batch_two, slots_one.T, slots_two.T, gates_one.T, gates_two.T)
    specs = [pl.BlockSpec(memory_space=pltpu.SMEM)] * 2
    specs += [pl.BlockSpec(memory_space=pl.ANY)] * (len(held) + 2)
    own_one, own_two, both = call(
        prepare_kernel,
        (jax.ShapeDtypeStruct((tok, width + PACK), jnp.bfloat16),) * 2
        + (jax.ShapeDtypeStruct((gate.shape[0], 2 * ff), jnp.bfloat16),),
        (table_old, table_new, *held, gate, up),
        8,
        10 * tok * width,
        8 * tok * width,
        [pltpu.VMEM(x.shape, x.dtype) for x in held]
        + [pltpu.SemaphoreType.DMA((len(held) + 2,))],
        specs,
    )
    own = (own_one, own_two)
    both_by = swap(both, Z_LOW)
    twins = (swap_core(both), swap_core(down))
    far = [swap(x, Z_HIGH) for x in own]
    far[0], twins = lax.optimization_barrier((far[0], twins))
    first = [halves(x, y) for x, y in zip(own, far)]
    second = [(swap(a1, X), swap(b1, Y)) for a1, b1 in first]
    pieces = [spread(*f, *s) for f, s in zip(first, second)]

    rows = 8 * tok
    scratch = (pltpu.VMEM((rows, width + PACK), jnp.bfloat16),)

    def own_total(p):
        return call(
            functools.partial(own_kernel, 8, group),
            jax.ShapeDtypeStruct((rows, width), jnp.float32),
            (*p, both, twins[0], down, twins[1]),
            20,
            6 * rows * width * ff,
            6 * width * ff + 6 * rows * width,
            scratch,
        )

    def beside_hidden(p):
        return call(
            functools.partial(beside_kernel, 8, group),
            (
                jax.ShapeDtypeStruct((rows, ff), jnp.bfloat16),
                jax.ShapeDtypeStruct((rows, PACK), jnp.float32),
            ),
            (*p, both_by, both_twin),
            16,
            4 * rows * width * ff,
            4 * width * ff + 2 * rows * width,
            scratch,
        )

    def join(total, hid, weight):
        return call(
            join_kernel,
            (jax.ShapeDtypeStruct((2 * tok, width), jnp.bfloat16),) * 2
            + (jax.ShapeDtypeStruct((2 * tok, width), jnp.float32),) * 2,
            (hid, weight, total, down_by, down_twin),
            14,
            2 * rows * width * ff,
            2 * width * ff + 8 * rows * width,
        )

    pieces[0], second[1] = lax.optimization_barrier((pieces[0], second[1]))
    total_one = own_total(pieces[0])
    down_later, both_by, total_one, pieces = lax.optimization_barrier(
        (down, both_by, total_one, pieces)
    )
    down_by = swap(down_later, Z_LOW)
    both_twin = swap_core(both_by)
    total_two = own_total(pieces[1])
    hidden_one, hidden_two = beside_hidden(pieces[0]), beside_hidden(pieces[1])
    down_by, total_two, hidden_one, hidden_two = lax.optimization_barrier(
        (down_by, total_two, hidden_one, hidden_two)
    )
    down_twin = swap_core(down_by)
    back_one = first_return(*join(total_one, *hidden_one))
    sums_two = join(total_two, *hidden_two)
    back_one, sums_two = lax.optimization_barrier((back_one, sums_two))
    back_two = first_return(*sums_two)
    return last_returns(*back_one), last_returns(*back_two)


def solution(mesh):
    in_specs = (
        P(("expert", "tensor"), None),
        P(("expert", "tensor"), None),
        P(),
        P(("expert", "tensor"), None),
        P(("expert", "tensor"), None),
        P(("expert", "tensor"), None),
        P(("expert", "tensor"), None),
        P(),
        P(),
        P("expert", "tensor", None),
        P("expert", "tensor", None),
        P("expert", None, "tensor"),
    )
    out_specs = (P(("expert", "tensor"), None), P(("expert", "tensor"), None))
    local = local_pairs if (mesh.shape["expert"], mesh.shape["tensor"]) == (16, 2) else local_any
    return jax.shard_map(local, mesh=mesh, in_specs=in_specs, out_specs=out_specs, check_vma=False)
```

```python
import functools

import jax
import jax.numpy as jnp
from jax import lax
from jax.experimental import pallas as pl
from jax.experimental.pallas import tpu as pltpu
from jax.sharding import PartitionSpec as P

EPS = 1e-05
PACK = 128
X, Y, Z_LOW, Z_HIGH = 1, 2, 4, 8


def rms_rows(tokens, norm_gain):
    values = tokens.astype(jnp.float32)
    square = jnp.mean(values * values, axis=-1, keepdims=True)
    return (values * lax.rsqrt(square + EPS) * norm_gain.astype(jnp.float32)).astype(jnp.bfloat16)


def source_slots(table_old, table_new):
    group = table_old.shape[0]
    slot_index = jnp.arange(group, dtype=jnp.int32)
    picked = jnp.where(
        table_new == jnp.roll(table_old, 1), (slot_index - 1) % group, (slot_index + 1) % group
    )
    return jnp.where(table_new == table_old, slot_index, picked).astype(jnp.int32)


def slot_weights(route_slots, route_gates, held_by):
    group = held_by.shape[0]
    hit = route_slots[:, :, None] == jnp.arange(group, dtype=jnp.int32)
    by_slot = jnp.sum(jnp.where(hit, route_gates[:, :, None], 0.0), axis=1)
    moved = held_by[:, None] == jnp.arange(group, dtype=jnp.int32)
    return jnp.sum(jnp.where(moved[None], by_slot[:, :, None], 0.0), axis=1)


def expert_part(rows, weight, gate_full, up_full, down_full):
    gate_act = jnp.dot(rows, gate_full, preferred_element_type=jnp.float32)
    up_act = jnp.dot(rows, up_full, preferred_element_type=jnp.float32)
    hidden = (jax.nn.silu(gate_act) * up_act).astype(jnp.bfloat16)
    result = jnp.dot(hidden, down_full, preferred_element_type=jnp.float32)
    return (result * weight[:, None]).astype(jnp.bfloat16)


def local_any(
    batch_one,
    batch_two,
    norm_gain,
    slots_one,
    slots_two,
    gates_one,
    gates_two,
    table_old,
    table_new,
    gate_old,
    up_old,
    down_old,
):
    group = table_old.shape[0]
    me = lax.axis_index("expert")
    gate_full = lax.all_gather(gate_old[0], "tensor", axis=0, tiled=True)
    up_full = lax.all_gather(up_old[0], "tensor", axis=0, tiled=True)
    down_full = lax.all_gather(down_old[0], "tensor", axis=1, tiled=True)
    rows_one = lax.all_gather(rms_rows(batch_one, norm_gain), "expert", axis=0, tiled=True)
    rows_two = lax.all_gather(rms_rows(batch_two, norm_gain), "expert", axis=0, tiled=True)
    own = jnp.arange(group, dtype=jnp.int32)
    weights = jnp.stack(
        [
            slot_weights(slots_one, gates_one, own),
            slot_weights(slots_two, gates_two, source_slots(table_old, table_new)),
        ]
    )
    all_weights = lax.all_gather(weights, "expert", axis=1, tiled=True)
    mine = lax.dynamic_index_in_dim(all_weights, me, axis=2, keepdims=False)
    outs = []
    for rows, weight in ((rows_one, mine[0]), (rows_two, mine[1])):
        part = expert_part(rows, weight, gate_full, up_full, down_full)
        outs.append(lax.psum_scatter(part, "expert", scatter_dimension=0, tiled=True))
    return tuple(outs)


def call(body, outs, ins, vmem_mb, flops=0, moved=0, scratch=(), specs=None):
    smem = pl.BlockSpec(memory_space=pltpu.SMEM)
    vmem = pl.BlockSpec(memory_space=pltpu.VMEM)
    return pl.pallas_call(
        body,
        out_shape=outs,
        in_specs=specs
        or [smem if x.ndim == 1 and x.dtype == jnp.int32 else vmem for x in ins],
        out_specs=jax.tree.map(lambda _: vmem, outs),
        scratch_shapes=list(scratch),
        compiler_params=pltpu.CompilerParams(vmem_limit_bytes=vmem_mb * 1024 * 1024),
        cost_estimate=pl.CostEstimate(flops=flops, bytes_accessed=moved, transcendentals=0),
    )(*ins)


def prepare_kernel(*refs):
    hbm, outs, held, sems = refs[:9], refs[9:11], refs[11:20], refs[20]
    copies = [pltpu.make_async_copy(a, b, sems.at[i]) for i, (a, b) in enumerate(zip(hbm, held))]
    for copy in copies:
        copy.start()
    for copy in copies:
        copy.wait()
    old_ref, new_ref = held[7:]
    group = old_ref.shape[0]
    sources = []
    for s in range(group):
        left, right = (s - 1) % group, (s + 1) % group
        wanted = new_ref[s]
        other = jnp.where(wanted == old_ref[left], left, right)
        sources.append(jnp.where(wanted == old_ref[s], s, other))
    gain = held[0][...].astype(jnp.float32).reshape(1, -1)
    for b in range(2):
        tokens_ref, slots_ref, gates_ref = held[1 + b], held[3 + b], held[5 + b]
        out_ref = outs[b]
        tok, width = tokens_ref.shape
        values = tokens_ref[...].astype(jnp.float32)
        square = jnp.mean(values * values, axis=-1, keepdims=True)
        out_ref[:, :width] = (values * lax.rsqrt(square + EPS) * gain).astype(jnp.bfloat16)
        slots, gates = slots_ref[...], gates_ref[...]
        if b == 1:
            holder = jnp.zeros_like(slots)
            for s in range(group):
                holder = jnp.where(slots == s, sources[s], holder)
            slots = holder
        expert = lax.broadcasted_iota(jnp.int32, (group, tok), 0)
        total = jnp.zeros((group, tok), jnp.float32)
        for k in range(slots.shape[0]):
            total += jnp.where(expert == slots[k : k + 1, :], gates[k : k + 1, :], 0.0)
        high = total.astype(jnp.bfloat16)
        rest = total - high.astype(jnp.float32)
        middle = rest.astype(jnp.bfloat16)
        low = (rest - middle.astype(jnp.float32)).astype(jnp.bfloat16)
        packed = jnp.concatenate([high, middle, low], axis=0)
        row = lax.broadcasted_iota(jnp.int32, (3 * group, PACK), 0)
        lane = lax.broadcasted_iota(jnp.int32, (3 * group, PACK), 1)
        turned = lax.dot_general(
            packed,
            (row == lane).astype(jnp.bfloat16),
            (((0,), (0,)), ((), ())),
            preferred_element_type=jnp.float32,
        )
        out_ref[:, width:] = turned.astype(jnp.bfloat16)


def pack_kernel(gate_ref, up_ref, both_ref, sems):
    ff = gate_ref.shape[1]
    copies = [
        pltpu.make_async_copy(gate_ref, both_ref.at[:, :ff], sems.at[0]),
        pltpu.make_async_copy(up_ref, both_ref.at[:, ff:], sems.at[1]),
    ]
    for copy in copies:
        copy.start()
    for copy in copies:
        copy.wait()


def hidden_of(place, rows_ref, both_refs, begin, count):
    depth, ff = both_refs[0].shape[0], both_refs[0].shape[1] // 2
    acts = None
    for which, ref in enumerate(both_refs):
        half = place if which == 0 else 1 - place
        columns = pl.ds(pl.multiple_of(half * depth, depth), depth)
        rows = rows_ref[pl.ds(begin, count), columns]
        term = jnp.dot(rows, ref[...], preferred_element_type=jnp.float32)
        acts = term if acts is None else acts + term
    gate_act, up_act = acts[:, :ff], acts[:, ff:]
    return (gate_act / (1.0 + jnp.exp(-gate_act)) * up_act).astype(jnp.bfloat16)


def weight_of(expert, group, packed):
    lane = lax.broadcasted_iota(jnp.int32, packed.shape, 1)
    chosen = (lane & (group - 1)) == expert
    return jnp.sum(jnp.where(chosen, packed.astype(jnp.float32), 0.0), axis=1, keepdims=True)


def own_kernel(pieces, group, *refs):
    piece_refs, refs = refs[:pieces], refs[pieces:]
    both_a, both_b, down_a, down_b, total_ref, rows_ref = refs
    tok = piece_refs[0].shape[0]
    width = total_ref.shape[1]
    for i, ref in enumerate(piece_refs):
        rows_ref[i * tok : (i + 1) * tok, :] = ref[...]
    place, expert = lax.axis_index("tensor"), lax.axis_index("expert")
    block = 256

    @pl.loop(0, rows_ref.shape[0] // block)
    def _(step):
        begin = pl.multiple_of(step * block, block)
        hidden = hidden_of(place, rows_ref, (both_a, both_b), begin, block)
        weight = weight_of(expert, group, rows_ref[pl.ds(begin, block), width:])
        for which, ref in enumerate((down_a, down_b)):
            half = place if which == 0 else 1 - place
            columns = pl.ds(pl.multiple_of(half * ref.shape[1], ref.shape[1]), ref.shape[1])
            part = jnp.dot(hidden, ref[...], preferred_element_type=jnp.float32)
            total_ref[pl.ds(begin, block), columns] = part * weight


def beside_kernel(pieces, group, *refs):
    piece_refs, refs = refs[:pieces], refs[pieces:]
    both_a, both_b, hidden_ref, weight_ref, rows_ref = refs
    tok = piece_refs[0].shape[0]
    width = rows_ref.shape[1] - PACK
    for i, ref in enumerate(piece_refs):
        rows_ref[i * tok : (i + 1) * tok, :] = ref[...]
    place, expert = lax.axis_index("tensor"), lax.axis_index("expert") ^ Z_LOW
    block = 256

    @pl.loop(0, rows_ref.shape[0] // block)
    def _(step):
        begin = pl.multiple_of(step * block, block)
        hidden_ref[pl.ds(begin, block), :] = hidden_of(
            place, rows_ref, (both_a, both_b), begin, block
        )
        weight = weight_of(expert, group, rows_ref[pl.ds(begin, block), width:])
        weight_ref[pl.ds(begin, block), :] = jnp.broadcast_to(weight, (block, PACK))


def join_kernel(hidden_ref, weight_ref, total_ref, down_a, down_b, send_a, send_b, keep_a, keep_b):
    place = lax.axis_index("tensor")
    count = send_a.shape[0]
    for pair, outs in ((0, (send_a, send_b)), (1, (keep_a, keep_b))):
        rows = slice(pair * 2 * count, (pair + 1) * 2 * count)
        weight = weight_ref[rows, :1]
        for which, ref in enumerate((down_a, down_b)):
            half = place if which == 0 else 1 - place
            columns = pl.ds(pl.multiple_of(half * ref.shape[1], ref.shape[1]), ref.shape[1])
            part = jnp.dot(hidden_ref[rows, :], ref[...], preferred_element_type=jnp.float32)
            part = part * weight + total_ref[rows, columns]
            outs[0][:, columns] = part[:count].astype(outs[0].dtype)
            outs[1][:, columns] = part[count:].astype(outs[1].dtype)


def first_sum_kernel(keep_ref, got_ref, send_ref, held_ref):
    half = held_ref.shape[0]
    held_ref[...] = keep_ref[:half] + got_ref[:half].astype(jnp.float32)
    send_ref[...] = (keep_ref[half:] + got_ref[half:].astype(jnp.float32)).astype(jnp.bfloat16)


def second_sum_kernel(keep_a, got_a, keep_b, got_b, send_ref, held_ref):
    half = keep_a.shape[0] // 2
    for i, (keep, got) in enumerate(((keep_a, got_a), (keep_b, got_b))):
        rows = slice(i * half, (i + 1) * half)
        held_ref[rows, :] = keep[:half] + got[:half].astype(jnp.float32)
        send_ref[rows, :] = (keep[half:] + got[half:].astype(jnp.float32)).astype(jnp.bfloat16)


def last_sum_kernel(keep_ref, got_ref, out_ref):
    out_ref[...] = (keep_ref[...] + got_ref[...].astype(jnp.float32)).astype(jnp.bfloat16)


def swap(block, distance):
    count = lax.axis_size("expert")
    return lax.ppermute(block, "expert", [(i, i ^ distance) for i in range(count)])


def swap_core(block):
    return lax.ppermute(block, "tensor", [(0, 1), (1, 0)])


def halves(own, far):
    half = own.shape[0] // 2
    return [jnp.concatenate([own[i : i + half], far[i : i + half]]) for i in (0, half)]


def spread(a1, b1, a2, b2):
    a3, b3 = swap(a1, Y), swap(b1, X)
    a4, b4 = swap(a2, Y), swap(b2, X)
    return [a3, a4, b3, b4, a1, a2, b1, b2]


def first_return(send_a, send_b, keep_a, keep_b):
    quarter, width = keep_a.shape[0] // 2, keep_a.shape[1]
    outs = (
        jax.ShapeDtypeStruct((quarter, width), jnp.bfloat16),
        jax.ShapeDtypeStruct((quarter, width), jnp.float32),
    )
    size = quarter * width
    got_a, got_b = swap(send_a, Y), swap(send_b, X)
    next_a, held_a = call(first_sum_kernel, outs, (keep_a, got_a), 8, size, 18 * size)
    next_b, held_b = call(first_sum_kernel, outs, (keep_b, got_b), 8, size, 18 * size)
    return next_a, next_b, held_a, held_b


def last_returns(next_a, next_b, held_a, held_b):
    outs = (
        jax.ShapeDtypeStruct(held_a.shape, jnp.bfloat16),
        jax.ShapeDtypeStruct(held_a.shape, jnp.float32),
    )
    size = held_a.size
    got_a, got_b = swap(next_a, X), swap(next_b, Y)
    next_z, held_z = call(
        second_sum_kernel, outs, (held_a, got_a, held_b, got_b), 8, size, 18 * size
    )
    got_z = swap(next_z, Z_HIGH)
    return call(last_sum_kernel, outs[0], (held_z, got_z), 8, size, 8 * size)


def local_pairs(
    batch_one,
    batch_two,
    norm_gain,
    slots_one,
    slots_two,
    gates_one,
    gates_two,
    table_old,
    table_new,
    gate_old,
    up_old,
    down_old,
):
    group = table_old.shape[0]
    tok, width = batch_one.shape
    ff = gate_old.shape[2]
    gate, up, down = gate_old[0], up_old[0], down_old[0]
    held = (
        norm_gain, batch_one, batch_two, slots_one.T, slots_two.T, gates_one.T, gates_two.T,
        table_old, table_new,
    )
    hbm = pl.BlockSpec(memory_space=pltpu.HBM)
    own = call(
        prepare_kernel,
        (jax.ShapeDtypeStruct((tok, width + PACK), jnp.bfloat16),) * 2,
        held,
        8,
        10 * tok * width,
        8 * tok * width,
        [(pltpu.SMEM if x.ndim == 1 and x.dtype == jnp.int32 else pltpu.VMEM)(x.shape, x.dtype) for x in held]
        + [pltpu.SemaphoreType.DMA((len(held),))],
        [hbm] * len(held),
    )
    both = call(
        pack_kernel,
        jax.ShapeDtypeStruct((gate.shape[0], 2 * ff), jnp.bfloat16),
        (gate, up),
        8,
        0,
        8 * gate.size,
        [pltpu.SemaphoreType.DMA((2,))],
        [hbm] * 2,
    )
    twins = (swap_core(both), swap_core(down))
    far = [swap(x, Z_HIGH) for x in own]
    far[0], twins, both_later = lax.optimization_barrier((far[0], twins, both))
    both_by = swap(both_later, Z_LOW)
    first_one = halves(own[0], far[0])
    second_one = swap(first_one[0], X), swap(first_one[1], Y)
    far[1], second_one = lax.optimization_barrier((far[1], second_one))
    first_two = halves(own[1], far[1])
    second_two = swap(first_two[0], X), swap(first_two[1], Y)
    pieces = [spread(*first_one, *second_one), spread(*first_two, *second_two)]

    rows = 8 * tok
    scratch = (pltpu.VMEM((rows, width + PACK), jnp.bfloat16),)

    def own_total(p):
        return call(
            functools.partial(own_kernel, 8, group),
            jax.ShapeDtypeStruct((rows, width), jnp.float32),
            (*p, both, twins[0], down, twins[1]),
            20,
            6 * rows * width * ff,
            6 * width * ff + 6 * rows * width,
            scratch,
        )

    def beside_hidden(p):
        return call(
            functools.partial(beside_kernel, 8, group),
            (
                jax.ShapeDtypeStruct((rows, ff), jnp.bfloat16),
                jax.ShapeDtypeStruct((rows, PACK), jnp.float32),
            ),
            (*p, both_by, both_twin),
            16,
            4 * rows * width * ff,
            4 * width * ff + 2 * rows * width,
            scratch,
        )

    def join(total, hid, weight):
        return call(
            join_kernel,
            (jax.ShapeDtypeStruct((2 * tok, width), jnp.bfloat16),) * 2
            + (jax.ShapeDtypeStruct((2 * tok, width), jnp.float32),) * 2,
            (hid, weight, total, down_by, down_twin),
            14,
            2 * rows * width * ff,
            2 * width * ff + 8 * rows * width,
        )

    total_one = own_total(pieces[0])
    down_later, both_by, total_one, pieces = lax.optimization_barrier(
        (down, both_by, total_one, pieces)
    )
    down_by = swap(down_later, Z_LOW)
    both_twin = swap_core(both_by)
    total_two = own_total(pieces[1])
    hidden_one, hidden_two = beside_hidden(pieces[0]), beside_hidden(pieces[1])
    down_by, total_two, hidden_one, hidden_two = lax.optimization_barrier(
        (down_by, total_two, hidden_one, hidden_two)
    )
    down_twin = swap_core(down_by)
    back_one = first_return(*join(total_one, *hidden_one))
    back_two = first_return(*join(total_two, *hidden_two))
    return last_returns(*back_one), last_returns(*back_two)


def solution(mesh):
    in_specs = (
        P(("expert", "tensor"), None),
        P(("expert", "tensor"), None),
        P(),
        P(("expert", "tensor"), None),
        P(("expert", "tensor"), None),
        P(("expert", "tensor"), None),
        P(("expert", "tensor"), None),
        P(),
        P(),
        P("expert", "tensor", None),
        P("expert", "tensor", None),
        P("expert", None, "tensor"),
    )
    out_specs = (P(("expert", "tensor"), None), P(("expert", "tensor"), None))
    local = local_pairs if (mesh.shape["expert"], mesh.shape["tensor"]) == (16, 2) else local_any
    return jax.shard_map(local, mesh=mesh, in_specs=in_specs, out_specs=out_specs, check_vma=False)
```

```python
import functools

import jax
import jax.numpy as jnp
from jax import lax
from jax.experimental import pallas as pl
from jax.experimental.pallas import tpu as pltpu
from jax.sharding import PartitionSpec as P

EPS = 1e-05
PACK = 128
X, Y, Z_LOW, Z_HIGH = 1, 2, 4, 8 | 1


def rms_rows(tokens, norm_gain):
    values = tokens.astype(jnp.float32)
    square = jnp.mean(values * values, axis=-1, keepdims=True)
    return (values * lax.rsqrt(square + EPS) * norm_gain.astype(jnp.float32)).astype(jnp.bfloat16)


def source_slots(table_old, table_new):
    group = table_old.shape[0]
    slot_index = jnp.arange(group, dtype=jnp.int32)
    picked = jnp.where(
        table_new == jnp.roll(table_old, 1), (slot_index - 1) % group, (slot_index + 1) % group
    )
    return jnp.where(table_new == table_old, slot_index, picked).astype(jnp.int32)


def slot_weights(route_slots, route_gates, held_by):
    group = held_by.shape[0]
    hit = route_slots[:, :, None] == jnp.arange(group, dtype=jnp.int32)
    by_slot = jnp.sum(jnp.where(hit, route_gates[:, :, None], 0.0), axis=1)
    moved = held_by[:, None] == jnp.arange(group, dtype=jnp.int32)
    return jnp.sum(jnp.where(moved[None], by_slot[:, :, None], 0.0), axis=1)


def expert_part(rows, weight, gate_full, up_full, down_full):
    gate_act = jnp.dot(rows, gate_full, preferred_element_type=jnp.float32)
    up_act = jnp.dot(rows, up_full, preferred_element_type=jnp.float32)
    hidden = (jax.nn.silu(gate_act) * up_act).astype(jnp.bfloat16)
    result = jnp.dot(hidden, down_full, preferred_element_type=jnp.float32)
    return (result * weight[:, None]).astype(jnp.bfloat16)


def local_any(
    batch_one,
    batch_two,
    norm_gain,
    slots_one,
    slots_two,
    gates_one,
    gates_two,
    table_old,
    table_new,
    gate_old,
    up_old,
    down_old,
):
    group = table_old.shape[0]
    me = lax.axis_index("expert")
    gate_full = lax.all_gather(gate_old[0], "tensor", axis=0, tiled=True)
    up_full = lax.all_gather(up_old[0], "tensor", axis=0, tiled=True)
    down_full = lax.all_gather(down_old[0], "tensor", axis=1, tiled=True)
    rows_one = lax.all_gather(rms_rows(batch_one, norm_gain), "expert", axis=0, tiled=True)
    rows_two = lax.all_gather(rms_rows(batch_two, norm_gain), "expert", axis=0, tiled=True)
    own = jnp.arange(group, dtype=jnp.int32)
    weights = jnp.stack(
        [
            slot_weights(slots_one, gates_one, own),
            slot_weights(slots_two, gates_two, source_slots(table_old, table_new)),
        ]
    )
    all_weights = lax.all_gather(weights, "expert", axis=1, tiled=True)
    mine = lax.dynamic_index_in_dim(all_weights, me, axis=2, keepdims=False)
    outs = []
    for rows, weight in ((rows_one, mine[0]), (rows_two, mine[1])):
        part = expert_part(rows, weight, gate_full, up_full, down_full)
        outs.append(lax.psum_scatter(part, "expert", scatter_dimension=0, tiled=True))
    return tuple(outs)


def call(body, outs, ins, vmem_mb, flops=0, moved=0, scratch=(), specs=None):
    smem = pl.BlockSpec(memory_space=pltpu.SMEM)
    vmem = pl.BlockSpec(memory_space=pltpu.VMEM)
    return pl.pallas_call(
        body,
        out_shape=outs,
        in_specs=specs
        or [smem if x.ndim == 1 and x.dtype == jnp.int32 else vmem for x in ins],
        out_specs=jax.tree.map(lambda _: vmem, outs),
        scratch_shapes=list(scratch),
        compiler_params=pltpu.CompilerParams(vmem_limit_bytes=vmem_mb * 1024 * 1024),
        cost_estimate=pl.CostEstimate(flops=flops, bytes_accessed=moved, transcendentals=0),
    )(*ins)


def prepare_kernel(*refs):
    hbm, outs, held, sems = refs[:9], refs[9:11], refs[11:20], refs[20]
    copies = [pltpu.make_async_copy(a, b, sems.at[i]) for i, (a, b) in enumerate(zip(hbm, held))]
    for copy in copies:
        copy.start()
    for copy in copies:
        copy.wait()
    old_ref, new_ref = held[7:]
    group = old_ref.shape[0]
    sources = []
    for s in range(group):
        left, right = (s - 1) % group, (s + 1) % group
        wanted = new_ref[s]
        other = jnp.where(wanted == old_ref[left], left, right)
        sources.append(jnp.where(wanted == old_ref[s], s, other))
    gain = held[0][...].astype(jnp.float32).reshape(1, -1)
    for b in range(2):
        tokens_ref, slots_ref, gates_ref = held[1 + b], held[3 + b], held[5 + b]
        out_ref = outs[b]
        tok, width = tokens_ref.shape
        values = tokens_ref[...].astype(jnp.float32)
        square = jnp.mean(values * values, axis=-1, keepdims=True)
        out_ref[:, :width] = (values * lax.rsqrt(square + EPS) * gain).astype(jnp.bfloat16)
        slots, gates = slots_ref[...], gates_ref[...]
        if b == 1:
            holder = jnp.zeros_like(slots)
            for s in range(group):
                holder = jnp.where(slots == s, sources[s], holder)
            slots = holder
        expert = lax.broadcasted_iota(jnp.int32, (group, tok), 0)
        total = jnp.zeros((group, tok), jnp.float32)
        for k in range(slots.shape[0]):
            total += jnp.where(expert == slots[k : k + 1, :], gates[k : k + 1, :], 0.0)
        high = total.astype(jnp.bfloat16)
        rest = total - high.astype(jnp.float32)
        middle = rest.astype(jnp.bfloat16)
        low = (rest - middle.astype(jnp.float32)).astype(jnp.bfloat16)
        packed = jnp.concatenate([high, middle, low], axis=0)
        row = lax.broadcasted_iota(jnp.int32, (3 * group, PACK), 0)
        lane = lax.broadcasted_iota(jnp.int32, (3 * group, PACK), 1)
        turned = lax.dot_general(
            packed,
            (row == lane).astype(jnp.bfloat16),
            (((0,), (0,)), ((), ())),
            preferred_element_type=jnp.float32,
        )
        out_ref[:, width:] = turned.astype(jnp.bfloat16)


def pack_kernel(gate_ref, up_ref, both_ref, sems):
    ff = gate_ref.shape[1]
    copies = [
        pltpu.make_async_copy(gate_ref, both_ref.at[:, :ff], sems.at[0]),
        pltpu.make_async_copy(up_ref, both_ref.at[:, ff:], sems.at[1]),
    ]
    for copy in copies:
        copy.start()
    for copy in copies:
        copy.wait()


def hidden_of(place, rows_ref, both_refs, begin, count):
    depth, ff = both_refs[0].shape[0], both_refs[0].shape[1] // 2
    acts = None
    for which, ref in enumerate(both_refs):
        half = place if which == 0 else 1 - place
        columns = pl.ds(pl.multiple_of(half * depth, depth), depth)
        rows = rows_ref[pl.ds(begin, count), columns]
        term = jnp.dot(rows, ref[...], preferred_element_type=jnp.float32)
        acts = term if acts is None else acts + term
    gate_act, up_act = acts[:, :ff], acts[:, ff:]
    return (gate_act / (1.0 + jnp.exp(-gate_act)) * up_act).astype(jnp.bfloat16)


def weight_of(expert, group, packed):
    lane = lax.broadcasted_iota(jnp.int32, packed.shape, 1)
    chosen = (lane & (group - 1)) == expert
    return jnp.sum(jnp.where(chosen, packed.astype(jnp.float32), 0.0), axis=1, keepdims=True)


def own_kernel(pieces, group, *refs):
    piece_refs, refs = refs[:pieces], refs[pieces:]
    both_a, both_b, down_a, down_b, total_ref, rows_ref = refs
    tok = piece_refs[0].shape[0]
    width = total_ref.shape[1]
    for i, ref in enumerate(piece_refs):
        rows_ref[i * tok : (i + 1) * tok, :] = ref[...]
    place, expert = lax.axis_index("tensor"), lax.axis_index("expert")
    block = 256

    @pl.loop(0, rows_ref.shape[0] // block)
    def _(step):
        begin = pl.multiple_of(step * block, block)
        hidden = hidden_of(place, rows_ref, (both_a, both_b), begin, block)
        weight = weight_of(expert, group, rows_ref[pl.ds(begin, block), width:])
        for which, ref in enumerate((down_a, down_b)):
            half = place if which == 0 else 1 - place
            columns = pl.ds(pl.multiple_of(half * ref.shape[1], ref.shape[1]), ref.shape[1])
            part = jnp.dot(hidden, ref[...], preferred_element_type=jnp.float32)
            total_ref[pl.ds(begin, block), columns] = part * weight


def beside_kernel(pieces, group, *refs):
    piece_refs, refs = refs[:pieces], refs[pieces:]
    both_a, both_b, hidden_ref, weight_ref, rows_ref = refs
    tok = piece_refs[0].shape[0]
    width = rows_ref.shape[1] - PACK
    for i, ref in enumerate(piece_refs):
        rows_ref[i * tok : (i + 1) * tok, :] = ref[...]
    place, expert = lax.axis_index("tensor"), lax.axis_index("expert") ^ Z_LOW
    block = 256

    @pl.loop(0, rows_ref.shape[0] // block)
    def _(step):
        begin = pl.multiple_of(step * block, block)
        hidden_ref[pl.ds(begin, block), :] = hidden_of(
            place, rows_ref, (both_a, both_b), begin, block
        )
        weight = weight_of(expert, group, rows_ref[pl.ds(begin, block), width:])
        weight_ref[pl.ds(begin, block), :] = jnp.broadcast_to(weight, (block, PACK))


def join_kernel(hidden_ref, weight_ref, total_ref, down_a, down_b, send_a, send_b, keep_a, keep_b):
    place = lax.axis_index("tensor")
    count = send_a.shape[0]
    for pair, outs in ((0, (send_a, send_b)), (1, (keep_a, keep_b))):
        rows = slice(pair * 2 * count, (pair + 1) * 2 * count)
        weight = weight_ref[rows, :1]
        for which, ref in enumerate((down_a, down_b)):
            half = place if which == 0 else 1 - place
            columns = pl.ds(pl.multiple_of(half * ref.shape[1], ref.shape[1]), ref.shape[1])
            part = jnp.dot(hidden_ref[rows, :], ref[...], preferred_element_type=jnp.float32)
            part = part * weight + total_ref[rows, columns]
            outs[0][:, columns] = part[:count].astype(outs[0].dtype)
            outs[1][:, columns] = part[count:].astype(outs[1].dtype)


def first_sum_kernel(keep_ref, got_ref, send_ref, held_ref):
    half = held_ref.shape[0]
    held_ref[...] = keep_ref[:half] + got_ref[:half].astype(jnp.float32)
    send_ref[...] = (keep_ref[half:] + got_ref[half:].astype(jnp.float32)).astype(jnp.bfloat16)


def second_sum_kernel(keep_a, got_a, keep_b, got_b, send_ref, held_ref):
    half = keep_a.shape[0] // 2
    for i, (keep, got) in enumerate(((keep_a, got_a), (keep_b, got_b))):
        rows = slice(i * half, (i + 1) * half)
        held_ref[rows, :] = keep[:half] + got[:half].astype(jnp.float32)
        send_ref[rows, :] = (keep[half:] + got[half:].astype(jnp.float32)).astype(jnp.bfloat16)


def last_sum_kernel(keep_ref, got_ref, out_ref):
    out_ref[...] = (keep_ref[...] + got_ref[...].astype(jnp.float32)).astype(jnp.bfloat16)


def swap(block, distance):
    count = lax.axis_size("expert")
    return lax.ppermute(block, "expert", [(i, i ^ distance) for i in range(count)])


def swap_core(block):
    return lax.ppermute(block, "tensor", [(0, 1), (1, 0)])


def halves(own, far):
    half = own.shape[0] // 2
    return [jnp.concatenate([own[i : i + half], far[i : i + half]]) for i in (0, half)]


def spread(a1, b1, a2, b2):
    a3, b3 = swap(a1, Y), swap(b1, X)
    a4, b4 = swap(a2, Y), swap(b2, X)
    return [a3, a4, b3, b4, a1, a2, b1, b2]


def first_return(send_a, send_b, keep_a, keep_b):
    quarter, width = keep_a.shape[0] // 2, keep_a.shape[1]
    outs = (
        jax.ShapeDtypeStruct((quarter, width), jnp.bfloat16),
        jax.ShapeDtypeStruct((quarter, width), jnp.float32),
    )
    size = quarter * width
    got_a, got_b = swap(send_a, Y), swap(send_b, X)
    next_a, held_a = call(first_sum_kernel, outs, (keep_a, got_a), 8, size, 18 * size)
    next_b, held_b = call(first_sum_kernel, outs, (keep_b, got_b), 8, size, 18 * size)
    return next_a, next_b, held_a, held_b


def last_returns(next_a, next_b, held_a, held_b):
    outs = (
        jax.ShapeDtypeStruct(held_a.shape, jnp.bfloat16),
        jax.ShapeDtypeStruct(held_a.shape, jnp.float32),
    )
    size = held_a.size
    got_a, got_b = swap(next_a, X), swap(next_b, Y)
    next_z, held_z = call(
        second_sum_kernel, outs, (held_a, got_a, held_b, got_b), 8, size, 18 * size
    )
    got_z = swap(next_z, Z_HIGH)
    return call(last_sum_kernel, outs[0], (held_z, got_z), 8, size, 8 * size)


def local_pairs(
    batch_one,
    batch_two,
    norm_gain,
    slots_one,
    slots_two,
    gates_one,
    gates_two,
    table_old,
    table_new,
    gate_old,
    up_old,
    down_old,
):
    group = table_old.shape[0]
    tok, width = batch_one.shape
    ff = gate_old.shape[2]
    gate, up, down = gate_old[0], up_old[0], down_old[0]
    held = (
        norm_gain, batch_one, batch_two, slots_one.T, slots_two.T, gates_one.T, gates_two.T,
        table_old, table_new,
    )
    hbm = pl.BlockSpec(memory_space=pltpu.HBM)
    own = call(
        prepare_kernel,
        (jax.ShapeDtypeStruct((tok, width + PACK), jnp.bfloat16),) * 2,
        held,
        8,
        10 * tok * width,
        8 * tok * width,
        [(pltpu.SMEM if x.ndim == 1 and x.dtype == jnp.int32 else pltpu.VMEM)(x.shape, x.dtype) for x in held]
        + [pltpu.SemaphoreType.DMA((len(held),))],
        [hbm] * len(held),
    )
    own, gate, up = lax.optimization_barrier((own, gate, up))
    both = call(
        pack_kernel,
        jax.ShapeDtypeStruct((gate.shape[0], 2 * ff), jnp.bfloat16),
        (gate, up),
        8,
        0,
        8 * gate.size,
        [pltpu.SemaphoreType.DMA((2,))],
        [hbm] * 2,
    )
    twins = (swap_core(both), swap_core(down))
    far = [swap(x, Z_HIGH) for x in own]
    both_by = swap(both, Z_LOW)
    first_one = halves(own[0], far[0])
    second_one = swap(first_one[0], X), swap(first_one[1], Y)
    far[1], second_one = lax.optimization_barrier((far[1], second_one))
    first_two = halves(own[1], far[1])
    second_two = swap(first_two[0], X), swap(first_two[1], Y)
    pieces = [spread(*first_one, *second_one), spread(*first_two, *second_two)]

    rows = 8 * tok
    scratch = (pltpu.VMEM((rows, width + PACK), jnp.bfloat16),)

    def own_total(p):
        return call(
            functools.partial(own_kernel, 8, group),
            jax.ShapeDtypeStruct((rows, width), jnp.float32),
            (*p, both, twins[0], down, twins[1]),
            20,
            6 * rows * width * ff,
            6 * width * ff + 6 * rows * width,
            scratch,
        )

    def beside_hidden(p):
        return call(
            functools.partial(beside_kernel, 8, group),
            (
                jax.ShapeDtypeStruct((rows, ff), jnp.bfloat16),
                jax.ShapeDtypeStruct((rows, PACK), jnp.float32),
            ),
            (*p, both_by, both_twin),
            16,
            4 * rows * width * ff,
            4 * width * ff + 2 * rows * width,
            scratch,
        )

    def join(total, hid, weight):
        return call(
            join_kernel,
            (jax.ShapeDtypeStruct((2 * tok, width), jnp.bfloat16),) * 2
            + (jax.ShapeDtypeStruct((2 * tok, width), jnp.float32),) * 2,
            (hid, weight, total, down_by, down_twin),
            14,
            2 * rows * width * ff,
            2 * width * ff + 8 * rows * width,
        )

    total_one = own_total(pieces[0])
    down_later, both_by, total_one, second_two = lax.optimization_barrier(
        (down, both_by, total_one, second_two)
    )
    down_by = swap(down_later, Z_LOW)
    both_twin = swap_core(both_by)
    total_two = own_total(pieces[1])
    hidden_one, hidden_two = beside_hidden(pieces[0]), beside_hidden(pieces[1])
    down_by, total_two, hidden_one, hidden_two = lax.optimization_barrier(
        (down_by, total_two, hidden_one, hidden_two)
    )
    down_twin = swap_core(down_by)
    back_one = first_return(*join(total_one, *hidden_one))
    back_two = first_return(*join(total_two, *hidden_two))
    return last_returns(*back_one), last_returns(*back_two)


def solution(mesh):
    in_specs = (
        P(("expert", "tensor"), None),
        P(("expert", "tensor"), None),
        P(),
        P(("expert", "tensor"), None),
        P(("expert", "tensor"), None),
        P(("expert", "tensor"), None),
        P(("expert", "tensor"), None),
        P(),
        P(),
        P("expert", "tensor", None),
        P("expert", "tensor", None),
        P("expert", None, "tensor"),
    )
    out_specs = (P(("expert", "tensor"), None), P(("expert", "tensor"), None))
    local = local_pairs if (mesh.shape["expert"], mesh.shape["tensor"]) == (16, 2) else local_any
    return jax.shard_map(local, mesh=mesh, in_specs=in_specs, out_specs=out_specs, check_vma=False)
```

```python
import functools

import jax
import jax.numpy as jnp
from jax import lax
from jax.experimental import pallas as pl
from jax.experimental.pallas import tpu as pltpu
from jax.sharding import PartitionSpec as P

EPS = 1e-05
PACK = 128
X, Y, Z_LOW, Z_HIGH = 1, 2, 4, 8


def rms_rows(tokens, norm_gain):
    values = tokens.astype(jnp.float32)
    square = jnp.mean(values * values, axis=-1, keepdims=True)
    return (values * lax.rsqrt(square + EPS) * norm_gain.astype(jnp.float32)).astype(jnp.bfloat16)


def source_slots(table_old, table_new):
    group = table_old.shape[0]
    slot_index = jnp.arange(group, dtype=jnp.int32)
    picked = jnp.where(
        table_new == jnp.roll(table_old, 1), (slot_index - 1) % group, (slot_index + 1) % group
    )
    return jnp.where(table_new == table_old, slot_index, picked).astype(jnp.int32)


def slot_weights(route_slots, route_gates, held_by):
    group = held_by.shape[0]
    hit = route_slots[:, :, None] == jnp.arange(group, dtype=jnp.int32)
    by_slot = jnp.sum(jnp.where(hit, route_gates[:, :, None], 0.0), axis=1)
    moved = held_by[:, None] == jnp.arange(group, dtype=jnp.int32)
    return jnp.sum(jnp.where(moved[None], by_slot[:, :, None], 0.0), axis=1)


def expert_part(rows, weight, gate_full, up_full, down_full):
    gate_act = jnp.dot(rows, gate_full, preferred_element_type=jnp.float32)
    up_act = jnp.dot(rows, up_full, preferred_element_type=jnp.float32)
    hidden = (jax.nn.silu(gate_act) * up_act).astype(jnp.bfloat16)
    result = jnp.dot(hidden, down_full, preferred_element_type=jnp.float32)
    return (result * weight[:, None]).astype(jnp.bfloat16)


def local_any(
    batch_one,
    batch_two,
    norm_gain,
    slots_one,
    slots_two,
    gates_one,
    gates_two,
    table_old,
    table_new,
    gate_old,
    up_old,
    down_old,
):
    group = table_old.shape[0]
    me = lax.axis_index("expert")
    gate_full = lax.all_gather(gate_old[0], "tensor", axis=0, tiled=True)
    up_full = lax.all_gather(up_old[0], "tensor", axis=0, tiled=True)
    down_full = lax.all_gather(down_old[0], "tensor", axis=1, tiled=True)
    rows_one = lax.all_gather(rms_rows(batch_one, norm_gain), "expert", axis=0, tiled=True)
    rows_two = lax.all_gather(rms_rows(batch_two, norm_gain), "expert", axis=0, tiled=True)
    own = jnp.arange(group, dtype=jnp.int32)
    weights = jnp.stack(
        [
            slot_weights(slots_one, gates_one, own),
            slot_weights(slots_two, gates_two, source_slots(table_old, table_new)),
        ]
    )
    all_weights = lax.all_gather(weights, "expert", axis=1, tiled=True)
    mine = lax.dynamic_index_in_dim(all_weights, me, axis=2, keepdims=False)
    outs = []
    for rows, weight in ((rows_one, mine[0]), (rows_two, mine[1])):
        part = expert_part(rows, weight, gate_full, up_full, down_full)
        outs.append(lax.psum_scatter(part, "expert", scatter_dimension=0, tiled=True))
    return tuple(outs)


def call(body, outs, ins, vmem_mb, flops=0, moved=0, scratch=(), specs=None):
    smem = pl.BlockSpec(memory_space=pltpu.SMEM)
    vmem = pl.BlockSpec(memory_space=pltpu.VMEM)
    return pl.pallas_call(
        body,
        out_shape=outs,
        in_specs=specs
        or [smem if x.ndim == 1 and x.dtype == jnp.int32 else vmem for x in ins],
        out_specs=jax.tree.map(lambda _: vmem, outs),
        scratch_shapes=list(scratch),
        compiler_params=pltpu.CompilerParams(vmem_limit_bytes=vmem_mb * 1024 * 1024),
        cost_estimate=pl.CostEstimate(flops=flops, bytes_accessed=moved, transcendentals=0),
    )(*ins)


def prepare_kernel(*refs):
    hbm, outs, held, sems = refs[:9], refs[9:11], refs[11:20], refs[20]
    copies = [pltpu.make_async_copy(a, b, sems.at[i]) for i, (a, b) in enumerate(zip(hbm, held))]
    for copy in copies:
        copy.start()
    for copy in copies:
        copy.wait()
    old_ref, new_ref = held[7:]
    group = old_ref.shape[0]
    sources = []
    for s in range(group):
        left, right = (s - 1) % group, (s + 1) % group
        wanted = new_ref[s]
        other = jnp.where(wanted == old_ref[left], left, right)
        sources.append(jnp.where(wanted == old_ref[s], s, other))
    gain = held[0][...].astype(jnp.float32).reshape(1, -1)
    for b in range(2):
        tokens_ref, slots_ref, gates_ref = held[1 + b], held[3 + b], held[5 + b]
        out_ref = outs[b]
        tok, width = tokens_ref.shape
        values = tokens_ref[...].astype(jnp.float32)
        square = jnp.mean(values * values, axis=-1, keepdims=True)
        out_ref[:, :width] = (values * lax.rsqrt(square + EPS) * gain).astype(jnp.bfloat16)
        slots, gates = slots_ref[...], gates_ref[...]
        if b == 1:
            holder = jnp.zeros_like(slots)
            for s in range(group):
                holder = jnp.where(slots == s, sources[s], holder)
            slots = holder
        expert = lax.broadcasted_iota(jnp.int32, (group, tok), 0)
        total = jnp.zeros((group, tok), jnp.float32)
        for k in range(slots.shape[0]):
            total += jnp.where(expert == slots[k : k + 1, :], gates[k : k + 1, :], 0.0)
        high = total.astype(jnp.bfloat16)
        rest = total - high.astype(jnp.float32)
        middle = rest.astype(jnp.bfloat16)
        low = (rest - middle.astype(jnp.float32)).astype(jnp.bfloat16)
        packed = jnp.concatenate([high, middle, low], axis=0)
        row = lax.broadcasted_iota(jnp.int32, (3 * group, PACK), 0)
        lane = lax.broadcasted_iota(jnp.int32, (3 * group, PACK), 1)
        turned = lax.dot_general(
            packed,
            (row == lane).astype(jnp.bfloat16),
            (((0,), (0,)), ((), ())),
            preferred_element_type=jnp.float32,
        )
        out_ref[:, width:] = turned.astype(jnp.bfloat16)


def pack_kernel(gate_ref, up_ref, both_ref, sems):
    ff = gate_ref.shape[1]
    copies = [
        pltpu.make_async_copy(gate_ref, both_ref.at[:, :ff], sems.at[0]),
        pltpu.make_async_copy(up_ref, both_ref.at[:, ff:], sems.at[1]),
    ]
    for copy in copies:
        copy.start()
    for copy in copies:
        copy.wait()


def hidden_of(place, rows_ref, both_refs, begin, count):
    depth, ff = both_refs[0].shape[0], both_refs[0].shape[1] // 2
    acts = None
    for which, ref in enumerate(both_refs):
        half = place if which == 0 else 1 - place
        columns = pl.ds(pl.multiple_of(half * depth, depth), depth)
        rows = rows_ref[pl.ds(begin, count), columns]
        term = jnp.dot(rows, ref[...], preferred_element_type=jnp.float32)
        acts = term if acts is None else acts + term
    gate_act, up_act = acts[:, :ff], acts[:, ff:]
    return (gate_act / (1.0 + jnp.exp(-gate_act)) * up_act).astype(jnp.bfloat16)


def weight_of(expert, group, packed):
    lane = lax.broadcasted_iota(jnp.int32, packed.shape, 1)
    chosen = (lane & (group - 1)) == expert
    return jnp.sum(jnp.where(chosen, packed.astype(jnp.float32), 0.0), axis=1, keepdims=True)


def own_kernel(pieces, group, *refs):
    piece_refs, refs = refs[:pieces], refs[pieces:]
    both_a, both_b, down_a, down_b, total_ref, rows_ref = refs
    tok = piece_refs[0].shape[0]
    width = total_ref.shape[1]
    for i, ref in enumerate(piece_refs):
        rows_ref[i * tok : (i + 1) * tok, :] = ref[...]
    place, expert = lax.axis_index("tensor"), lax.axis_index("expert")
    block = 256

    @pl.loop(0, rows_ref.shape[0] // block)
    def _(step):
        begin = pl.multiple_of(step * block, block)
        hidden = hidden_of(place, rows_ref, (both_a, both_b), begin, block)
        weight = weight_of(expert, group, rows_ref[pl.ds(begin, block), width:])
        for which, ref in enumerate((down_a, down_b)):
            half = place if which == 0 else 1 - place
            columns = pl.ds(pl.multiple_of(half * ref.shape[1], ref.shape[1]), ref.shape[1])
            part = jnp.dot(hidden, ref[...], preferred_element_type=jnp.float32)
            total_ref[pl.ds(begin, block), columns] = part * weight


def beside_kernel(pieces, group, *refs):
    piece_refs, refs = refs[:pieces], refs[pieces:]
    both_a, both_b, hidden_ref, weight_ref, rows_ref = refs
    tok = piece_refs[0].shape[0]
    width = rows_ref.shape[1] - PACK
    for i, ref in enumerate(piece_refs):
        rows_ref[i * tok : (i + 1) * tok, :] = ref[...]
    place, expert = lax.axis_index("tensor"), lax.axis_index("expert") ^ Z_LOW
    block = 256

    @pl.loop(0, rows_ref.shape[0] // block)
    def _(step):
        begin = pl.multiple_of(step * block, block)
        hidden_ref[pl.ds(begin, block), :] = hidden_of(
            place, rows_ref, (both_a, both_b), begin, block
        )
        weight = weight_of(expert, group, rows_ref[pl.ds(begin, block), width:])
        weight_ref[pl.ds(begin, block), :] = jnp.broadcast_to(weight, (block, PACK))


def join_kernel(hidden_ref, weight_ref, total_ref, down_a, down_b, send_a, send_b, keep_a, keep_b):
    place = lax.axis_index("tensor")
    count = send_a.shape[0]
    for pair, outs in ((0, (send_a, send_b)), (1, (keep_a, keep_b))):
        rows = slice(pair * 2 * count, (pair + 1) * 2 * count)
        weight = weight_ref[rows, :1]
        for which, ref in enumerate((down_a, down_b)):
            half = place if which == 0 else 1 - place
            columns = pl.ds(pl.multiple_of(half * ref.shape[1], ref.shape[1]), ref.shape[1])
            part = jnp.dot(hidden_ref[rows, :], ref[...], preferred_element_type=jnp.float32)
            part = part * weight + total_ref[rows, columns]
            outs[0][:, columns] = part[:count].astype(outs[0].dtype)
            outs[1][:, columns] = part[count:].astype(outs[1].dtype)


def first_sum_kernel(keep_ref, got_ref, send_ref, held_ref):
    half = held_ref.shape[0]
    held_ref[...] = keep_ref[:half] + got_ref[:half].astype(jnp.float32)
    send_ref[...] = (keep_ref[half:] + got_ref[half:].astype(jnp.float32)).astype(jnp.bfloat16)


def second_sum_kernel(keep_a, got_a, keep_b, got_b, send_ref, held_ref):
    half = keep_a.shape[0] // 2
    for i, (keep, got) in enumerate(((keep_a, got_a), (keep_b, got_b))):
        rows = slice(i * half, (i + 1) * half)
        held_ref[rows, :] = keep[:half] + got[:half].astype(jnp.float32)
        send_ref[rows, :] = (keep[half:] + got[half:].astype(jnp.float32)).astype(jnp.bfloat16)


def last_sum_kernel(keep_ref, got_ref, out_ref):
    out_ref[...] = (keep_ref[...] + got_ref[...].astype(jnp.float32)).astype(jnp.bfloat16)


def swap(block, distance):
    count = lax.axis_size("expert")
    return lax.ppermute(block, "expert", [(i, i ^ distance) for i in range(count)])


def swap_core(block):
    return lax.ppermute(block, "tensor", [(0, 1), (1, 0)])


def halves(own, far):
    half = own.shape[0] // 2
    return [jnp.concatenate([own[i : i + half], far[i : i + half]]) for i in (0, half)]


def spread(a1, b1, a2, b2):
    a3, b3 = swap(a1, Y), swap(b1, X)
    a4, b4 = swap(a2, Y), swap(b2, X)
    return [a3, a4, b3, b4, a1, a2, b1, b2]


def first_return(send_a, send_b, keep_a, keep_b):
    quarter, width = keep_a.shape[0] // 2, keep_a.shape[1]
    outs = (
        jax.ShapeDtypeStruct((quarter, width), jnp.bfloat16),
        jax.ShapeDtypeStruct((quarter, width), jnp.float32),
    )
    size = quarter * width
    got_a, got_b = swap(send_a, Y), swap(send_b, X)
    next_a, held_a = call(first_sum_kernel, outs, (keep_a, got_a), 8, size, 18 * size)
    next_b, held_b = call(first_sum_kernel, outs, (keep_b, got_b), 8, size, 18 * size)
    return next_a, next_b, held_a, held_b


def last_returns(next_a, next_b, held_a, held_b):
    outs = (
        jax.ShapeDtypeStruct(held_a.shape, jnp.bfloat16),
        jax.ShapeDtypeStruct(held_a.shape, jnp.float32),
    )
    size = held_a.size
    got_a, got_b = swap(next_a, X), swap(next_b, Y)
    next_z, held_z = call(
        second_sum_kernel, outs, (held_a, got_a, held_b, got_b), 8, size, 18 * size
    )
    got_z = swap(next_z, Z_HIGH)
    return call(last_sum_kernel, outs[0], (held_z, got_z), 8, size, 8 * size)


def local_pairs(
    batch_one,
    batch_two,
    norm_gain,
    slots_one,
    slots_two,
    gates_one,
    gates_two,
    table_old,
    table_new,
    gate_old,
    up_old,
    down_old,
):
    group = table_old.shape[0]
    tok, width = batch_one.shape
    ff = gate_old.shape[2]
    gate, up, down = gate_old[0], up_old[0], down_old[0]
    held = (
        norm_gain, batch_one, batch_two, slots_one.T, slots_two.T, gates_one.T, gates_two.T,
        table_old, table_new,
    )
    hbm = pl.BlockSpec(memory_space=pltpu.HBM)
    own = call(
        prepare_kernel,
        (jax.ShapeDtypeStruct((tok, width + PACK), jnp.bfloat16),) * 2,
        held,
        8,
        10 * tok * width,
        8 * tok * width,
        [(pltpu.SMEM if x.ndim == 1 and x.dtype == jnp.int32 else pltpu.VMEM)(x.shape, x.dtype) for x in held]
        + [pltpu.SemaphoreType.DMA((len(held),))],
        [hbm] * len(held),
    )
    own, gate, up = lax.optimization_barrier((own, gate, up))
    both = call(
        pack_kernel,
        jax.ShapeDtypeStruct((gate.shape[0], 2 * ff), jnp.bfloat16),
        (gate, up),
        8,
        0,
        8 * gate.size,
        [pltpu.SemaphoreType.DMA((2,))],
        [hbm] * 2,
    )
    twins = (swap_core(both), swap_core(down))
    far_one = swap(own[0], Z_HIGH)
    far_one, both_later = lax.optimization_barrier((far_one, both))
    both_by = swap(both_later, Z_LOW)
    first_one = halves(own[0], far_one)
    second_one = swap(first_one[0], X), swap(first_one[1], Y)
    second_one, own_two = lax.optimization_barrier((second_one, own[1]))
    far_two = swap(own_two, Z_HIGH)
    pieces_one = spread(*first_one, *second_one)

    rows = 8 * tok
    scratch = (pltpu.VMEM((rows, width + PACK), jnp.bfloat16),)

    def own_total(p):
        return call(
            functools.partial(own_kernel, 8, group),
            jax.ShapeDtypeStruct((rows, width), jnp.float32),
            (*p, both, twins[0], down, twins[1]),
            20,
            6 * rows * width * ff,
            6 * width * ff + 6 * rows * width,
            scratch,
        )

    def beside_hidden(p):
        return call(
            functools.partial(beside_kernel, 8, group),
            (
                jax.ShapeDtypeStruct((rows, ff), jnp.bfloat16),
                jax.ShapeDtypeStruct((rows, PACK), jnp.float32),
            ),
            (*p, both_by, both_twin),
            16,
            4 * rows * width * ff,
            4 * width * ff + 2 * rows * width,
            scratch,
        )

    def join(total, hid, weight):
        return call(
            join_kernel,
            (jax.ShapeDtypeStruct((2 * tok, width), jnp.bfloat16),) * 2
            + (jax.ShapeDtypeStruct((2 * tok, width), jnp.float32),) * 2,
            (hid, weight, total, down_by, down_twin),
            14,
            2 * rows * width * ff,
            2 * width * ff + 8 * rows * width,
        )

    total_one = own_total(pieces_one)
    down_later, both_by, total_one = lax.optimization_barrier((down, both_by, total_one))
    down_by = swap(down_later, Z_LOW)
    both_twin = swap_core(both_by)
    hidden_one = beside_hidden(pieces_one)
    hidden_one, far_two = lax.optimization_barrier((hidden_one, far_two))
    first_two = halves(own[1], far_two)
    second_two = swap(first_two[0], X), swap(first_two[1], Y)
    pieces_two = spread(*first_two, *second_two)
    down_by, hidden_one, pieces_two = lax.optimization_barrier((down_by, hidden_one, pieces_two))
    down_twin = swap_core(down_by)
    sums_one, pieces_two = lax.optimization_barrier((join(total_one, *hidden_one), pieces_two))
    back_one = first_return(*sums_one)
    total_two, hidden_two = own_total(pieces_two), beside_hidden(pieces_two)
    back_two = first_return(*join(total_two, *hidden_two))
    return last_returns(*back_one), last_returns(*back_two)


def solution(mesh):
    in_specs = (
        P(("expert", "tensor"), None),
        P(("expert", "tensor"), None),
        P(),
        P(("expert", "tensor"), None),
        P(("expert", "tensor"), None),
        P(("expert", "tensor"), None),
        P(("expert", "tensor"), None),
        P(),
        P(),
        P("expert", "tensor", None),
        P("expert", "tensor", None),
        P("expert", None, "tensor"),
    )
    out_specs = (P(("expert", "tensor"), None), P(("expert", "tensor"), None))
    local = local_pairs if (mesh.shape["expert"], mesh.shape["tensor"]) == (16, 2) else local_any
    return jax.shard_map(local, mesh=mesh, in_specs=in_specs, out_specs=out_specs, check_vma=False)
```

```python
import functools

import jax
import jax.numpy as jnp
from jax import lax
from jax.experimental import pallas as pl
from jax.experimental.pallas import tpu as pltpu
from jax.sharding import PartitionSpec as P

EPS = 1e-05
PACK = 128
X, Y, Z_LOW, Z_HIGH = 1, 2, 4, 8


def rms_rows(tokens, norm_gain):
    values = tokens.astype(jnp.float32)
    square = jnp.mean(values * values, axis=-1, keepdims=True)
    return (values * lax.rsqrt(square + EPS) * norm_gain.astype(jnp.float32)).astype(jnp.bfloat16)


def source_slots(table_old, table_new):
    group = table_old.shape[0]
    slot_index = jnp.arange(group, dtype=jnp.int32)
    picked = jnp.where(
        table_new == jnp.roll(table_old, 1), (slot_index - 1) % group, (slot_index + 1) % group
    )
    return jnp.where(table_new == table_old, slot_index, picked).astype(jnp.int32)


def slot_weights(route_slots, route_gates, held_by):
    group = held_by.shape[0]
    hit = route_slots[:, :, None] == jnp.arange(group, dtype=jnp.int32)
    by_slot = jnp.sum(jnp.where(hit, route_gates[:, :, None], 0.0), axis=1)
    moved = held_by[:, None] == jnp.arange(group, dtype=jnp.int32)
    return jnp.sum(jnp.where(moved[None], by_slot[:, :, None], 0.0), axis=1)


def expert_part(rows, weight, gate_full, up_full, down_full):
    gate_act = jnp.dot(rows, gate_full, preferred_element_type=jnp.float32)
    up_act = jnp.dot(rows, up_full, preferred_element_type=jnp.float32)
    hidden = (jax.nn.silu(gate_act) * up_act).astype(jnp.bfloat16)
    result = jnp.dot(hidden, down_full, preferred_element_type=jnp.float32)
    return (result * weight[:, None]).astype(jnp.bfloat16)


def local_any(
    batch_one,
    batch_two,
    norm_gain,
    slots_one,
    slots_two,
    gates_one,
    gates_two,
    table_old,
    table_new,
    gate_old,
    up_old,
    down_old,
):
    group = table_old.shape[0]
    me = lax.axis_index("expert")
    gate_full = lax.all_gather(gate_old[0], "tensor", axis=0, tiled=True)
    up_full = lax.all_gather(up_old[0], "tensor", axis=0, tiled=True)
    down_full = lax.all_gather(down_old[0], "tensor", axis=1, tiled=True)
    rows_one = lax.all_gather(rms_rows(batch_one, norm_gain), "expert", axis=0, tiled=True)
    rows_two = lax.all_gather(rms_rows(batch_two, norm_gain), "expert", axis=0, tiled=True)
    own = jnp.arange(group, dtype=jnp.int32)
    weights = jnp.stack(
        [
            slot_weights(slots_one, gates_one, own),
            slot_weights(slots_two, gates_two, source_slots(table_old, table_new)),
        ]
    )
    all_weights = lax.all_gather(weights, "expert", axis=1, tiled=True)
    mine = lax.dynamic_index_in_dim(all_weights, me, axis=2, keepdims=False)
    outs = []
    for rows, weight in ((rows_one, mine[0]), (rows_two, mine[1])):
        part = expert_part(rows, weight, gate_full, up_full, down_full)
        outs.append(lax.psum_scatter(part, "expert", scatter_dimension=0, tiled=True))
    return tuple(outs)


def call(body, outs, ins, vmem_mb, flops=0, moved=0, scratch=(), specs=None):
    smem = pl.BlockSpec(memory_space=pltpu.SMEM)
    vmem = pl.BlockSpec(memory_space=pltpu.VMEM)
    return pl.pallas_call(
        body,
        out_shape=outs,
        in_specs=specs
        or [smem if x.ndim == 1 and x.dtype == jnp.int32 else vmem for x in ins],
        out_specs=jax.tree.map(lambda _: vmem, outs),
        scratch_shapes=list(scratch),
        compiler_params=pltpu.CompilerParams(vmem_limit_bytes=vmem_mb * 1024 * 1024),
        cost_estimate=pl.CostEstimate(flops=flops, bytes_accessed=moved, transcendentals=0),
    )(*ins)


def prepare_kernel(*refs):
    hbm, outs, held, sems = refs[:9], refs[9:11], refs[11:20], refs[20]
    copies = [pltpu.make_async_copy(a, b, sems.at[i]) for i, (a, b) in enumerate(zip(hbm, held))]
    for copy in copies:
        copy.start()
    for copy in copies:
        copy.wait()
    old_ref, new_ref = held[7:]
    group = old_ref.shape[0]
    sources = []
    for s in range(group):
        left, right = (s - 1) % group, (s + 1) % group
        wanted = new_ref[s]
        other = jnp.where(wanted == old_ref[left], left, right)
        sources.append(jnp.where(wanted == old_ref[s], s, other))
    gain = held[0][...].astype(jnp.float32).reshape(1, -1)
    for b in range(2):
        tokens_ref, slots_ref, gates_ref = held[1 + b], held[3 + b], held[5 + b]
        out_ref = outs[b]
        tok, width = tokens_ref.shape
        values = tokens_ref[...].astype(jnp.float32)
        square = jnp.mean(values * values, axis=-1, keepdims=True)
        out_ref[:, :width] = (values * lax.rsqrt(square + EPS) * gain).astype(jnp.bfloat16)
        slots, gates = slots_ref[...], gates_ref[...]
        if b == 1:
            holder = jnp.zeros_like(slots)
            for s in range(group):
                holder = jnp.where(slots == s, sources[s], holder)
            slots = holder
        expert = lax.broadcasted_iota(jnp.int32, (group, tok), 0)
        total = jnp.zeros((group, tok), jnp.float32)
        for k in range(slots.shape[0]):
            total += jnp.where(expert == slots[k : k + 1, :], gates[k : k + 1, :], 0.0)
        high = total.astype(jnp.bfloat16)
        rest = total - high.astype(jnp.float32)
        middle = rest.astype(jnp.bfloat16)
        low = (rest - middle.astype(jnp.float32)).astype(jnp.bfloat16)
        packed = jnp.concatenate([high, middle, low], axis=0)
        row = lax.broadcasted_iota(jnp.int32, (3 * group, PACK), 0)
        lane = lax.broadcasted_iota(jnp.int32, (3 * group, PACK), 1)
        turned = lax.dot_general(
            packed,
            (row == lane).astype(jnp.bfloat16),
            (((0,), (0,)), ((), ())),
            preferred_element_type=jnp.float32,
        )
        out_ref[:, width:] = turned.astype(jnp.bfloat16)


def hidden_of(place, rows_ref, gate_refs, up_refs, begin, count):
    depth = gate_refs[0].shape[0]
    acts = [None, None]
    for which in range(2):
        half = place if which == 0 else 1 - place
        columns = pl.ds(pl.multiple_of(half * depth, depth), depth)
        rows = rows_ref[pl.ds(begin, count), columns]
        for i, refs in enumerate((gate_refs, up_refs)):
            term = jnp.dot(rows, refs[which][...], preferred_element_type=jnp.float32)
            acts[i] = term if acts[i] is None else acts[i] + term
    gate_act, up_act = acts
    return (gate_act / (1.0 + jnp.exp(-gate_act)) * up_act).astype(jnp.bfloat16)


def weight_of(expert, group, packed):
    lane = lax.broadcasted_iota(jnp.int32, packed.shape, 1)
    chosen = (lane & (group - 1)) == expert
    return jnp.sum(jnp.where(chosen, packed.astype(jnp.float32), 0.0), axis=1, keepdims=True)


def own_kernel(pieces, group, *refs):
    piece_refs, refs = refs[:pieces], refs[pieces:]
    gate_a, gate_b, up_a, up_b, down_a, down_b, total_ref, rows_ref = refs
    tok = piece_refs[0].shape[0]
    width = total_ref.shape[1]
    for i, ref in enumerate(piece_refs):
        rows_ref[i * tok : (i + 1) * tok, :] = ref[...]
    place, expert = lax.axis_index("tensor"), lax.axis_index("expert")
    block = 256

    @pl.loop(0, rows_ref.shape[0] // block)
    def _(step):
        begin = pl.multiple_of(step * block, block)
        hidden = hidden_of(place, rows_ref, (gate_a, gate_b), (up_a, up_b), begin, block)
        weight = weight_of(expert, group, rows_ref[pl.ds(begin, block), width:])
        for which, ref in enumerate((down_a, down_b)):
            half = place if which == 0 else 1 - place
            columns = pl.ds(pl.multiple_of(half * ref.shape[1], ref.shape[1]), ref.shape[1])
            part = jnp.dot(hidden, ref[...], preferred_element_type=jnp.float32)
            total_ref[pl.ds(begin, block), columns] = part * weight


def beside_kernel(pieces, group, *refs):
    piece_refs, refs = refs[:pieces], refs[pieces:]
    gate_a, gate_b, up_a, up_b, hidden_ref, weight_ref, rows_ref = refs
    tok = piece_refs[0].shape[0]
    width = rows_ref.shape[1] - PACK
    for i, ref in enumerate(piece_refs):
        rows_ref[i * tok : (i + 1) * tok, :] = ref[...]
    place, expert = lax.axis_index("tensor"), lax.axis_index("expert") ^ Z_LOW
    block = 256

    @pl.loop(0, rows_ref.shape[0] // block)
    def _(step):
        begin = pl.multiple_of(step * block, block)
        hidden_ref[pl.ds(begin, block), :] = hidden_of(
            place, rows_ref, (gate_a, gate_b), (up_a, up_b), begin, block
        )
        weight = weight_of(expert, group, rows_ref[pl.ds(begin, block), width:])
        weight_ref[pl.ds(begin, block), :] = jnp.broadcast_to(weight, (block, PACK))


def join_kernel(hidden_ref, weight_ref, total_ref, down_a, down_b, send_a, send_b, keep_a, keep_b):
    place = lax.axis_index("tensor")
    count = send_a.shape[0]
    for pair, outs in ((0, (send_a, send_b)), (1, (keep_a, keep_b))):
        rows = slice(pair * 2 * count, (pair + 1) * 2 * count)
        weight = weight_ref[rows, :1]
        for which, ref in enumerate((down_a, down_b)):
            half = place if which == 0 else 1 - place
            columns = pl.ds(pl.multiple_of(half * ref.shape[1], ref.shape[1]), ref.shape[1])
            part = jnp.dot(hidden_ref[rows, :], ref[...], preferred_element_type=jnp.float32)
            part = part * weight + total_ref[rows, columns]
            outs[0][:, columns] = part[:count].astype(outs[0].dtype)
            outs[1][:, columns] = part[count:].astype(outs[1].dtype)


def first_sum_kernel(keep_ref, got_ref, send_ref, held_ref):
    half = held_ref.shape[0]
    held_ref[...] = keep_ref[:half] + got_ref[:half].astype(jnp.float32)
    send_ref[...] = (keep_ref[half:] + got_ref[half:].astype(jnp.float32)).astype(jnp.bfloat16)


def second_sum_kernel(keep_a, got_a, keep_b, got_b, send_ref, held_ref):
    half = keep_a.shape[0] // 2
    for i, (keep, got) in enumerate(((keep_a, got_a), (keep_b, got_b))):
        rows = slice(i * half, (i + 1) * half)
        held_ref[rows, :] = keep[:half] + got[:half].astype(jnp.float32)
        send_ref[rows, :] = (keep[half:] + got[half:].astype(jnp.float32)).astype(jnp.bfloat16)


def last_sum_kernel(keep_ref, got_ref, out_ref):
    out_ref[...] = (keep_ref[...] + got_ref[...].astype(jnp.float32)).astype(jnp.bfloat16)


def swap(block, distance):
    count = lax.axis_size("expert")
    return lax.ppermute(block, "expert", [(i, i ^ distance) for i in range(count)])


def pair_gather(block):
    count = lax.axis_size("expert")
    pairs = [[i, i | Z_LOW] for i in range(count) if not i & Z_LOW]
    return lax.all_gather(block, "expert", axis_index_groups=pairs)


def beside_copy_kernel(pair_ref, out_ref, sem):
    other = 1 - lax.axis_index("expert") // Z_LOW % 2
    copy = pltpu.make_async_copy(pair_ref.at[other], out_ref, sem)
    copy.start()
    copy.wait()


def beside(pair):
    return call(
        beside_copy_kernel,
        jax.ShapeDtypeStruct(pair.shape[1:], pair.dtype),
        (pair,),
        4,
        0,
        2 * pair.size,
        [pltpu.SemaphoreType.DMA],
        [pl.BlockSpec(memory_space=pltpu.HBM)],
    )


def swap_core(block):
    return lax.ppermute(block, "tensor", [(0, 1), (1, 0)])


def halves(own, far):
    half = own.shape[0] // 2
    return [jnp.concatenate([own[i : i + half], far[i : i + half]]) for i in (0, half)]


def spread(a1, b1, a2, b2):
    a3, b3 = swap(a1, Y), swap(b1, X)
    a4, b4 = swap(a2, Y), swap(b2, X)
    return [a3, a4, b3, b4, a1, a2, b1, b2]


def first_return(send_a, send_b, keep_a, keep_b):
    quarter, width = keep_a.shape[0] // 2, keep_a.shape[1]
    outs = (
        jax.ShapeDtypeStruct((quarter, width), jnp.bfloat16),
        jax.ShapeDtypeStruct((quarter, width), jnp.float32),
    )
    size = quarter * width
    got_a, got_b = swap(send_a, Y), swap(send_b, X)
    next_a, held_a = call(first_sum_kernel, outs, (keep_a, got_a), 8, size, 18 * size)
    next_b, held_b = call(first_sum_kernel, outs, (keep_b, got_b), 8, size, 18 * size)
    return next_a, next_b, held_a, held_b


def last_returns(next_a, next_b, held_a, held_b):
    outs = (
        jax.ShapeDtypeStruct(held_a.shape, jnp.bfloat16),
        jax.ShapeDtypeStruct(held_a.shape, jnp.float32),
    )
    size = held_a.size
    got_a, got_b = swap(next_a, X), swap(next_b, Y)
    next_z, held_z = call(
        second_sum_kernel, outs, (held_a, got_a, held_b, got_b), 8, size, 18 * size
    )
    got_z = swap(next_z, Z_HIGH)
    return call(last_sum_kernel, outs[0], (held_z, got_z), 8, size, 8 * size)


def local_pairs(
    batch_one,
    batch_two,
    norm_gain,
    slots_one,
    slots_two,
    gates_one,
    gates_two,
    table_old,
    table_new,
    gate_old,
    up_old,
    down_old,
):
    group = table_old.shape[0]
    tok, width = batch_one.shape
    ff = gate_old.shape[2]
    gate, up, down = gate_old[0], up_old[0], down_old[0]
    held = (
        norm_gain, batch_one, batch_two, slots_one.T, slots_two.T, gates_one.T, gates_two.T,
        table_old, table_new,
    )
    hbm = pl.BlockSpec(memory_space=pltpu.HBM)
    own = call(
        prepare_kernel,
        (jax.ShapeDtypeStruct((tok, width + PACK), jnp.bfloat16),) * 2,
        held,
        8,
        10 * tok * width,
        8 * tok * width,
        [(pltpu.SMEM if x.ndim == 1 and x.dtype == jnp.int32 else pltpu.VMEM)(x.shape, x.dtype) for x in held]
        + [pltpu.SemaphoreType.DMA((len(held),))],
        [hbm] * len(held),
    )
    mine = (gate, up, down)
    gathered = [pair_gather(w) for w in mine]
    twins = [swap_core(w) for w in mine]
    far = [swap(x, Z_HIGH) for x in own]
    far[0], twins = lax.optimization_barrier((far[0], twins))
    first_one = halves(own[0], far[0])
    second_one = swap(first_one[0], X), swap(first_one[1], Y)
    far[1], second_one = lax.optimization_barrier((far[1], second_one))
    first_two = halves(own[1], far[1])
    second_two = swap(first_two[0], X), swap(first_two[1], Y)
    pieces = [spread(*first_one, *second_one), spread(*first_two, *second_two)]

    rows = 8 * tok
    scratch = (pltpu.VMEM((rows, width + PACK), jnp.bfloat16),)

    def own_total(p):
        return call(
            functools.partial(own_kernel, 8, group),
            jax.ShapeDtypeStruct((rows, width), jnp.float32),
            (*p, gate, twins[0], up, twins[1], down, twins[2]),
            20,
            6 * rows * width * ff,
            6 * width * ff + 6 * rows * width,
            scratch,
        )

    def beside_hidden(p):
        return call(
            functools.partial(beside_kernel, 8, group),
            (
                jax.ShapeDtypeStruct((rows, ff), jnp.bfloat16),
                jax.ShapeDtypeStruct((rows, PACK), jnp.float32),
            ),
            (*p, gate_by, gate_twin, up_by, up_twin),
            16,
            4 * rows * width * ff,
            4 * width * ff + 2 * rows * width,
            scratch,
        )

    def join(total, hid, weight):
        return call(
            join_kernel,
            (jax.ShapeDtypeStruct((2 * tok, width), jnp.bfloat16),) * 2
            + (jax.ShapeDtypeStruct((2 * tok, width), jnp.float32),) * 2,
            (hid, weight, total, down_by, down_twin),
            14,
            2 * rows * width * ff,
            2 * width * ff + 8 * rows * width,
        )

    total_one, total_two = own_total(pieces[0]), own_total(pieces[1])
    gate_pair, up_pair, total_one, total_two = lax.optimization_barrier(
        (*gathered[:2], total_one, total_two)
    )
    gate_by, up_by = beside(gate_pair), beside(up_pair)
    gate_twin, up_twin = swap_core(gate_by), swap_core(up_by)
    hidden_one, hidden_two = beside_hidden(pieces[0]), beside_hidden(pieces[1])
    down_pair, hidden_one, hidden_two = lax.optimization_barrier(
        (gathered[2], hidden_one, hidden_two)
    )
    down_by = beside(down_pair)
    down_twin = swap_core(down_by)
    back_one = first_return(*join(total_one, *hidden_one))
    back_two = first_return(*join(total_two, *hidden_two))
    return last_returns(*back_one), last_returns(*back_two)


def solution(mesh):
    in_specs = (
        P(("expert", "tensor"), None),
        P(("expert", "tensor"), None),
        P(),
        P(("expert", "tensor"), None),
        P(("expert", "tensor"), None),
        P(("expert", "tensor"), None),
        P(("expert", "tensor"), None),
        P(),
        P(),
        P("expert", "tensor", None),
        P("expert", "tensor", None),
        P("expert", None, "tensor"),
    )
    out_specs = (P(("expert", "tensor"), None), P(("expert", "tensor"), None))
    local = local_pairs if (mesh.shape["expert"], mesh.shape["tensor"]) == (16, 2) else local_any
    return jax.shard_map(local, mesh=mesh, in_specs=in_specs, out_specs=out_specs, check_vma=False)
```

```python
import functools

import jax
import jax.numpy as jnp
from jax import lax
from jax.experimental import pallas as pl
from jax.experimental.pallas import tpu as pltpu
from jax.sharding import PartitionSpec as P

EPS = 1e-05
PACK = 128
X, Y = 1, 2
Z_WAYS = (12, 8, 4)


def rms_rows(tokens, norm_gain):
    values = tokens.astype(jnp.float32)
    square = jnp.mean(values * values, axis=-1, keepdims=True)
    return (values * lax.rsqrt(square + EPS) * norm_gain.astype(jnp.float32)).astype(jnp.bfloat16)


def source_slots(table_old, table_new):
    group = table_old.shape[0]
    slot_index = jnp.arange(group, dtype=jnp.int32)
    picked = jnp.where(
        table_new == jnp.roll(table_old, 1), (slot_index - 1) % group, (slot_index + 1) % group
    )
    return jnp.where(table_new == table_old, slot_index, picked).astype(jnp.int32)


def slot_weights(route_slots, route_gates, held_by):
    group = held_by.shape[0]
    hit = route_slots[:, :, None] == jnp.arange(group, dtype=jnp.int32)
    by_slot = jnp.sum(jnp.where(hit, route_gates[:, :, None], 0.0), axis=1)
    moved = held_by[:, None] == jnp.arange(group, dtype=jnp.int32)
    return jnp.sum(jnp.where(moved[None], by_slot[:, :, None], 0.0), axis=1)


def expert_part(rows, weight, gate_full, up_full, down_full):
    gate_act = jnp.dot(rows, gate_full, preferred_element_type=jnp.float32)
    up_act = jnp.dot(rows, up_full, preferred_element_type=jnp.float32)
    hidden = (jax.nn.silu(gate_act) * up_act).astype(jnp.bfloat16)
    result = jnp.dot(hidden, down_full, preferred_element_type=jnp.float32)
    return (result * weight[:, None]).astype(jnp.bfloat16)


def local_any(
    batch_one,
    batch_two,
    norm_gain,
    slots_one,
    slots_two,
    gates_one,
    gates_two,
    table_old,
    table_new,
    gate_old,
    up_old,
    down_old,
):
    group = table_old.shape[0]
    me = lax.axis_index("expert")
    gate_full = lax.all_gather(gate_old[0], "tensor", axis=0, tiled=True)
    up_full = lax.all_gather(up_old[0], "tensor", axis=0, tiled=True)
    down_full = lax.all_gather(down_old[0], "tensor", axis=1, tiled=True)
    rows_one = lax.all_gather(rms_rows(batch_one, norm_gain), "expert", axis=0, tiled=True)
    rows_two = lax.all_gather(rms_rows(batch_two, norm_gain), "expert", axis=0, tiled=True)
    own = jnp.arange(group, dtype=jnp.int32)
    weights = jnp.stack(
        [
            slot_weights(slots_one, gates_one, own),
            slot_weights(slots_two, gates_two, source_slots(table_old, table_new)),
        ]
    )
    all_weights = lax.all_gather(weights, "expert", axis=1, tiled=True)
    mine = lax.dynamic_index_in_dim(all_weights, me, axis=2, keepdims=False)
    outs = []
    for rows, weight in ((rows_one, mine[0]), (rows_two, mine[1])):
        part = expert_part(rows, weight, gate_full, up_full, down_full)
        outs.append(lax.psum_scatter(part, "expert", scatter_dimension=0, tiled=True))
    return tuple(outs)


def call(body, outs, ins, vmem_mb, flops=0, moved=0, scratch=(), specs=None):
    smem = pl.BlockSpec(memory_space=pltpu.SMEM)
    vmem = pl.BlockSpec(memory_space=pltpu.VMEM)
    return pl.pallas_call(
        body,
        out_shape=outs,
        in_specs=specs
        or [smem if x.ndim == 1 and x.dtype == jnp.int32 else vmem for x in ins],
        out_specs=jax.tree.map(lambda _: vmem, outs),
        scratch_shapes=list(scratch),
        compiler_params=pltpu.CompilerParams(vmem_limit_bytes=vmem_mb * 1024 * 1024),
        cost_estimate=pl.CostEstimate(flops=flops, bytes_accessed=moved, transcendentals=0),
    )(*ins)


def prepare_kernel(*refs):
    hbm, outs, held, sems = refs[:9], refs[9:11], refs[11:20], refs[20]
    copies = [pltpu.make_async_copy(a, b, sems.at[i]) for i, (a, b) in enumerate(zip(hbm, held))]
    for copy in copies:
        copy.start()
    for copy in copies:
        copy.wait()
    old_ref, new_ref = held[7:]
    group = old_ref.shape[0]
    sources = []
    for s in range(group):
        left, right = (s - 1) % group, (s + 1) % group
        wanted = new_ref[s]
        other = jnp.where(wanted == old_ref[left], left, right)
        sources.append(jnp.where(wanted == old_ref[s], s, other))
    gain = held[0][...].astype(jnp.float32).reshape(1, -1)
    for b in range(2):
        tokens_ref, slots_ref, gates_ref = held[1 + b], held[3 + b], held[5 + b]
        out_ref = outs[b]
        tok, width = tokens_ref.shape
        values = tokens_ref[...].astype(jnp.float32)
        square = jnp.mean(values * values, axis=-1, keepdims=True)
        out_ref[:, :width] = (values * lax.rsqrt(square + EPS) * gain).astype(jnp.bfloat16)
        slots, gates = slots_ref[...], gates_ref[...]
        if b == 1:
            holder = jnp.zeros_like(slots)
            for s in range(group):
                holder = jnp.where(slots == s, sources[s], holder)
            slots = holder
        expert = lax.broadcasted_iota(jnp.int32, (group, tok), 0)
        total = jnp.zeros((group, tok), jnp.float32)
        for k in range(slots.shape[0]):
            total += jnp.where(expert == slots[k : k + 1, :], gates[k : k + 1, :], 0.0)
        high = total.astype(jnp.bfloat16)
        rest = total - high.astype(jnp.float32)
        middle = rest.astype(jnp.bfloat16)
        low = (rest - middle.astype(jnp.float32)).astype(jnp.bfloat16)
        packed = jnp.concatenate([high, middle, low], axis=0)
        row = lax.broadcasted_iota(jnp.int32, (3 * group, PACK), 0)
        lane = lax.broadcasted_iota(jnp.int32, (3 * group, PACK), 1)
        turned = lax.dot_general(
            packed,
            (row == lane).astype(jnp.bfloat16),
            (((0,), (0,)), ((), ())),
            preferred_element_type=jnp.float32,
        )
        out_ref[:, width:] = turned.astype(jnp.bfloat16)


def pack_kernel(gate_ref, up_ref, both_ref, sems):
    ff = gate_ref.shape[1]
    copies = [
        pltpu.make_async_copy(gate_ref, both_ref.at[:, :ff], sems.at[0]),
        pltpu.make_async_copy(up_ref, both_ref.at[:, ff:], sems.at[1]),
    ]
    for copy in copies:
        copy.start()
    for copy in copies:
        copy.wait()


def hidden_of(place, rows_ref, both_refs, begin, count):
    depth, ff = both_refs[0].shape[0], both_refs[0].shape[1] // 2
    acts = None
    for which, ref in enumerate(both_refs):
        half = place if which == 0 else 1 - place
        columns = pl.ds(pl.multiple_of(half * depth, depth), depth)
        rows = rows_ref[pl.ds(begin, count), columns]
        term = jnp.dot(rows, ref[...], preferred_element_type=jnp.float32)
        acts = term if acts is None else acts + term
    gate_act, up_act = acts[:, :ff], acts[:, ff:]
    return (gate_act / (1.0 + jnp.exp(-gate_act)) * up_act).astype(jnp.bfloat16)


def weight_of(expert, group, packed):
    lane = lax.broadcasted_iota(jnp.int32, packed.shape, 1)
    chosen = (lane & (group - 1)) == expert
    return jnp.sum(jnp.where(chosen, packed.astype(jnp.float32), 0.0), axis=1, keepdims=True)


def own_kernel(pieces, group, *refs):
    piece_refs, refs = refs[:pieces], refs[pieces:]
    both_a, both_b, down_a, down_b, total_ref, rows_ref = refs
    tok = piece_refs[0].shape[0]
    width = total_ref.shape[1]
    for i, ref in enumerate(piece_refs):
        rows_ref[i * tok : (i + 1) * tok, :] = ref[...]
    place, expert = lax.axis_index("tensor"), lax.axis_index("expert")
    block = 256

    @pl.loop(0, rows_ref.shape[0] // block)
    def _(step):
        begin = pl.multiple_of(step * block, block)
        hidden = hidden_of(place, rows_ref, (both_a, both_b), begin, block)
        weight = weight_of(expert, group, rows_ref[pl.ds(begin, block), width:])
        for which, ref in enumerate((down_a, down_b)):
            half = place if which == 0 else 1 - place
            columns = pl.ds(pl.multiple_of(half * ref.shape[1], ref.shape[1]), ref.shape[1])
            part = jnp.dot(hidden, ref[...], preferred_element_type=jnp.float32)
            total_ref[pl.ds(begin, block), columns] = part * weight


def beside_kernel(pieces, group, *refs):
    piece_refs, refs = refs[:pieces], refs[pieces:]
    both_a, both_b, hidden_ref, weight_ref, rows_ref = refs
    tok = piece_refs[0].shape[0]
    width = rows_ref.shape[1] - PACK
    for i, ref in enumerate(piece_refs):
        rows_ref[i * tok : (i + 1) * tok, :] = ref[...]
    place, expert = lax.axis_index("tensor"), lax.axis_index("expert") ^ X
    block = 256

    @pl.loop(0, rows_ref.shape[0] // block)
    def _(step):
        begin = pl.multiple_of(step * block, block)
        hidden_ref[pl.ds(begin, block), :] = hidden_of(
            place, rows_ref, (both_a, both_b), begin, block
        )
        weight = weight_of(expert, group, rows_ref[pl.ds(begin, block), width:])
        weight_ref[pl.ds(begin, block), :] = jnp.broadcast_to(weight, (block, PACK))


def join_kernel(hidden_ref, weight_ref, total_ref, down_a, down_b, *outs):
    place = lax.axis_index("tensor")
    count = outs[0].shape[0]
    block = 4 * count
    for part in range(len(outs) // 4):
        rows = slice(part * block, (part + 1) * block)
        weight = weight_ref[rows, :1]
        for which, ref in enumerate((down_a, down_b)):
            half = place if which == 0 else 1 - place
            columns = pl.ds(pl.multiple_of(half * ref.shape[1], ref.shape[1]), ref.shape[1])
            result = jnp.dot(hidden_ref[rows, :], ref[...], preferred_element_type=jnp.float32)
            result = result * weight + total_ref[rows, columns]
            for i, out in enumerate(outs[4 * part : 4 * part + 4]):
                out[:, columns] = result[i * count : (i + 1) * count].astype(out.dtype)


def sum_kernel(*refs):
    total = refs[0][...].astype(jnp.float32)
    for ref in refs[1:-1]:
        total = total + ref[...].astype(jnp.float32)
    refs[-1][...] = total.astype(jnp.bfloat16)


def swap(block, distance):
    count = lax.axis_size("expert")
    return lax.ppermute(block, "expert", [(i, i ^ distance) for i in range(count)])


def swap_core(block):
    return lax.ppermute(block, "tensor", [(0, 1), (1, 0)])


def line(own):
    return [swap(own, way) for way in Z_WAYS] + [own]


def add(*terms):
    out = jax.ShapeDtypeStruct(terms[0].shape, jnp.bfloat16)
    size = terms[0].size
    return call(sum_kernel, out, terms, 8, len(terms) * size, 4 * len(terms) * size)


def send_back(parts):
    leave, stay = parts[:4], parts[4:]
    got = [swap(x, Y) for x in leave]
    far = [swap(add(x, y), way) for x, y, way in zip(stay, got, Z_WAYS)]
    return add(stay[3], got[3], *far)


def local_pairs(
    batch_one,
    batch_two,
    norm_gain,
    slots_one,
    slots_two,
    gates_one,
    gates_two,
    table_old,
    table_new,
    gate_old,
    up_old,
    down_old,
):
    group = table_old.shape[0]
    tok, width = batch_one.shape
    ff = gate_old.shape[2]
    gate, up, down = gate_old[0], up_old[0], down_old[0]
    held = (
        norm_gain, batch_one, batch_two, slots_one.T, slots_two.T, gates_one.T, gates_two.T,
        table_old, table_new,
    )
    hbm = pl.BlockSpec(memory_space=pltpu.HBM)
    own = call(
        prepare_kernel,
        (jax.ShapeDtypeStruct((tok, width + PACK), jnp.bfloat16),) * 2,
        held,
        8,
        10 * tok * width,
        8 * tok * width,
        [(pltpu.SMEM if x.ndim == 1 and x.dtype == jnp.int32 else pltpu.VMEM)(x.shape, x.dtype) for x in held]
        + [pltpu.SemaphoreType.DMA((len(held),))],
        [hbm] * len(held),
    )
    both = call(
        pack_kernel,
        jax.ShapeDtypeStruct((gate.shape[0], 2 * ff), jnp.bfloat16),
        (gate, up),
        8,
        0,
        8 * gate.size,
        [pltpu.SemaphoreType.DMA((2,))],
        [hbm] * 2,
    )
    both_by = swap(both, X)
    twins = (swap_core(both), swap_core(down))
    line_one = line(own[0])
    line_one[:2], twins, own_two = lax.optimization_barrier((line_one[:2], twins, own[1]))
    line_two = line(own_two)
    pieces_one = [swap(x, Y) for x in line_one] + line_one
    pieces_one, line_two = lax.optimization_barrier((pieces_one, line_two))
    pieces = [pieces_one, [swap(x, Y) for x in line_two] + line_two]

    rows = 8 * tok
    scratch = (pltpu.VMEM((rows, width + PACK), jnp.bfloat16),)

    def own_total(p):
        return call(
            functools.partial(own_kernel, 8, group),
            jax.ShapeDtypeStruct((rows, width), jnp.float32),
            (*p, both, twins[0], down, twins[1]),
            20,
            6 * rows * width * ff,
            6 * width * ff + 6 * rows * width,
            scratch,
        )

    def beside_hidden(p):
        return call(
            functools.partial(beside_kernel, 8, group),
            (
                jax.ShapeDtypeStruct((rows, ff), jnp.bfloat16),
                jax.ShapeDtypeStruct((rows, PACK), jnp.float32),
            ),
            (*p, both_by, both_twin),
            16,
            4 * rows * width * ff,
            4 * width * ff + 2 * rows * width,
            scratch,
        )

    def join(total, hid, weight):
        return call(
            join_kernel,
            (jax.ShapeDtypeStruct((tok, width), jnp.bfloat16),) * 4
            + (jax.ShapeDtypeStruct((tok, width), jnp.float32),) * 4,
            (hid, weight, total, down_by, down_twin),
            14,
            2 * rows * width * ff,
            2 * width * ff + 8 * rows * width,
        )

    total_one = own_total(pieces[0])
    down_later, both_by, total_one = lax.optimization_barrier((down, both_by, total_one))
    down_by = swap(down_later, X)
    both_twin = swap_core(both_by)
    total_two = own_total(pieces[1])
    hidden_one, hidden_two = beside_hidden(pieces[0]), beside_hidden(pieces[1])
    down_by, total_two, hidden_one, hidden_two = lax.optimization_barrier(
        (down_by, total_two, hidden_one, hidden_two)
    )
    down_twin = swap_core(down_by)
    return send_back(join(total_one, *hidden_one)), send_back(join(total_two, *hidden_two))


def solution(mesh):
    in_specs = (
        P(("expert", "tensor"), None),
        P(("expert", "tensor"), None),
        P(),
        P(("expert", "tensor"), None),
        P(("expert", "tensor"), None),
        P(("expert", "tensor"), None),
        P(("expert", "tensor"), None),
        P(),
        P(),
        P("expert", "tensor", None),
        P("expert", "tensor", None),
        P("expert", None, "tensor"),
    )
    out_specs = (P(("expert", "tensor"), None), P(("expert", "tensor"), None))
    local = local_pairs if (mesh.shape["expert"], mesh.shape["tensor"]) == (16, 2) else local_any
    return jax.shard_map(local, mesh=mesh, in_specs=in_specs, out_specs=out_specs, check_vma=False)
```

```python
import functools

import jax
import jax.numpy as jnp
from jax import lax
from jax.experimental import pallas as pl
from jax.experimental.pallas import tpu as pltpu
from jax.sharding import PartitionSpec as P

EPS = 1e-05
PACK = 128
X, Y, Z_LOW, Z_HIGH = 1, 2, 4, 8


def rms_rows(tokens, norm_gain):
    values = tokens.astype(jnp.float32)
    square = jnp.mean(values * values, axis=-1, keepdims=True)
    return (values * lax.rsqrt(square + EPS) * norm_gain.astype(jnp.float32)).astype(jnp.bfloat16)


def source_slots(table_old, table_new):
    group = table_old.shape[0]
    slot_index = jnp.arange(group, dtype=jnp.int32)
    picked = jnp.where(
        table_new == jnp.roll(table_old, 1), (slot_index - 1) % group, (slot_index + 1) % group
    )
    return jnp.where(table_new == table_old, slot_index, picked).astype(jnp.int32)


def slot_weights(route_slots, route_gates, held_by):
    group = held_by.shape[0]
    hit = route_slots[:, :, None] == jnp.arange(group, dtype=jnp.int32)
    by_slot = jnp.sum(jnp.where(hit, route_gates[:, :, None], 0.0), axis=1)
    moved = held_by[:, None] == jnp.arange(group, dtype=jnp.int32)
    return jnp.sum(jnp.where(moved[None], by_slot[:, :, None], 0.0), axis=1)


def expert_part(rows, weight, gate_full, up_full, down_full):
    gate_act = jnp.dot(rows, gate_full, preferred_element_type=jnp.float32)
    up_act = jnp.dot(rows, up_full, preferred_element_type=jnp.float32)
    hidden = (jax.nn.silu(gate_act) * up_act).astype(jnp.bfloat16)
    result = jnp.dot(hidden, down_full, preferred_element_type=jnp.float32)
    return (result * weight[:, None]).astype(jnp.bfloat16)


def local_any(
    batch_one,
    batch_two,
    norm_gain,
    slots_one,
    slots_two,
    gates_one,
    gates_two,
    table_old,
    table_new,
    gate_old,
    up_old,
    down_old,
):
    group = table_old.shape[0]
    me = lax.axis_index("expert")
    gate_full = lax.all_gather(gate_old[0], "tensor", axis=0, tiled=True)
    up_full = lax.all_gather(up_old[0], "tensor", axis=0, tiled=True)
    down_full = lax.all_gather(down_old[0], "tensor", axis=1, tiled=True)
    rows_one = lax.all_gather(rms_rows(batch_one, norm_gain), "expert", axis=0, tiled=True)
    rows_two = lax.all_gather(rms_rows(batch_two, norm_gain), "expert", axis=0, tiled=True)
    own = jnp.arange(group, dtype=jnp.int32)
    weights = jnp.stack(
        [
            slot_weights(slots_one, gates_one, own),
            slot_weights(slots_two, gates_two, source_slots(table_old, table_new)),
        ]
    )
    all_weights = lax.all_gather(weights, "expert", axis=1, tiled=True)
    mine = lax.dynamic_index_in_dim(all_weights, me, axis=2, keepdims=False)
    outs = []
    for rows, weight in ((rows_one, mine[0]), (rows_two, mine[1])):
        part = expert_part(rows, weight, gate_full, up_full, down_full)
        outs.append(lax.psum_scatter(part, "expert", scatter_dimension=0, tiled=True))
    return tuple(outs)


def call(body, outs, ins, vmem_mb, flops=0, moved=0, scratch=(), specs=None):
    smem = pl.BlockSpec(memory_space=pltpu.SMEM)
    vmem = pl.BlockSpec(memory_space=pltpu.VMEM)
    return pl.pallas_call(
        body,
        out_shape=outs,
        in_specs=specs
        or [smem if x.ndim == 1 and x.dtype == jnp.int32 else vmem for x in ins],
        out_specs=jax.tree.map(lambda _: vmem, outs),
        scratch_shapes=list(scratch),
        compiler_params=pltpu.CompilerParams(vmem_limit_bytes=vmem_mb * 1024 * 1024),
        cost_estimate=pl.CostEstimate(flops=flops, bytes_accessed=moved, transcendentals=0),
    )(*ins)


def prepare_kernel(*refs):
    hbm, outs, held, sems = refs[:9], refs[9:11], refs[11:20], refs[20]
    copies = [pltpu.make_async_copy(a, b, sems.at[i]) for i, (a, b) in enumerate(zip(hbm, held))]
    for copy in copies:
        copy.start()
    for copy in copies:
        copy.wait()
    old_ref, new_ref = held[7:]
    group = old_ref.shape[0]
    sources = []
    for s in range(group):
        left, right = (s - 1) % group, (s + 1) % group
        wanted = new_ref[s]
        other = jnp.where(wanted == old_ref[left], left, right)
        sources.append(jnp.where(wanted == old_ref[s], s, other))
    gain = held[0][...].astype(jnp.float32).reshape(1, -1)
    for b in range(2):
        tokens_ref, slots_ref, gates_ref = held[1 + b], held[3 + b], held[5 + b]
        out_ref = outs[b]
        tok, width = tokens_ref.shape
        values = tokens_ref[...].astype(jnp.float32)
        square = jnp.mean(values * values, axis=-1, keepdims=True)
        out_ref[:, :width] = (values * lax.rsqrt(square + EPS) * gain).astype(jnp.bfloat16)
        slots, gates = slots_ref[...], gates_ref[...]
        if b == 1:
            holder = jnp.zeros_like(slots)
            for s in range(group):
                holder = jnp.where(slots == s, sources[s], holder)
            slots = holder
        expert = lax.broadcasted_iota(jnp.int32, (group, tok), 0)
        total = jnp.zeros((group, tok), jnp.float32)
        for k in range(slots.shape[0]):
            total += jnp.where(expert == slots[k : k + 1, :], gates[k : k + 1, :], 0.0)
        high = total.astype(jnp.bfloat16)
        rest = total - high.astype(jnp.float32)
        middle = rest.astype(jnp.bfloat16)
        low = (rest - middle.astype(jnp.float32)).astype(jnp.bfloat16)
        packed = jnp.concatenate([high, middle, low], axis=0)
        row = lax.broadcasted_iota(jnp.int32, (3 * group, PACK), 0)
        lane = lax.broadcasted_iota(jnp.int32, (3 * group, PACK), 1)
        turned = lax.dot_general(
            packed,
            (row == lane).astype(jnp.bfloat16),
            (((0,), (0,)), ((), ())),
            preferred_element_type=jnp.float32,
        )
        out_ref[:, width:] = turned.astype(jnp.bfloat16)


def pack_kernel(gate_ref, up_ref, down_ref, both_ref, first_ref, last_ref, sems):
    ff, half = gate_ref.shape[1], first_ref.shape[0]
    copies = [
        pltpu.make_async_copy(down_ref.at[:half, :], first_ref, sems.at[0]),
        pltpu.make_async_copy(down_ref.at[half:, :], last_ref, sems.at[1]),
        pltpu.make_async_copy(gate_ref, both_ref.at[:, :ff], sems.at[2]),
        pltpu.make_async_copy(up_ref, both_ref.at[:, ff:], sems.at[3]),
    ]
    for copy in copies:
        copy.start()
    for copy in copies:
        copy.wait()


def hidden_of(place, rows_ref, both_refs, begin, count):
    depth, ff = both_refs[0].shape[0], both_refs[0].shape[1] // 2
    acts = None
    for which, ref in enumerate(both_refs):
        half = place if which == 0 else 1 - place
        columns = pl.ds(pl.multiple_of(half * depth, depth), depth)
        rows = rows_ref[pl.ds(begin, count), columns]
        term = jnp.dot(rows, ref[...], preferred_element_type=jnp.float32)
        acts = term if acts is None else acts + term
    gate_act, up_act = acts[:, :ff], acts[:, ff:]
    return (gate_act / (1.0 + jnp.exp(-gate_act)) * up_act).astype(jnp.bfloat16)


def weight_of(expert, group, packed):
    lane = lax.broadcasted_iota(jnp.int32, packed.shape, 1)
    chosen = (lane & (group - 1)) == expert
    return jnp.sum(jnp.where(chosen, packed.astype(jnp.float32), 0.0), axis=1, keepdims=True)


def own_kernel(pieces, group, *refs):
    piece_refs, refs = refs[:pieces], refs[pieces:]
    both_a, both_b, down_a, down_b, total_ref, rows_ref = refs
    tok = piece_refs[0].shape[0]
    width = total_ref.shape[1]
    for i, ref in enumerate(piece_refs):
        rows_ref[i * tok : (i + 1) * tok, :] = ref[...]
    place, expert = lax.axis_index("tensor"), lax.axis_index("expert")
    block = 256

    @pl.loop(0, rows_ref.shape[0] // block)
    def _(step):
        begin = pl.multiple_of(step * block, block)
        hidden = hidden_of(place, rows_ref, (both_a, both_b), begin, block)
        weight = weight_of(expert, group, rows_ref[pl.ds(begin, block), width:])
        for which, ref in enumerate((down_a, down_b)):
            half = place if which == 0 else 1 - place
            columns = pl.ds(pl.multiple_of(half * ref.shape[1], ref.shape[1]), ref.shape[1])
            part = jnp.dot(hidden, ref[...], preferred_element_type=jnp.float32)
            total_ref[pl.ds(begin, block), columns] = part * weight


def beside_kernel(pieces, group, *refs):
    piece_refs, refs = refs[:pieces], refs[pieces:]
    both_a, both_b, hidden_ref, weight_ref, rows_ref = refs
    tok = piece_refs[0].shape[0]
    width = rows_ref.shape[1] - PACK
    for i, ref in enumerate(piece_refs):
        rows_ref[i * tok : (i + 1) * tok, :] = ref[...]
    place, expert = lax.axis_index("tensor"), lax.axis_index("expert") ^ Z_LOW
    block = 256

    @pl.loop(0, rows_ref.shape[0] // block)
    def _(step):
        begin = pl.multiple_of(step * block, block)
        hidden_ref[pl.ds(begin, block), :] = hidden_of(
            place, rows_ref, (both_a, both_b), begin, block
        )
        weight = weight_of(expert, group, rows_ref[pl.ds(begin, block), width:])
        weight_ref[pl.ds(begin, block), :] = jnp.broadcast_to(weight, (block, PACK))


def join_kernel(
    hidden_ref, weight_ref, total_ref, first_a, last_a, first_b, last_b, send_a, send_b, keep_a, keep_b
):
    place = lax.axis_index("tensor")
    count = send_a.shape[0]
    inner, width = first_a.shape
    for pair, outs in ((0, (send_a, send_b)), (1, (keep_a, keep_b))):
        rows = slice(pair * 2 * count, (pair + 1) * 2 * count)
        weight = weight_ref[rows, :1]
        for which, (first, last) in enumerate(((first_a, last_a), (first_b, last_b))):
            half = place if which == 0 else 1 - place
            columns = pl.ds(pl.multiple_of(half * width, width), width)
            part = jnp.dot(
                hidden_ref[rows, :inner], first[...], preferred_element_type=jnp.float32
            ) + jnp.dot(hidden_ref[rows, inner:], last[...], preferred_element_type=jnp.float32)
            part = part * weight + total_ref[rows, columns]
            outs[0][:, columns] = part[:count].astype(outs[0].dtype)
            outs[1][:, columns] = part[count:].astype(outs[1].dtype)


def first_sum_kernel(keep_ref, got_ref, send_ref, held_ref):
    half = held_ref.shape[0]
    held_ref[...] = keep_ref[:half] + got_ref[:half].astype(jnp.float32)
    send_ref[...] = (keep_ref[half:] + got_ref[half:].astype(jnp.float32)).astype(jnp.bfloat16)


def second_sum_kernel(keep_a, got_a, keep_b, got_b, send_ref, held_ref):
    half = keep_a.shape[0] // 2
    for i, (keep, got) in enumerate(((keep_a, got_a), (keep_b, got_b))):
        rows = slice(i * half, (i + 1) * half)
        held_ref[rows, :] = keep[:half] + got[:half].astype(jnp.float32)
        send_ref[rows, :] = (keep[half:] + got[half:].astype(jnp.float32)).astype(jnp.bfloat16)


def last_sum_kernel(keep_ref, got_ref, out_ref):
    out_ref[...] = (keep_ref[...] + got_ref[...].astype(jnp.float32)).astype(jnp.bfloat16)


def swap(block, distance):
    count = lax.axis_size("expert")
    return lax.ppermute(block, "expert", [(i, i ^ distance) for i in range(count)])


def swap_core(block):
    return lax.ppermute(block, "tensor", [(0, 1), (1, 0)])


def halves(own, far):
    half = own.shape[0] // 2
    return [jnp.concatenate([own[i : i + half], far[i : i + half]]) for i in (0, half)]


def spread(a1, b1, a2, b2):
    a3, b3 = swap(a1, Y), swap(b1, X)
    a4, b4 = swap(a2, Y), swap(b2, X)
    return [a3, a4, b3, b4, a1, a2, b1, b2]


def first_return(send_a, send_b, keep_a, keep_b):
    quarter, width = keep_a.shape[0] // 2, keep_a.shape[1]
    outs = (
        jax.ShapeDtypeStruct((quarter, width), jnp.bfloat16),
        jax.ShapeDtypeStruct((quarter, width), jnp.float32),
    )
    size = quarter * width
    got_a, got_b = swap(send_a, Y), swap(send_b, X)
    next_a, held_a = call(first_sum_kernel, outs, (keep_a, got_a), 8, size, 18 * size)
    next_b, held_b = call(first_sum_kernel, outs, (keep_b, got_b), 8, size, 18 * size)
    return next_a, next_b, held_a, held_b


def last_returns(next_a, next_b, held_a, held_b):
    outs = (
        jax.ShapeDtypeStruct(held_a.shape, jnp.bfloat16),
        jax.ShapeDtypeStruct(held_a.shape, jnp.float32),
    )
    size = held_a.size
    got_a, got_b = swap(next_a, X), swap(next_b, Y)
    next_z, held_z = call(
        second_sum_kernel, outs, (held_a, got_a, held_b, got_b), 8, size, 18 * size
    )
    got_z = swap(next_z, Z_HIGH)
    return call(last_sum_kernel, outs[0], (held_z, got_z), 8, size, 8 * size)


def local_pairs(
    batch_one,
    batch_two,
    norm_gain,
    slots_one,
    slots_two,
    gates_one,
    gates_two,
    table_old,
    table_new,
    gate_old,
    up_old,
    down_old,
):
    group = table_old.shape[0]
    tok, width = batch_one.shape
    ff = gate_old.shape[2]
    gate, up, down = gate_old[0], up_old[0], down_old[0]
    held = (
        norm_gain, batch_one, batch_two, slots_one.T, slots_two.T, gates_one.T, gates_two.T,
        table_old, table_new,
    )
    hbm = pl.BlockSpec(memory_space=pltpu.HBM)
    own = call(
        prepare_kernel,
        (jax.ShapeDtypeStruct((tok, width + PACK), jnp.bfloat16),) * 2,
        held,
        8,
        10 * tok * width,
        8 * tok * width,
        [(pltpu.SMEM if x.ndim == 1 and x.dtype == jnp.int32 else pltpu.VMEM)(x.shape, x.dtype) for x in held]
        + [pltpu.SemaphoreType.DMA((len(held),))],
        [hbm] * len(held),
    )
    half_down = jax.ShapeDtypeStruct((ff // 2, down.shape[1]), jnp.bfloat16)
    both, down_first, down_last = call(
        pack_kernel,
        (jax.ShapeDtypeStruct((gate.shape[0], 2 * ff), jnp.bfloat16), half_down, half_down),
        (gate, up, down),
        12,
        0,
        12 * gate.size,
        [pltpu.SemaphoreType.DMA((4,))],
        [hbm] * 3,
    )
    by_first = swap(down_first, Z_LOW)
    twins = (swap_core(both), swap_core(down))
    far = [swap(x, Z_HIGH) for x in own]
    far[0], twins, both_later, by_first = lax.optimization_barrier(
        (far[0], twins, both, by_first)
    )
    both_by = swap(both_later, Z_LOW)
    first_one = halves(own[0], far[0])
    second_one = swap(first_one[0], X), swap(first_one[1], Y)
    far[1], second_one = lax.optimization_barrier((far[1], second_one))
    first_two = halves(own[1], far[1])
    second_two = swap(first_two[0], X), swap(first_two[1], Y)
    pieces = [spread(*first_one, *second_one), spread(*first_two, *second_two)]

    rows = 8 * tok
    scratch = (pltpu.VMEM((rows, width + PACK), jnp.bfloat16),)

    def own_total(p):
        return call(
            functools.partial(own_kernel, 8, group),
            jax.ShapeDtypeStruct((rows, width), jnp.float32),
            (*p, both, twins[0], down, twins[1]),
            20,
            6 * rows * width * ff,
            6 * width * ff + 6 * rows * width,
            scratch,
        )

    def beside_hidden(p):
        return call(
            functools.partial(beside_kernel, 8, group),
            (
                jax.ShapeDtypeStruct((rows, ff), jnp.bfloat16),
                jax.ShapeDtypeStruct((rows, PACK), jnp.float32),
            ),
            (*p, both_by, both_twin),
            16,
            4 * rows * width * ff,
            4 * width * ff + 2 * rows * width,
            scratch,
        )

    def join(total, hid, weight):
        return call(
            join_kernel,
            (jax.ShapeDtypeStruct((2 * tok, width), jnp.bfloat16),) * 2
            + (jax.ShapeDtypeStruct((2 * tok, width), jnp.float32),) * 2,
            (hid, weight, total, *down_by),
            14,
            2 * rows * width * ff,
            2 * width * ff + 8 * rows * width,
        )

    total_one = own_total(pieces[0])
    down_last, both_by, total_one, pieces = lax.optimization_barrier(
        (down_last, both_by, total_one, pieces)
    )
    by_last = swap(down_last, Z_LOW)
    twin_first = swap_core(by_first)
    both_twin = swap_core(both_by)
    total_two = own_total(pieces[1])
    hidden_one, hidden_two = beside_hidden(pieces[0]), beside_hidden(pieces[1])
    by_last, twin_first, total_two, hidden_one, hidden_two = lax.optimization_barrier(
        (by_last, twin_first, total_two, hidden_one, hidden_two)
    )
    down_by = (by_first, by_last, twin_first, swap_core(by_last))
    back_one = first_return(*join(total_one, *hidden_one))
    back_two = first_return(*join(total_two, *hidden_two))
    return last_returns(*back_one), last_returns(*back_two)


def solution(mesh):
    in_specs = (
        P(("expert", "tensor"), None),
        P(("expert", "tensor"), None),
        P(),
        P(("expert", "tensor"), None),
        P(("expert", "tensor"), None),
        P(("expert", "tensor"), None),
        P(("expert", "tensor"), None),
        P(),
        P(),
        P("expert", "tensor", None),
        P("expert", "tensor", None),
        P("expert", None, "tensor"),
    )
    out_specs = (P(("expert", "tensor"), None), P(("expert", "tensor"), None))
    local = local_pairs if (mesh.shape["expert"], mesh.shape["tensor"]) == (16, 2) else local_any
    return jax.shard_map(local, mesh=mesh, in_specs=in_specs, out_specs=out_specs, check_vma=False)
```

```python
import functools

import jax
import jax.numpy as jnp
from jax import lax
from jax.experimental import pallas as pl
from jax.experimental.pallas import tpu as pltpu
from jax.sharding import PartitionSpec as P

EPS = 1e-05
PACK = 128
X, Y, Z_LOW, Z_HIGH = 1, 2, 4, 8


def rms_rows(tokens, norm_gain):
    values = tokens.astype(jnp.float32)
    square = jnp.mean(values * values, axis=-1, keepdims=True)
    return (values * lax.rsqrt(square + EPS) * norm_gain.astype(jnp.float32)).astype(jnp.bfloat16)


def source_slots(table_old, table_new):
    group = table_old.shape[0]
    slot_index = jnp.arange(group, dtype=jnp.int32)
    picked = jnp.where(
        table_new == jnp.roll(table_old, 1), (slot_index - 1) % group, (slot_index + 1) % group
    )
    return jnp.where(table_new == table_old, slot_index, picked).astype(jnp.int32)


def slot_weights(route_slots, route_gates, held_by):
    group = held_by.shape[0]
    hit = route_slots[:, :, None] == jnp.arange(group, dtype=jnp.int32)
    by_slot = jnp.sum(jnp.where(hit, route_gates[:, :, None], 0.0), axis=1)
    moved = held_by[:, None] == jnp.arange(group, dtype=jnp.int32)
    return jnp.sum(jnp.where(moved[None], by_slot[:, :, None], 0.0), axis=1)


def expert_part(rows, weight, gate_full, up_full, down_full):
    gate_act = jnp.dot(rows, gate_full, preferred_element_type=jnp.float32)
    up_act = jnp.dot(rows, up_full, preferred_element_type=jnp.float32)
    hidden = (jax.nn.silu(gate_act) * up_act).astype(jnp.bfloat16)
    result = jnp.dot(hidden, down_full, preferred_element_type=jnp.float32)
    return (result * weight[:, None]).astype(jnp.bfloat16)


def local_any(
    batch_one,
    batch_two,
    norm_gain,
    slots_one,
    slots_two,
    gates_one,
    gates_two,
    table_old,
    table_new,
    gate_old,
    up_old,
    down_old,
):
    group = table_old.shape[0]
    me = lax.axis_index("expert")
    gate_full = lax.all_gather(gate_old[0], "tensor", axis=0, tiled=True)
    up_full = lax.all_gather(up_old[0], "tensor", axis=0, tiled=True)
    down_full = lax.all_gather(down_old[0], "tensor", axis=1, tiled=True)
    rows_one = lax.all_gather(rms_rows(batch_one, norm_gain), "expert", axis=0, tiled=True)
    rows_two = lax.all_gather(rms_rows(batch_two, norm_gain), "expert", axis=0, tiled=True)
    own = jnp.arange(group, dtype=jnp.int32)
    weights = jnp.stack(
        [
            slot_weights(slots_one, gates_one, own),
            slot_weights(slots_two, gates_two, source_slots(table_old, table_new)),
        ]
    )
    all_weights = lax.all_gather(weights, "expert", axis=1, tiled=True)
    mine = lax.dynamic_index_in_dim(all_weights, me, axis=2, keepdims=False)
    outs = []
    for rows, weight in ((rows_one, mine[0]), (rows_two, mine[1])):
        part = expert_part(rows, weight, gate_full, up_full, down_full)
        outs.append(lax.psum_scatter(part, "expert", scatter_dimension=0, tiled=True))
    return tuple(outs)


def call(body, outs, ins, vmem_mb, flops=0, moved=0, scratch=(), specs=None):
    smem = pl.BlockSpec(memory_space=pltpu.SMEM)
    vmem = pl.BlockSpec(memory_space=pltpu.VMEM)
    return pl.pallas_call(
        body,
        out_shape=outs,
        in_specs=specs
        or [smem if x.ndim == 1 and x.dtype == jnp.int32 else vmem for x in ins],
        out_specs=jax.tree.map(lambda _: vmem, outs),
        scratch_shapes=list(scratch),
        compiler_params=pltpu.CompilerParams(vmem_limit_bytes=vmem_mb * 1024 * 1024),
        cost_estimate=pl.CostEstimate(flops=flops, bytes_accessed=moved, transcendentals=0),
    )(*ins)


def prepare_kernel(*refs):
    hbm, outs, held, sems = refs[:9], refs[9:11], refs[11:20], refs[20]
    copies = [pltpu.make_async_copy(a, b, sems.at[i]) for i, (a, b) in enumerate(zip(hbm, held))]
    for copy in copies:
        copy.start()
    for copy in copies:
        copy.wait()
    old_ref, new_ref = held[7:]
    group = old_ref.shape[0]
    sources = []
    for s in range(group):
        left, right = (s - 1) % group, (s + 1) % group
        wanted = new_ref[s]
        other = jnp.where(wanted == old_ref[left], left, right)
        sources.append(jnp.where(wanted == old_ref[s], s, other))
    gain = held[0][...].astype(jnp.float32).reshape(1, -1)
    for b in range(2):
        tokens_ref, slots_ref, gates_ref = held[1 + b], held[3 + b], held[5 + b]
        out_ref = outs[b]
        tok, width = tokens_ref.shape
        values = tokens_ref[...].astype(jnp.float32)
        square = jnp.mean(values * values, axis=-1, keepdims=True)
        out_ref[:, :width] = (values * lax.rsqrt(square + EPS) * gain).astype(jnp.bfloat16)
        slots, gates = slots_ref[...], gates_ref[...]
        if b == 1:
            holder = jnp.zeros_like(slots)
            for s in range(group):
                holder = jnp.where(slots == s, sources[s], holder)
            slots = holder
        expert = lax.broadcasted_iota(jnp.int32, (group, tok), 0)
        total = jnp.zeros((group, tok), jnp.float32)
        for k in range(slots.shape[0]):
            total += jnp.where(expert == slots[k : k + 1, :], gates[k : k + 1, :], 0.0)
        high = total.astype(jnp.bfloat16)
        rest = total - high.astype(jnp.float32)
        middle = rest.astype(jnp.bfloat16)
        low = (rest - middle.astype(jnp.float32)).astype(jnp.bfloat16)
        packed = jnp.concatenate([high, middle, low], axis=0)
        row = lax.broadcasted_iota(jnp.int32, (3 * group, PACK), 0)
        lane = lax.broadcasted_iota(jnp.int32, (3 * group, PACK), 1)
        turned = lax.dot_general(
            packed,
            (row == lane).astype(jnp.bfloat16),
            (((0,), (0,)), ((), ())),
            preferred_element_type=jnp.float32,
        )
        out_ref[:, width:] = turned.astype(jnp.bfloat16)


def pack_kernel(gate_ref, up_ref, down_ref, both_ref, first_ref, last_ref, sems):
    ff, half = gate_ref.shape[1], first_ref.shape[0]
    copies = [
        pltpu.make_async_copy(down_ref.at[:half, :], first_ref, sems.at[0]),
        pltpu.make_async_copy(down_ref.at[half:, :], last_ref, sems.at[1]),
        pltpu.make_async_copy(gate_ref, both_ref.at[:, :ff], sems.at[2]),
        pltpu.make_async_copy(up_ref, both_ref.at[:, ff:], sems.at[3]),
    ]
    for copy in copies:
        copy.start()
    for copy in copies:
        copy.wait()


def hidden_of(place, rows_ref, both_refs, begin, count):
    depth, ff = both_refs[0].shape[0], both_refs[0].shape[1] // 2
    acts = None
    for which, ref in enumerate(both_refs):
        half = place if which == 0 else 1 - place
        columns = pl.ds(pl.multiple_of(half * depth, depth), depth)
        rows = rows_ref[pl.ds(begin, count), columns]
        term = jnp.dot(rows, ref[...], preferred_element_type=jnp.float32)
        acts = term if acts is None else acts + term
    gate_act, up_act = acts[:, :ff], acts[:, ff:]
    return (gate_act / (1.0 + jnp.exp(-gate_act)) * up_act).astype(jnp.bfloat16)


def weight_of(expert, group, packed):
    lane = lax.broadcasted_iota(jnp.int32, packed.shape, 1)
    chosen = (lane & (group - 1)) == expert
    return jnp.sum(jnp.where(chosen, packed.astype(jnp.float32), 0.0), axis=1, keepdims=True)


def own_kernel(pieces, group, *refs):
    piece_refs, refs = refs[:pieces], refs[pieces:]
    both_a, both_b, down_a, down_b, total_ref, rows_ref = refs
    tok = piece_refs[0].shape[0]
    width = total_ref.shape[1]
    for i, ref in enumerate(piece_refs):
        rows_ref[i * tok : (i + 1) * tok, :] = ref[...]
    place, expert = lax.axis_index("tensor"), lax.axis_index("expert")
    block = 256

    @pl.loop(0, rows_ref.shape[0] // block)
    def _(step):
        begin = pl.multiple_of(step * block, block)
        hidden = hidden_of(place, rows_ref, (both_a, both_b), begin, block)
        weight = weight_of(expert, group, rows_ref[pl.ds(begin, block), width:])
        for which, ref in enumerate((down_a, down_b)):
            half = place if which == 0 else 1 - place
            columns = pl.ds(pl.multiple_of(half * ref.shape[1], ref.shape[1]), ref.shape[1])
            part = jnp.dot(hidden, ref[...], preferred_element_type=jnp.float32)
            total_ref[pl.ds(begin, block), columns] = part * weight


def beside_kernel(pieces, group, *refs):
    piece_refs, refs = refs[:pieces], refs[pieces:]
    both_a, both_b, hidden_ref, weight_ref, rows_ref = refs
    tok = piece_refs[0].shape[0]
    width = rows_ref.shape[1] - PACK
    for i, ref in enumerate(piece_refs):
        rows_ref[i * tok : (i + 1) * tok, :] = ref[...]
    place, expert = lax.axis_index("tensor"), lax.axis_index("expert") ^ Z_LOW
    block = 256

    @pl.loop(0, rows_ref.shape[0] // block)
    def _(step):
        begin = pl.multiple_of(step * block, block)
        hidden_ref[pl.ds(begin, block), :] = hidden_of(
            place, rows_ref, (both_a, both_b), begin, block
        )
        weight = weight_of(expert, group, rows_ref[pl.ds(begin, block), width:])
        weight_ref[pl.ds(begin, block), :] = jnp.broadcast_to(weight, (block, PACK))


def join_kernel(
    hidden_ref, weight_ref, total_ref, first_a, last_a, first_b, last_b, send_a, send_b, keep_a, keep_b
):
    place = lax.axis_index("tensor")
    count = send_a.shape[0]
    inner, width = first_a.shape
    for pair, outs in ((0, (send_a, send_b)), (1, (keep_a, keep_b))):
        rows = slice(pair * 2 * count, (pair + 1) * 2 * count)
        weight = weight_ref[rows, :1]
        for which, (first, last) in enumerate(((first_a, last_a), (first_b, last_b))):
            half = place if which == 0 else 1 - place
            columns = pl.ds(pl.multiple_of(half * width, width), width)
            part = jnp.dot(
                hidden_ref[rows, :inner], first[...], preferred_element_type=jnp.float32
            ) + jnp.dot(hidden_ref[rows, inner:], last[...], preferred_element_type=jnp.float32)
            part = part * weight + total_ref[rows, columns]
            outs[0][:, columns] = part[:count].astype(outs[0].dtype)
            outs[1][:, columns] = part[count:].astype(outs[1].dtype)


def first_sum_kernel(keep_ref, got_ref, send_ref, held_ref):
    half = held_ref.shape[0]
    held_ref[...] = keep_ref[:half] + got_ref[:half].astype(jnp.float32)
    send_ref[...] = (keep_ref[half:] + got_ref[half:].astype(jnp.float32)).astype(jnp.bfloat16)


def second_sum_kernel(keep_a, got_a, keep_b, got_b, send_ref, held_ref):
    half = keep_a.shape[0] // 2
    for i, (keep, got) in enumerate(((keep_a, got_a), (keep_b, got_b))):
        rows = slice(i * half, (i + 1) * half)
        held_ref[rows, :] = keep[:half] + got[:half].astype(jnp.float32)
        send_ref[rows, :] = (keep[half:] + got[half:].astype(jnp.float32)).astype(jnp.bfloat16)


def last_sum_kernel(keep_ref, got_ref, out_ref):
    out_ref[...] = (keep_ref[...] + got_ref[...].astype(jnp.float32)).astype(jnp.bfloat16)


def swap(block, distance):
    count = lax.axis_size("expert")
    return lax.ppermute(block, "expert", [(i, i ^ distance) for i in range(count)])


def swap_core(block):
    return lax.ppermute(block, "tensor", [(0, 1), (1, 0)])


def halves(own, far):
    half = own.shape[0] // 2
    return [jnp.concatenate([own[i : i + half], far[i : i + half]]) for i in (0, half)]


def spread(a1, b1, a2, b2):
    a3, b3 = swap(a1, Y), swap(b1, X)
    a4, b4 = swap(a2, Y), swap(b2, X)
    return [a3, a4, b3, b4, a1, a2, b1, b2]


def first_return(send_a, send_b, keep_a, keep_b):
    quarter, width = keep_a.shape[0] // 2, keep_a.shape[1]
    outs = (
        jax.ShapeDtypeStruct((quarter, width), jnp.bfloat16),
        jax.ShapeDtypeStruct((quarter, width), jnp.float32),
    )
    size = quarter * width
    got_a, got_b = swap(send_a, Y), swap(send_b, X)
    next_a, held_a = call(first_sum_kernel, outs, (keep_a, got_a), 8, size, 18 * size)
    next_b, held_b = call(first_sum_kernel, outs, (keep_b, got_b), 8, size, 18 * size)
    return next_a, next_b, held_a, held_b


def last_returns(next_a, next_b, held_a, held_b):
    outs = (
        jax.ShapeDtypeStruct(held_a.shape, jnp.bfloat16),
        jax.ShapeDtypeStruct(held_a.shape, jnp.float32),
    )
    size = held_a.size
    got_a, got_b = swap(next_a, X), swap(next_b, Y)
    next_z, held_z = call(
        second_sum_kernel, outs, (held_a, got_a, held_b, got_b), 8, size, 18 * size
    )
    got_z = swap(next_z, Z_HIGH)
    return call(last_sum_kernel, outs[0], (held_z, got_z), 8, size, 8 * size)


def local_pairs(
    batch_one,
    batch_two,
    norm_gain,
    slots_one,
    slots_two,
    gates_one,
    gates_two,
    table_old,
    table_new,
    gate_old,
    up_old,
    down_old,
):
    group = table_old.shape[0]
    tok, width = batch_one.shape
    ff = gate_old.shape[2]
    gate, up, down = gate_old[0], up_old[0], down_old[0]
    held = (
        norm_gain, batch_one, batch_two, slots_one.T, slots_two.T, gates_one.T, gates_two.T,
        table_old, table_new,
    )
    hbm = pl.BlockSpec(memory_space=pltpu.HBM)
    own = call(
        prepare_kernel,
        (jax.ShapeDtypeStruct((tok, width + PACK), jnp.bfloat16),) * 2,
        held,
        8,
        10 * tok * width,
        8 * tok * width,
        [(pltpu.SMEM if x.ndim == 1 and x.dtype == jnp.int32 else pltpu.VMEM)(x.shape, x.dtype) for x in held]
        + [pltpu.SemaphoreType.DMA((len(held),))],
        [hbm] * len(held),
    )
    half_down = jax.ShapeDtypeStruct((ff // 2, down.shape[1]), jnp.bfloat16)
    both, down_first, down_last = call(
        pack_kernel,
        (jax.ShapeDtypeStruct((gate.shape[0], 2 * ff), jnp.bfloat16), half_down, half_down),
        (gate, up, down),
        59,
        0,
        12 * gate.size,
        [pltpu.SemaphoreType.DMA((4,))],
        [hbm] * 3,
    )
    by_first = swap(down_first, Z_LOW)
    twins = (swap_core(both), swap_core(down))
    far = [swap(x, Z_HIGH) for x in own]
    far[0], twins, both_later = lax.optimization_barrier((far[0], twins, both))
    both_by = swap(both_later, Z_LOW)
    first_one = halves(own[0], far[0])
    second_one = swap(first_one[0], X), swap(first_one[1], Y)
    far[1], second_one, by_first = lax.optimization_barrier((far[1], second_one, by_first))
    first_two = halves(own[1], far[1])
    second_two = swap(first_two[0], X), swap(first_two[1], Y)
    pieces = [spread(*first_one, *second_one), spread(*first_two, *second_two)]

    rows = 8 * tok
    scratch = (pltpu.VMEM((rows, width + PACK), jnp.bfloat16),)

    def own_total(p):
        return call(
            functools.partial(own_kernel, 8, group),
            jax.ShapeDtypeStruct((rows, width), jnp.float32),
            (*p, both, twins[0], down, twins[1]),
            20,
            0,
            6 * width * ff + 6 * rows * width,
            scratch,
        )

    def beside_hidden(p):
        return call(
            functools.partial(beside_kernel, 8, group),
            (
                jax.ShapeDtypeStruct((rows, ff), jnp.bfloat16),
                jax.ShapeDtypeStruct((rows, PACK), jnp.float32),
            ),
            (*p, both_by, both_twin),
            16,
            4 * rows * width * ff,
            4 * width * ff + 2 * rows * width,
            scratch,
        )

    def join(total, hid, weight):
        return call(
            join_kernel,
            (jax.ShapeDtypeStruct((2 * tok, width), jnp.bfloat16),) * 2
            + (jax.ShapeDtypeStruct((2 * tok, width), jnp.float32),) * 2,
            (hid, weight, total, *down_by),
            14,
            2 * rows * width * ff,
            2 * width * ff + 8 * rows * width,
        )

    total_one = own_total(pieces[0])
    down_last, far[1] = lax.optimization_barrier((down_last, far[1]))
    by_last = swap(down_last, Z_LOW)
    both_by, total_one, pieces = lax.optimization_barrier((both_by, total_one, pieces))
    twin_first = swap_core(by_first)
    both_twin = swap_core(both_by)
    total_two = own_total(pieces[1])
    hidden_one, hidden_two = beside_hidden(pieces[0]), beside_hidden(pieces[1])
    by_last, twin_first, total_two, hidden_one, hidden_two = lax.optimization_barrier(
        (by_last, twin_first, total_two, hidden_one, hidden_two)
    )
    down_by = (by_first, by_last, twin_first, swap_core(by_last))
    back_one = first_return(*join(total_one, *hidden_one))
    back_two = first_return(*join(total_two, *hidden_two))
    return last_returns(*back_one), last_returns(*back_two)


def solution(mesh):
    in_specs = (
        P(("expert", "tensor"), None),
        P(("expert", "tensor"), None),
        P(),
        P(("expert", "tensor"), None),
        P(("expert", "tensor"), None),
        P(("expert", "tensor"), None),
        P(("expert", "tensor"), None),
        P(),
        P(),
        P("expert", "tensor", None),
        P("expert", "tensor", None),
        P("expert", None, "tensor"),
    )
    out_specs = (P(("expert", "tensor"), None), P(("expert", "tensor"), None))
    local = local_pairs if (mesh.shape["expert"], mesh.shape["tensor"]) == (16, 2) else local_any
    return jax.shard_map(local, mesh=mesh, in_specs=in_specs, out_specs=out_specs, check_vma=False)
```

```python
import functools

import jax
import jax.numpy as jnp
from jax import lax
from jax.experimental import pallas as pl
from jax.experimental.pallas import tpu as pltpu
from jax.sharding import PartitionSpec as P

EPS = 1e-05
PACK = 128
X, Y, Z_LOW, Z_HIGH = 1, 2, 4, 8


def rms_rows(tokens, norm_gain):
    values = tokens.astype(jnp.float32)
    square = jnp.mean(values * values, axis=-1, keepdims=True)
    return (values * lax.rsqrt(square + EPS) * norm_gain.astype(jnp.float32)).astype(jnp.bfloat16)


def source_slots(table_old, table_new):
    group = table_old.shape[0]
    slot_index = jnp.arange(group, dtype=jnp.int32)
    picked = jnp.where(
        table_new == jnp.roll(table_old, 1), (slot_index - 1) % group, (slot_index + 1) % group
    )
    return jnp.where(table_new == table_old, slot_index, picked).astype(jnp.int32)


def slot_weights(route_slots, route_gates, held_by):
    group = held_by.shape[0]
    hit = route_slots[:, :, None] == jnp.arange(group, dtype=jnp.int32)
    by_slot = jnp.sum(jnp.where(hit, route_gates[:, :, None], 0.0), axis=1)
    moved = held_by[:, None] == jnp.arange(group, dtype=jnp.int32)
    return jnp.sum(jnp.where(moved[None], by_slot[:, :, None], 0.0), axis=1)


def expert_part(rows, weight, gate_full, up_full, down_full):
    gate_act = jnp.dot(rows, gate_full, preferred_element_type=jnp.float32)
    up_act = jnp.dot(rows, up_full, preferred_element_type=jnp.float32)
    hidden = (jax.nn.silu(gate_act) * up_act).astype(jnp.bfloat16)
    result = jnp.dot(hidden, down_full, preferred_element_type=jnp.float32)
    return (result * weight[:, None]).astype(jnp.bfloat16)


def local_any(
    batch_one,
    batch_two,
    norm_gain,
    slots_one,
    slots_two,
    gates_one,
    gates_two,
    table_old,
    table_new,
    gate_old,
    up_old,
    down_old,
):
    group = table_old.shape[0]
    me = lax.axis_index("expert")
    gate_full = lax.all_gather(gate_old[0], "tensor", axis=0, tiled=True)
    up_full = lax.all_gather(up_old[0], "tensor", axis=0, tiled=True)
    down_full = lax.all_gather(down_old[0], "tensor", axis=1, tiled=True)
    rows_one = lax.all_gather(rms_rows(batch_one, norm_gain), "expert", axis=0, tiled=True)
    rows_two = lax.all_gather(rms_rows(batch_two, norm_gain), "expert", axis=0, tiled=True)
    own = jnp.arange(group, dtype=jnp.int32)
    weights = jnp.stack(
        [
            slot_weights(slots_one, gates_one, own),
            slot_weights(slots_two, gates_two, source_slots(table_old, table_new)),
        ]
    )
    all_weights = lax.all_gather(weights, "expert", axis=1, tiled=True)
    mine = lax.dynamic_index_in_dim(all_weights, me, axis=2, keepdims=False)
    outs = []
    for rows, weight in ((rows_one, mine[0]), (rows_two, mine[1])):
        part = expert_part(rows, weight, gate_full, up_full, down_full)
        outs.append(lax.psum_scatter(part, "expert", scatter_dimension=0, tiled=True))
    return tuple(outs)


def call(body, outs, ins, vmem_mb, flops=0, moved=0, scratch=(), specs=None):
    smem = pl.BlockSpec(memory_space=pltpu.SMEM)
    vmem = pl.BlockSpec(memory_space=pltpu.VMEM)
    return pl.pallas_call(
        body,
        out_shape=outs,
        in_specs=specs
        or [smem if x.ndim == 1 and x.dtype == jnp.int32 else vmem for x in ins],
        out_specs=jax.tree.map(lambda _: vmem, outs),
        scratch_shapes=list(scratch),
        compiler_params=pltpu.CompilerParams(vmem_limit_bytes=vmem_mb * 1024 * 1024),
        cost_estimate=pl.CostEstimate(flops=flops, bytes_accessed=moved, transcendentals=0),
    )(*ins)


def prepare_kernel(*refs):
    hbm, outs, held, sems = refs[:9], refs[9:11], refs[11:20], refs[20]
    copies = [pltpu.make_async_copy(a, b, sems.at[i]) for i, (a, b) in enumerate(zip(hbm, held))]
    for copy in copies:
        copy.start()
    for copy in copies:
        copy.wait()
    old_ref, new_ref = held[7:]
    group = old_ref.shape[0]
    sources = []
    for s in range(group):
        left, right = (s - 1) % group, (s + 1) % group
        wanted = new_ref[s]
        other = jnp.where(wanted == old_ref[left], left, right)
        sources.append(jnp.where(wanted == old_ref[s], s, other))
    gain = held[0][...].astype(jnp.float32).reshape(1, -1)
    for b in range(2):
        tokens_ref, slots_ref, gates_ref = held[1 + b], held[3 + b], held[5 + b]
        out_ref = outs[b]
        tok, width = tokens_ref.shape
        values = tokens_ref[...].astype(jnp.float32)
        square = jnp.mean(values * values, axis=-1, keepdims=True)
        out_ref[:, :width] = (values * lax.rsqrt(square + EPS) * gain).astype(jnp.bfloat16)
        slots, gates = slots_ref[...], gates_ref[...]
        if b == 1:
            holder = jnp.zeros_like(slots)
            for s in range(group):
                holder = jnp.where(slots == s, sources[s], holder)
            slots = holder
        expert = lax.broadcasted_iota(jnp.int32, (group, tok), 0)
        total = jnp.zeros((group, tok), jnp.float32)
        for k in range(slots.shape[0]):
            total += jnp.where(expert == slots[k : k + 1, :], gates[k : k + 1, :], 0.0)
        high = total.astype(jnp.bfloat16)
        rest = total - high.astype(jnp.float32)
        middle = rest.astype(jnp.bfloat16)
        low = (rest - middle.astype(jnp.float32)).astype(jnp.bfloat16)
        packed = jnp.concatenate([high, middle, low], axis=0)
        row = lax.broadcasted_iota(jnp.int32, (3 * group, PACK), 0)
        lane = lax.broadcasted_iota(jnp.int32, (3 * group, PACK), 1)
        turned = lax.dot_general(
            packed,
            (row == lane).astype(jnp.bfloat16),
            (((0,), (0,)), ((), ())),
            preferred_element_type=jnp.float32,
        )
        out_ref[:, width:] = turned.astype(jnp.bfloat16)


def pack_kernel(gate_ref, up_ref, down_ref, both_ref, first_ref, last_ref, sems):
    ff, half = gate_ref.shape[1], first_ref.shape[0]
    copies = [
        pltpu.make_async_copy(down_ref.at[:half, :], first_ref, sems.at[0]),
        pltpu.make_async_copy(down_ref.at[half:, :], last_ref, sems.at[1]),
        pltpu.make_async_copy(gate_ref, both_ref.at[:, :ff], sems.at[2]),
        pltpu.make_async_copy(up_ref, both_ref.at[:, ff:], sems.at[3]),
    ]
    for copy in copies:
        copy.start()
    for copy in copies:
        copy.wait()


def hidden_of(place, rows_ref, both_refs, begin, count):
    depth, ff = both_refs[0].shape[0], both_refs[0].shape[1] // 2
    acts = None
    for which, ref in enumerate(both_refs):
        half = place if which == 0 else 1 - place
        columns = pl.ds(pl.multiple_of(half * depth, depth), depth)
        rows = rows_ref[pl.ds(begin, count), columns]
        term = jnp.dot(rows, ref[...], preferred_element_type=jnp.float32)
        acts = term if acts is None else acts + term
    gate_act, up_act = acts[:, :ff], acts[:, ff:]
    return (gate_act / (1.0 + jnp.exp(-gate_act)) * up_act).astype(jnp.bfloat16)


def weight_of(expert, group, packed):
    lane = lax.broadcasted_iota(jnp.int32, packed.shape, 1)
    chosen = (lane & (group - 1)) == expert
    return jnp.sum(jnp.where(chosen, packed.astype(jnp.float32), 0.0), axis=1, keepdims=True)


def own_kernel(pieces, group, *refs):
    piece_refs, refs = refs[:pieces], refs[pieces:]
    both_a, both_b, down_a, down_b, total_ref, rows_ref = refs
    tok = piece_refs[0].shape[0]
    width = total_ref.shape[1]
    for i, ref in enumerate(piece_refs):
        rows_ref[i * tok : (i + 1) * tok, :] = ref[...]
    place, expert = lax.axis_index("tensor"), lax.axis_index("expert")
    block = 256

    @pl.loop(0, rows_ref.shape[0] // block)
    def _(step):
        begin = pl.multiple_of(step * block, block)
        hidden = hidden_of(place, rows_ref, (both_a, both_b), begin, block)
        weight = weight_of(expert, group, rows_ref[pl.ds(begin, block), width:])
        for which, ref in enumerate((down_a, down_b)):
            half = place if which == 0 else 1 - place
            columns = pl.ds(pl.multiple_of(half * ref.shape[1], ref.shape[1]), ref.shape[1])
            part = jnp.dot(hidden, ref[...], preferred_element_type=jnp.float32)
            total_ref[pl.ds(begin, block), columns] = part * weight


def beside_kernel(pieces, group, *refs):
    piece_refs, refs = refs[:pieces], refs[pieces:]
    both_a, both_b, hidden_ref, weight_ref, rows_ref = refs
    tok = piece_refs[0].shape[0]
    width = rows_ref.shape[1] - PACK
    for i, ref in enumerate(piece_refs):
        rows_ref[i * tok : (i + 1) * tok, :] = ref[...]
    place, expert = lax.axis_index("tensor"), lax.axis_index("expert") ^ Z_LOW
    block = 256

    @pl.loop(0, rows_ref.shape[0] // block)
    def _(step):
        begin = pl.multiple_of(step * block, block)
        hidden_ref[pl.ds(begin, block), :] = hidden_of(
            place, rows_ref, (both_a, both_b), begin, block
        )
        weight = weight_of(expert, group, rows_ref[pl.ds(begin, block), width:])
        weight_ref[pl.ds(begin, block), :] = jnp.broadcast_to(weight, (block, PACK))


def join_kernel(hidden_ref, weight_ref, total_ref, first_a, last_a, first_b, last_b, *outs):
    place = lax.axis_index("tensor")
    inner, width = first_a.shape
    per, count = len(outs) // 2, outs[0].shape[0]
    for part in range(2):
        rows = slice(part * per * count, (part + 1) * per * count)
        weight = weight_ref[rows, :1]
        for which, (first, last) in enumerate(((first_a, last_a), (first_b, last_b))):
            half = place if which == 0 else 1 - place
            columns = pl.ds(pl.multiple_of(half * width, width), width)
            result = jnp.dot(
                hidden_ref[rows, :inner], first[...], preferred_element_type=jnp.float32
            ) + jnp.dot(hidden_ref[rows, inner:], last[...], preferred_element_type=jnp.float32)
            result = result * weight + total_ref[rows, columns]
            for i, out in enumerate(outs[per * part : per * (part + 1)]):
                out[:, columns] = result[i * count : (i + 1) * count].astype(out.dtype)


def part_sum_kernel(keep_ref, got_ref, send_ref):
    send_ref[...] = (keep_ref[...] + got_ref[...].astype(jnp.float32)).astype(jnp.bfloat16)


def three_sum_kernel(keep_a, got_a, far_a, keep_b, got_b, far_b, send_ref, held_ref):
    half = keep_a.shape[0] // 2
    for i, (keep, got, far) in enumerate(((keep_a, got_a, far_a), (keep_b, got_b, far_b))):
        rows = slice(i * half, (i + 1) * half)
        total = keep[...] + got[...].astype(jnp.float32) + far[...].astype(jnp.float32)
        held_ref[rows, :] = total[:half]
        send_ref[rows, :] = total[half:].astype(jnp.bfloat16)


def first_sum_kernel(keep_ref, got_ref, send_ref, held_ref):
    half = held_ref.shape[0]
    held_ref[...] = keep_ref[:half] + got_ref[:half].astype(jnp.float32)
    send_ref[...] = (keep_ref[half:] + got_ref[half:].astype(jnp.float32)).astype(jnp.bfloat16)


def second_sum_kernel(keep_a, got_a, keep_b, got_b, send_ref, held_ref):
    half = keep_a.shape[0] // 2
    for i, (keep, got) in enumerate(((keep_a, got_a), (keep_b, got_b))):
        rows = slice(i * half, (i + 1) * half)
        held_ref[rows, :] = keep[:half] + got[:half].astype(jnp.float32)
        send_ref[rows, :] = (keep[half:] + got[half:].astype(jnp.float32)).astype(jnp.bfloat16)


def last_sum_kernel(keep_ref, got_ref, out_ref):
    out_ref[...] = (keep_ref[...] + got_ref[...].astype(jnp.float32)).astype(jnp.bfloat16)


def swap(block, distance):
    count = lax.axis_size("expert")
    return lax.ppermute(block, "expert", [(i, i ^ distance) for i in range(count)])


def swap_core(block):
    return lax.ppermute(block, "tensor", [(0, 1), (1, 0)])


def halves(own, far):
    half = own.shape[0] // 2
    return [jnp.concatenate([own[i : i + half], far[i : i + half]]) for i in (0, half)]


def spread(a1, b1, a2, b2):
    a3, b3 = swap(a1, Y), swap(b1, X)
    a4, b4 = swap(a2, Y), swap(b2, X)
    return a1, b1, a2, b2, a3, b3, a4, b4


def send_back(one, two):
    send_a, send_b, keep_a, keep_b = one
    a4, b4, a3, b3, a2, b2, a1, b1 = two
    half = jax.ShapeDtypeStruct(a1.shape, jnp.bfloat16)
    held = jax.ShapeDtypeStruct(a1.shape, jnp.float32)
    size = a1.size
    got_a, got_b = swap(send_a, Y), swap(send_b, X)
    got_a4, got_b4 = swap(a4, Y), swap(b4, X)
    next_a, held_a = call(first_sum_kernel, (half, held), (keep_a, got_a), 8, size, 18 * size)
    next_b, held_b = call(first_sum_kernel, (half, held), (keep_b, got_b), 8, size, 18 * size)
    next_a, next_b, a2, b2, a3, b3 = lax.optimization_barrier((next_a, next_b, a2, b2, a3, b3))
    far_a, far_b = swap(next_a, X), swap(next_b, Y)
    next_z, held_z = call(
        second_sum_kernel, (half, held), (held_a, far_a, held_b, far_b), 8, size, 18 * size
    )
    next_a2 = call(part_sum_kernel, half, (a2, got_a4), 4, size, 8 * size)
    next_b2 = call(part_sum_kernel, half, (b2, got_b4), 4, size, 8 * size)
    got_a3, got_b3 = swap(a3, Y), swap(b3, X)
    far_a2, far_b2 = swap(next_a2, X), swap(next_b2, Y)
    got_z = swap(next_z, Z_HIGH)
    got_z, far_a2, far_b2 = lax.optimization_barrier((got_z, far_a2, far_b2))
    next_z2, held_z2 = call(
        three_sum_kernel, (half, held), (a1, got_a3, far_a2, b1, got_b3, far_b2), 8, size, 22 * size
    )
    got_z2 = swap(next_z2, Z_HIGH)
    return (
        call(last_sum_kernel, half, (held_z, got_z), 4, size, 8 * size),
        call(last_sum_kernel, half, (held_z2, got_z2), 4, size, 8 * size),
    )


def local_pairs(
    batch_one,
    batch_two,
    norm_gain,
    slots_one,
    slots_two,
    gates_one,
    gates_two,
    table_old,
    table_new,
    gate_old,
    up_old,
    down_old,
):
    group = table_old.shape[0]
    tok, width = batch_one.shape
    ff = gate_old.shape[2]
    gate, up, down = gate_old[0], up_old[0], down_old[0]
    held = (
        norm_gain, batch_one, batch_two, slots_one.T, slots_two.T, gates_one.T, gates_two.T,
        table_old, table_new,
    )
    hbm = pl.BlockSpec(memory_space=pltpu.HBM)
    own = call(
        prepare_kernel,
        (jax.ShapeDtypeStruct((tok, width + PACK), jnp.bfloat16),) * 2,
        held,
        8,
        10 * tok * width,
        8 * tok * width,
        [(pltpu.SMEM if x.ndim == 1 and x.dtype == jnp.int32 else pltpu.VMEM)(x.shape, x.dtype) for x in held]
        + [pltpu.SemaphoreType.DMA((len(held),))],
        [hbm] * len(held),
    )
    half_down = jax.ShapeDtypeStruct((ff // 2, down.shape[1]), jnp.bfloat16)
    both, down_first, down_last = call(
        pack_kernel,
        (jax.ShapeDtypeStruct((gate.shape[0], 2 * ff), jnp.bfloat16), half_down, half_down),
        (gate, up, down),
        59,
        0,
        12 * gate.size,
        [pltpu.SemaphoreType.DMA((4,))],
        [hbm] * 3,
    )
    by_first = swap(down_first, Z_LOW)
    twins = (swap_core(both), swap_core(down))
    far = [swap(x, Z_HIGH) for x in own]
    far[0], twins, both_later = lax.optimization_barrier((far[0], twins, both))
    both_by = swap(both_later, Z_LOW)
    first_one = halves(own[0], far[0])
    second_one = swap(first_one[0], X), swap(first_one[1], Y)
    far[1], second_one, by_first = lax.optimization_barrier((far[1], second_one, by_first))
    first_two = halves(own[1], far[1])
    second_two = swap(first_two[0], X), swap(first_two[1], Y)
    a1, b1, a2, b2, a3, b3, a4, b4 = spread(*first_one, *second_one)
    pieces_one = [a3, a4, b3, b4, a1, a2, b1, b2]
    a1, b1, a2, b2, a3, b3, a4, b4 = spread(*first_two, *second_two)
    pieces = [pieces_one, [a4, b4, a3, b3, a2, b2, a1, b1]]

    rows = 8 * tok
    scratch = (pltpu.VMEM((rows, width + PACK), jnp.bfloat16),)

    def own_total(p):
        return call(
            functools.partial(own_kernel, 8, group),
            jax.ShapeDtypeStruct((rows, width), jnp.float32),
            (*p, both, twins[0], down, twins[1]),
            20,
            0,
            6 * width * ff + 6 * rows * width,
            scratch,
        )

    def beside_hidden(p):
        return call(
            functools.partial(beside_kernel, 8, group),
            (
                jax.ShapeDtypeStruct((rows, ff), jnp.bfloat16),
                jax.ShapeDtypeStruct((rows, PACK), jnp.float32),
            ),
            (*p, both_by, both_twin),
            16,
            4 * rows * width * ff,
            4 * width * ff + 2 * rows * width,
            scratch,
        )

    def join(total, hid, weight, per):
        count = rows // 2 // per
        return call(
            join_kernel,
            (jax.ShapeDtypeStruct((count, width), jnp.bfloat16),) * per
            + (jax.ShapeDtypeStruct((count, width), jnp.float32),) * per,
            (hid, weight, total, *down_by),
            14,
            2 * rows * width * ff,
            2 * width * ff + 8 * rows * width,
        )

    total_one = own_total(pieces[0])
    down_last, far[1] = lax.optimization_barrier((down_last, far[1]))
    by_last = swap(down_last, Z_LOW)
    both_by, total_one, pieces = lax.optimization_barrier((both_by, total_one, pieces))
    twin_first = swap_core(by_first)
    both_twin = swap_core(both_by)
    total_two = own_total(pieces[1])
    hidden_one, hidden_two = beside_hidden(pieces[0]), beside_hidden(pieces[1])
    by_last, twin_first, total_two, hidden_one, hidden_two = lax.optimization_barrier(
        (by_last, twin_first, total_two, hidden_one, hidden_two)
    )
    down_by = (by_first, by_last, twin_first, swap_core(by_last))
    return send_back(join(total_one, *hidden_one, 2), join(total_two, *hidden_two, 4))


def solution(mesh):
    in_specs = (
        P(("expert", "tensor"), None),
        P(("expert", "tensor"), None),
        P(),
        P(("expert", "tensor"), None),
        P(("expert", "tensor"), None),
        P(("expert", "tensor"), None),
        P(("expert", "tensor"), None),
        P(),
        P(),
        P("expert", "tensor", None),
        P("expert", "tensor", None),
        P("expert", None, "tensor"),
    )
    out_specs = (P(("expert", "tensor"), None), P(("expert", "tensor"), None))
    local = local_pairs if (mesh.shape["expert"], mesh.shape["tensor"]) == (16, 2) else local_any
    return jax.shard_map(local, mesh=mesh, in_specs=in_specs, out_specs=out_specs, check_vma=False)
```

```python
import functools

import jax
import jax.numpy as jnp
from jax import lax
from jax.experimental import pallas as pl
from jax.experimental.pallas import tpu as pltpu
from jax.sharding import PartitionSpec as P

EPS = 1e-05
PACK = 128
X, Y, Z_LOW, Z_HIGH = 1, 2, 4, 8


def rms_rows(tokens, norm_gain):
    values = tokens.astype(jnp.float32)
    square = jnp.mean(values * values, axis=-1, keepdims=True)
    return (values * lax.rsqrt(square + EPS) * norm_gain.astype(jnp.float32)).astype(jnp.bfloat16)


def source_slots(table_old, table_new):
    group = table_old.shape[0]
    slot_index = jnp.arange(group, dtype=jnp.int32)
    picked = jnp.where(
        table_new == jnp.roll(table_old, 1), (slot_index - 1) % group, (slot_index + 1) % group
    )
    return jnp.where(table_new == table_old, slot_index, picked).astype(jnp.int32)


def slot_weights(route_slots, route_gates, held_by):
    group = held_by.shape[0]
    hit = route_slots[:, :, None] == jnp.arange(group, dtype=jnp.int32)
    by_slot = jnp.sum(jnp.where(hit, route_gates[:, :, None], 0.0), axis=1)
    moved = held_by[:, None] == jnp.arange(group, dtype=jnp.int32)
    return jnp.sum(jnp.where(moved[None], by_slot[:, :, None], 0.0), axis=1)


def expert_part(rows, weight, gate_full, up_full, down_full):
    gate_act = jnp.dot(rows, gate_full, preferred_element_type=jnp.float32)
    up_act = jnp.dot(rows, up_full, preferred_element_type=jnp.float32)
    hidden = (jax.nn.silu(gate_act) * up_act).astype(jnp.bfloat16)
    result = jnp.dot(hidden, down_full, preferred_element_type=jnp.float32)
    return (result * weight[:, None]).astype(jnp.bfloat16)


def local_any(
    batch_one,
    batch_two,
    norm_gain,
    slots_one,
    slots_two,
    gates_one,
    gates_two,
    table_old,
    table_new,
    gate_old,
    up_old,
    down_old,
):
    group = table_old.shape[0]
    me = lax.axis_index("expert")
    gate_full = lax.all_gather(gate_old[0], "tensor", axis=0, tiled=True)
    up_full = lax.all_gather(up_old[0], "tensor", axis=0, tiled=True)
    down_full = lax.all_gather(down_old[0], "tensor", axis=1, tiled=True)
    rows_one = lax.all_gather(rms_rows(batch_one, norm_gain), "expert", axis=0, tiled=True)
    rows_two = lax.all_gather(rms_rows(batch_two, norm_gain), "expert", axis=0, tiled=True)
    own = jnp.arange(group, dtype=jnp.int32)
    weights = jnp.stack(
        [
            slot_weights(slots_one, gates_one, own),
            slot_weights(slots_two, gates_two, source_slots(table_old, table_new)),
        ]
    )
    all_weights = lax.all_gather(weights, "expert", axis=1, tiled=True)
    mine = lax.dynamic_index_in_dim(all_weights, me, axis=2, keepdims=False)
    outs = []
    for rows, weight in ((rows_one, mine[0]), (rows_two, mine[1])):
        part = expert_part(rows, weight, gate_full, up_full, down_full)
        outs.append(lax.psum_scatter(part, "expert", scatter_dimension=0, tiled=True))
    return tuple(outs)


def call(body, outs, ins, vmem_mb, flops=0, moved=0, scratch=(), specs=None):
    smem = pl.BlockSpec(memory_space=pltpu.SMEM)
    vmem = pl.BlockSpec(memory_space=pltpu.VMEM)
    return pl.pallas_call(
        body,
        out_shape=outs,
        in_specs=specs
        or [smem if x.ndim == 1 and x.dtype == jnp.int32 else vmem for x in ins],
        out_specs=jax.tree.map(lambda _: vmem, outs),
        scratch_shapes=list(scratch),
        compiler_params=pltpu.CompilerParams(vmem_limit_bytes=vmem_mb * 1024 * 1024),
        cost_estimate=pl.CostEstimate(flops=flops, bytes_accessed=moved, transcendentals=0),
    )(*ins)


def prepare_kernel(*refs):
    hbm, outs, held, sems = refs[:9], refs[9:11], refs[11:20], refs[20]
    copies = [pltpu.make_async_copy(a, b, sems.at[i]) for i, (a, b) in enumerate(zip(hbm, held))]
    for copy in copies:
        copy.start()
    for copy in copies:
        copy.wait()
    old_ref, new_ref = held[7:]
    group = old_ref.shape[0]
    sources = []
    for s in range(group):
        left, right = (s - 1) % group, (s + 1) % group
        wanted = new_ref[s]
        other = jnp.where(wanted == old_ref[left], left, right)
        sources.append(jnp.where(wanted == old_ref[s], s, other))
    gain = held[0][...].astype(jnp.float32).reshape(1, -1)
    for b in range(2):
        tokens_ref, slots_ref, gates_ref = held[1 + b], held[3 + b], held[5 + b]
        out_ref = outs[b]
        tok, width = tokens_ref.shape
        values = tokens_ref[...].astype(jnp.float32)
        square = jnp.mean(values * values, axis=-1, keepdims=True)
        out_ref[:, :width] = (values * lax.rsqrt(square + EPS) * gain).astype(jnp.bfloat16)
        slots, gates = slots_ref[...], gates_ref[...]
        if b == 1:
            holder = jnp.zeros_like(slots)
            for s in range(group):
                holder = jnp.where(slots == s, sources[s], holder)
            slots = holder
        expert = lax.broadcasted_iota(jnp.int32, (group, tok), 0)
        total = jnp.zeros((group, tok), jnp.float32)
        for k in range(slots.shape[0]):
            total += jnp.where(expert == slots[k : k + 1, :], gates[k : k + 1, :], 0.0)
        high = total.astype(jnp.bfloat16)
        rest = total - high.astype(jnp.float32)
        middle = rest.astype(jnp.bfloat16)
        low = (rest - middle.astype(jnp.float32)).astype(jnp.bfloat16)
        packed = jnp.concatenate([high, middle, low], axis=0)
        row = lax.broadcasted_iota(jnp.int32, (3 * group, PACK), 0)
        lane = lax.broadcasted_iota(jnp.int32, (3 * group, PACK), 1)
        turned = lax.dot_general(
            packed,
            (row == lane).astype(jnp.bfloat16),
            (((0,), (0,)), ((), ())),
            preferred_element_type=jnp.float32,
        )
        out_ref[:, width:] = turned.astype(jnp.bfloat16)


def halve_kernel(whole_ref, first_ref, last_ref, sems):
    half = first_ref.shape[0]
    copies = [
        pltpu.make_async_copy(whole_ref.at[:half, :], first_ref, sems.at[0]),
        pltpu.make_async_copy(whole_ref.at[half:, :], last_ref, sems.at[1]),
    ]
    for copy in copies:
        copy.start()
    for copy in copies:
        copy.wait()


def pack_kernel(gate_ref, up_ref, both_ref, sems):
    ff = gate_ref.shape[1]
    copies = [
        pltpu.make_async_copy(gate_ref, both_ref.at[:, :ff], sems.at[0]),
        pltpu.make_async_copy(up_ref, both_ref.at[:, ff:], sems.at[1]),
    ]
    for copy in copies:
        copy.start()
    for copy in copies:
        copy.wait()


def hidden_of(place, rows_ref, both_refs, begin, count):
    depth, ff = both_refs[0].shape[0], both_refs[0].shape[1] // 2
    acts = None
    for which, ref in enumerate(both_refs):
        half = place if which == 0 else 1 - place
        columns = pl.ds(pl.multiple_of(half * depth, depth), depth)
        rows = rows_ref[pl.ds(begin, count), columns]
        term = jnp.dot(rows, ref[...], preferred_element_type=jnp.float32)
        acts = term if acts is None else acts + term
    gate_act, up_act = acts[:, :ff], acts[:, ff:]
    return (gate_act / (1.0 + jnp.exp(-gate_act)) * up_act).astype(jnp.bfloat16)


def weight_of(expert, group, packed):
    lane = lax.broadcasted_iota(jnp.int32, packed.shape, 1)
    chosen = (lane & (group - 1)) == expert
    return jnp.sum(jnp.where(chosen, packed.astype(jnp.float32), 0.0), axis=1, keepdims=True)


def own_kernel(pieces, group, *refs):
    piece_refs, refs = refs[:pieces], refs[pieces:]
    both_a, both_b, down_a, down_b, total_ref, rows_ref = refs
    tok = piece_refs[0].shape[0]
    width = total_ref.shape[1]
    for i, ref in enumerate(piece_refs):
        rows_ref[i * tok : (i + 1) * tok, :] = ref[...]
    place, expert = lax.axis_index("tensor"), lax.axis_index("expert")
    block = 256

    @pl.loop(0, rows_ref.shape[0] // block)
    def _(step):
        begin = pl.multiple_of(step * block, block)
        hidden = hidden_of(place, rows_ref, (both_a, both_b), begin, block)
        weight = weight_of(expert, group, rows_ref[pl.ds(begin, block), width:])
        for which, ref in enumerate((down_a, down_b)):
            half = place if which == 0 else 1 - place
            columns = pl.ds(pl.multiple_of(half * ref.shape[1], ref.shape[1]), ref.shape[1])
            part = jnp.dot(hidden, ref[...], preferred_element_type=jnp.float32)
            total_ref[pl.ds(begin, block), columns] = part * weight


def beside_kernel(pieces, group, *refs):
    piece_refs, refs = refs[:pieces], refs[pieces:]
    both_a, both_b, hidden_ref, weight_ref, rows_ref = refs
    tok = piece_refs[0].shape[0]
    width = rows_ref.shape[1] - PACK
    for i, ref in enumerate(piece_refs):
        rows_ref[i * tok : (i + 1) * tok, :] = ref[...]
    place, expert = lax.axis_index("tensor"), lax.axis_index("expert") ^ Z_LOW
    block = 256

    @pl.loop(0, rows_ref.shape[0] // block)
    def _(step):
        begin = pl.multiple_of(step * block, block)
        hidden_ref[pl.ds(begin, block), :] = hidden_of(
            place, rows_ref, (both_a, both_b), begin, block
        )
        weight = weight_of(expert, group, rows_ref[pl.ds(begin, block), width:])
        weight_ref[pl.ds(begin, block), :] = jnp.broadcast_to(weight, (block, PACK))


def join_kernel(hidden_ref, weight_ref, total_ref, first_a, last_a, first_b, last_b, *outs):
    place = lax.axis_index("tensor")
    inner, width = first_a.shape
    per, count = len(outs) // 2, outs[0].shape[0]
    for part in range(2):
        rows = slice(part * per * count, (part + 1) * per * count)
        weight = weight_ref[rows, :1]
        for which, (first, last) in enumerate(((first_a, last_a), (first_b, last_b))):
            half = place if which == 0 else 1 - place
            columns = pl.ds(pl.multiple_of(half * width, width), width)
            result = jnp.dot(
                hidden_ref[rows, :inner], first[...], preferred_element_type=jnp.float32
            ) + jnp.dot(hidden_ref[rows, inner:], last[...], preferred_element_type=jnp.float32)
            result = result * weight + total_ref[rows, columns]
            for i, out in enumerate(outs[per * part : per * (part + 1)]):
                out[:, columns] = result[i * count : (i + 1) * count].astype(out.dtype)


def part_sum_kernel(keep_ref, got_ref, send_ref):
    send_ref[...] = (keep_ref[...] + got_ref[...].astype(jnp.float32)).astype(jnp.bfloat16)


def three_sum_kernel(keep_a, got_a, far_a, keep_b, got_b, far_b, send_ref, held_ref):
    half = keep_a.shape[0] // 2
    for i, (keep, got, far) in enumerate(((keep_a, got_a, far_a), (keep_b, got_b, far_b))):
        rows = slice(i * half, (i + 1) * half)
        total = keep[...] + got[...].astype(jnp.float32) + far[...].astype(jnp.float32)
        held_ref[rows, :] = total[:half]
        send_ref[rows, :] = total[half:].astype(jnp.bfloat16)


def first_sum_kernel(keep_ref, got_ref, send_ref, held_ref):
    half = held_ref.shape[0]
    held_ref[...] = keep_ref[:half] + got_ref[:half].astype(jnp.float32)
    send_ref[...] = (keep_ref[half:] + got_ref[half:].astype(jnp.float32)).astype(jnp.bfloat16)


def second_sum_kernel(keep_a, got_a, keep_b, got_b, send_ref, held_ref):
    half = keep_a.shape[0] // 2
    for i, (keep, got) in enumerate(((keep_a, got_a), (keep_b, got_b))):
        rows = slice(i * half, (i + 1) * half)
        held_ref[rows, :] = keep[:half] + got[:half].astype(jnp.float32)
        send_ref[rows, :] = (keep[half:] + got[half:].astype(jnp.float32)).astype(jnp.bfloat16)


def last_sum_kernel(keep_ref, got_ref, out_ref):
    out_ref[...] = (keep_ref[...] + got_ref[...].astype(jnp.float32)).astype(jnp.bfloat16)


def swap(block, distance):
    count = lax.axis_size("expert")
    return lax.ppermute(block, "expert", [(i, i ^ distance) for i in range(count)])


def swap_core(block):
    return lax.ppermute(block, "tensor", [(0, 1), (1, 0)])


def halves(own, far):
    half = own.shape[0] // 2
    return [jnp.concatenate([own[i : i + half], far[i : i + half]]) for i in (0, half)]


def spread(a1, b1, a2, b2):
    a3, b3 = swap(a1, Y), swap(b1, X)
    a4, b4 = swap(a2, Y), swap(b2, X)
    return a1, b1, a2, b2, a3, b3, a4, b4


def send_back(one, two):
    send_a, send_b, keep_a, keep_b = one
    a4, b4, a3, b3, a2, b2, a1, b1 = two
    half = jax.ShapeDtypeStruct(a1.shape, jnp.bfloat16)
    held = jax.ShapeDtypeStruct(a1.shape, jnp.float32)
    size = a1.size
    got_a, got_b = swap(send_a, Y), swap(send_b, X)
    got_a4, got_b4 = swap(a4, Y), swap(b4, X)
    next_a, held_a = call(first_sum_kernel, (half, held), (keep_a, got_a), 8, size, 18 * size)
    next_b, held_b = call(first_sum_kernel, (half, held), (keep_b, got_b), 8, size, 18 * size)
    next_a, next_b, a2, b2, a3, b3 = lax.optimization_barrier((next_a, next_b, a2, b2, a3, b3))
    far_a, far_b = swap(next_a, X), swap(next_b, Y)
    next_z, held_z = call(
        second_sum_kernel, (half, held), (held_a, far_a, held_b, far_b), 8, size, 18 * size
    )
    next_a2 = call(part_sum_kernel, half, (a2, got_a4), 4, size, 8 * size)
    next_b2 = call(part_sum_kernel, half, (b2, got_b4), 4, size, 8 * size)
    got_a3, got_b3 = swap(a3, Y), swap(b3, X)
    far_a2, far_b2 = swap(next_a2, X), swap(next_b2, Y)
    got_z = swap(next_z, Z_HIGH)
    got_z, far_a2, far_b2 = lax.optimization_barrier((got_z, far_a2, far_b2))
    next_z2, held_z2 = call(
        three_sum_kernel, (half, held), (a1, got_a3, far_a2, b1, got_b3, far_b2), 8, size, 22 * size
    )
    got_z2 = swap(next_z2, Z_HIGH)
    return (
        call(last_sum_kernel, half, (held_z, got_z), 4, size, 8 * size),
        call(last_sum_kernel, half, (held_z2, got_z2), 4, size, 8 * size),
    )


def local_pairs(
    batch_one,
    batch_two,
    norm_gain,
    slots_one,
    slots_two,
    gates_one,
    gates_two,
    table_old,
    table_new,
    gate_old,
    up_old,
    down_old,
):
    group = table_old.shape[0]
    tok, width = batch_one.shape
    ff = gate_old.shape[2]
    gate, up, down = gate_old[0], up_old[0], down_old[0]
    held = (
        norm_gain, batch_one, batch_two, slots_one.T, slots_two.T, gates_one.T, gates_two.T,
        table_old, table_new,
    )
    hbm = pl.BlockSpec(memory_space=pltpu.HBM)
    own = call(
        prepare_kernel,
        (jax.ShapeDtypeStruct((tok, width + PACK), jnp.bfloat16),) * 2,
        held,
        59,
        10 * tok * width,
        8 * tok * width,
        [(pltpu.SMEM if x.ndim == 1 and x.dtype == jnp.int32 else pltpu.VMEM)(x.shape, x.dtype) for x in held]
        + [pltpu.SemaphoreType.DMA((len(held),))],
        [hbm] * len(held),
    )
    half_down = jax.ShapeDtypeStruct((ff // 2, down.shape[1]), jnp.bfloat16)
    down_first, down_last = call(
        halve_kernel,
        (half_down, half_down),
        (down,),
        59,
        0,
        4 * down.size,
        [pltpu.SemaphoreType.DMA((2,))],
        [hbm],
    )
    own, gate, up = lax.optimization_barrier((own, gate, up))
    both = call(
        pack_kernel,
        jax.ShapeDtypeStruct((gate.shape[0], 2 * ff), jnp.bfloat16),
        (gate, up),
        16,
        0,
        8 * gate.size,
        [pltpu.SemaphoreType.DMA((2,))],
        [hbm] * 2,
    )
    by_first = swap(down_first, Z_LOW)
    twins = (swap_core(both), swap_core(down))
    far = [swap(x, Z_HIGH) for x in own]
    far[0], by_first, both_later = lax.optimization_barrier((far[0], by_first, both))
    both_by = swap(both_later, Z_LOW)
    first_one = halves(own[0], far[0])
    second_one = swap(first_one[0], X), swap(first_one[1], Y)
    far[1], second_one, twins = lax.optimization_barrier((far[1], second_one, twins))
    first_two = halves(own[1], far[1])
    second_two = swap(first_two[0], X), swap(first_two[1], Y)
    a1, b1, a2, b2, a3, b3, a4, b4 = spread(*first_one, *second_one)
    pieces_one = [a3, a4, b3, b4, a1, a2, b1, b2]
    a1, b1, a2, b2, a3, b3, a4, b4 = spread(*first_two, *second_two)
    pieces_one, a3, b3 = lax.optimization_barrier((pieces_one, a3, b3))
    pieces = [pieces_one, [a4, b4, a3, b3, a2, b2, a1, b1]]

    rows = 8 * tok
    scratch = (pltpu.VMEM((rows, width + PACK), jnp.bfloat16),)

    def own_total(p):
        return call(
            functools.partial(own_kernel, 8, group),
            jax.ShapeDtypeStruct((rows, width), jnp.float32),
            (*p, both, twins[0], down, twins[1]),
            20,
            0,
            6 * width * ff + 6 * rows * width,
            scratch,
        )

    def beside_hidden(p):
        return call(
            functools.partial(beside_kernel, 8, group),
            (
                jax.ShapeDtypeStruct((rows, ff), jnp.bfloat16),
                jax.ShapeDtypeStruct((rows, PACK), jnp.float32),
            ),
            (*p, both_by, both_twin),
            16,
            4 * rows * width * ff,
            4 * width * ff + 2 * rows * width,
            scratch,
        )

    def join(total, hid, weight, per):
        count = rows // 2 // per
        return call(
            join_kernel,
            (jax.ShapeDtypeStruct((count, width), jnp.bfloat16),) * per
            + (jax.ShapeDtypeStruct((count, width), jnp.float32),) * per,
            (hid, weight, total, *down_by),
            14,
            2 * rows * width * ff,
            2 * width * ff + 8 * rows * width,
        )

    total_one, total_two = own_total(pieces[0]), own_total(pieces[1])
    down_last, far[1] = lax.optimization_barrier((down_last, far[1]))
    by_last = swap(down_last, Z_LOW)
    both_by, total_one, total_two = lax.optimization_barrier((both_by, total_one, total_two))
    twin_first = swap_core(by_first)
    both_twin = swap_core(both_by)
    hidden_one, hidden_two = beside_hidden(pieces[0]), beside_hidden(pieces[1])
    by_last, twin_first, total_two, hidden_one, hidden_two = lax.optimization_barrier(
        (by_last, twin_first, total_two, hidden_one, hidden_two)
    )
    down_by = (by_first, by_last, twin_first, swap_core(by_last))
    return send_back(join(total_one, *hidden_one, 2), join(total_two, *hidden_two, 4))


def solution(mesh):
    in_specs = (
        P(("expert", "tensor"), None),
        P(("expert", "tensor"), None),
        P(),
        P(("expert", "tensor"), None),
        P(("expert", "tensor"), None),
        P(("expert", "tensor"), None),
        P(("expert", "tensor"), None),
        P(),
        P(),
        P("expert", "tensor", None),
        P("expert", "tensor", None),
        P("expert", None, "tensor"),
    )
    out_specs = (P(("expert", "tensor"), None), P(("expert", "tensor"), None))
    local = local_pairs if (mesh.shape["expert"], mesh.shape["tensor"]) == (16, 2) else local_any
    return jax.shard_map(local, mesh=mesh, in_specs=in_specs, out_specs=out_specs, check_vma=False)
```

```python
import functools

import jax
import jax.numpy as jnp
from jax import lax
from jax.experimental import pallas as pl
from jax.experimental.pallas import tpu as pltpu
from jax.sharding import PartitionSpec as P

EPS = 1e-05
PACK = 128
X, Y, Z_LOW, Z_HIGH = 1, 2, 4, 8


def rms_rows(tokens, norm_gain):
    values = tokens.astype(jnp.float32)
    square = jnp.mean(values * values, axis=-1, keepdims=True)
    return (values * lax.rsqrt(square + EPS) * norm_gain.astype(jnp.float32)).astype(jnp.bfloat16)


def source_slots(table_old, table_new):
    group = table_old.shape[0]
    slot_index = jnp.arange(group, dtype=jnp.int32)
    picked = jnp.where(
        table_new == jnp.roll(table_old, 1), (slot_index - 1) % group, (slot_index + 1) % group
    )
    return jnp.where(table_new == table_old, slot_index, picked).astype(jnp.int32)


def slot_weights(route_slots, route_gates, held_by):
    group = held_by.shape[0]
    hit = route_slots[:, :, None] == jnp.arange(group, dtype=jnp.int32)
    by_slot = jnp.sum(jnp.where(hit, route_gates[:, :, None], 0.0), axis=1)
    moved = held_by[:, None] == jnp.arange(group, dtype=jnp.int32)
    return jnp.sum(jnp.where(moved[None], by_slot[:, :, None], 0.0), axis=1)


def expert_part(rows, weight, gate_full, up_full, down_full):
    gate_act = jnp.dot(rows, gate_full, preferred_element_type=jnp.float32)
    up_act = jnp.dot(rows, up_full, preferred_element_type=jnp.float32)
    hidden = (jax.nn.silu(gate_act) * up_act).astype(jnp.bfloat16)
    result = jnp.dot(hidden, down_full, preferred_element_type=jnp.float32)
    return (result * weight[:, None]).astype(jnp.bfloat16)


def local_any(
    batch_one,
    batch_two,
    norm_gain,
    slots_one,
    slots_two,
    gates_one,
    gates_two,
    table_old,
    table_new,
    gate_old,
    up_old,
    down_old,
):
    group = table_old.shape[0]
    me = lax.axis_index("expert")
    gate_full = lax.all_gather(gate_old[0], "tensor", axis=0, tiled=True)
    up_full = lax.all_gather(up_old[0], "tensor", axis=0, tiled=True)
    down_full = lax.all_gather(down_old[0], "tensor", axis=1, tiled=True)
    rows_one = lax.all_gather(rms_rows(batch_one, norm_gain), "expert", axis=0, tiled=True)
    rows_two = lax.all_gather(rms_rows(batch_two, norm_gain), "expert", axis=0, tiled=True)
    own = jnp.arange(group, dtype=jnp.int32)
    weights = jnp.stack(
        [
            slot_weights(slots_one, gates_one, own),
            slot_weights(slots_two, gates_two, source_slots(table_old, table_new)),
        ]
    )
    all_weights = lax.all_gather(weights, "expert", axis=1, tiled=True)
    mine = lax.dynamic_index_in_dim(all_weights, me, axis=2, keepdims=False)
    outs = []
    for rows, weight in ((rows_one, mine[0]), (rows_two, mine[1])):
        part = expert_part(rows, weight, gate_full, up_full, down_full)
        outs.append(lax.psum_scatter(part, "expert", scatter_dimension=0, tiled=True))
    return tuple(outs)


def call(body, outs, ins, vmem_mb, flops=0, moved=0, scratch=(), specs=None):
    smem = pl.BlockSpec(memory_space=pltpu.SMEM)
    vmem = pl.BlockSpec(memory_space=pltpu.VMEM)
    return pl.pallas_call(
        body,
        out_shape=outs,
        in_specs=specs
        or [smem if x.ndim == 1 and x.dtype == jnp.int32 else vmem for x in ins],
        out_specs=jax.tree.map(lambda _: vmem, outs),
        scratch_shapes=list(scratch),
        compiler_params=pltpu.CompilerParams(vmem_limit_bytes=vmem_mb * 1024 * 1024),
        cost_estimate=pl.CostEstimate(flops=flops, bytes_accessed=moved, transcendentals=0),
    )(*ins)


def prepare_kernel(*refs):
    hbm, outs, held, sems = refs[:9], refs[9:11], refs[11:20], refs[20]
    copies = [pltpu.make_async_copy(a, b, sems.at[i]) for i, (a, b) in enumerate(zip(hbm, held))]
    for copy in copies:
        copy.start()
    for copy in copies:
        copy.wait()
    old_ref, new_ref = held[7:]
    group = old_ref.shape[0]
    sources = []
    for s in range(group):
        left, right = (s - 1) % group, (s + 1) % group
        wanted = new_ref[s]
        other = jnp.where(wanted == old_ref[left], left, right)
        sources.append(jnp.where(wanted == old_ref[s], s, other))
    gain = held[0][...].astype(jnp.float32).reshape(1, -1)
    for b in range(2):
        tokens_ref, slots_ref, gates_ref = held[1 + b], held[3 + b], held[5 + b]
        out_ref = outs[b]
        tok, width = tokens_ref.shape
        values = tokens_ref[...].astype(jnp.float32)
        square = jnp.mean(values * values, axis=-1, keepdims=True)
        out_ref[:, :width] = (values * lax.rsqrt(square + EPS) * gain).astype(jnp.bfloat16)
        slots, gates = slots_ref[...], gates_ref[...]
        if b == 1:
            holder = jnp.zeros_like(slots)
            for s in range(group):
                holder = jnp.where(slots == s, sources[s], holder)
            slots = holder
        expert = lax.broadcasted_iota(jnp.int32, (group, tok), 0)
        total = jnp.zeros((group, tok), jnp.float32)
        for k in range(slots.shape[0]):
            total += jnp.where(expert == slots[k : k + 1, :], gates[k : k + 1, :], 0.0)
        high = total.astype(jnp.bfloat16)
        rest = total - high.astype(jnp.float32)
        middle = rest.astype(jnp.bfloat16)
        low = (rest - middle.astype(jnp.float32)).astype(jnp.bfloat16)
        packed = jnp.concatenate([high, middle, low], axis=0)
        row = lax.broadcasted_iota(jnp.int32, (3 * group, PACK), 0)
        lane = lax.broadcasted_iota(jnp.int32, (3 * group, PACK), 1)
        turned = lax.dot_general(
            packed,
            (row == lane).astype(jnp.bfloat16),
            (((0,), (0,)), ((), ())),
            preferred_element_type=jnp.float32,
        )
        out_ref[:, width:] = turned.astype(jnp.bfloat16)


def halve_kernel(whole_ref, first_ref, last_ref, sems):
    half = first_ref.shape[0]
    copies = [
        pltpu.make_async_copy(whole_ref.at[:half, :], first_ref, sems.at[0]),
        pltpu.make_async_copy(whole_ref.at[half:, :], last_ref, sems.at[1]),
    ]
    for copy in copies:
        copy.start()
    for copy in copies:
        copy.wait()


def pack_kernel(gate_ref, up_ref, both_ref, sems):
    ff = gate_ref.shape[1]
    copies = [
        pltpu.make_async_copy(gate_ref, both_ref.at[:, :ff], sems.at[0]),
        pltpu.make_async_copy(up_ref, both_ref.at[:, ff:], sems.at[1]),
    ]
    for copy in copies:
        copy.start()
    for copy in copies:
        copy.wait()


def hidden_of(place, rows_ref, both_refs, begin, count):
    depth, ff = both_refs[0].shape[0], both_refs[0].shape[1] // 2
    acts = None
    for which, ref in enumerate(both_refs):
        half = place if which == 0 else 1 - place
        columns = pl.ds(pl.multiple_of(half * depth, depth), depth)
        rows = rows_ref[pl.ds(begin, count), columns]
        term = jnp.dot(rows, ref[...], preferred_element_type=jnp.float32)
        acts = term if acts is None else acts + term
    gate_act, up_act = acts[:, :ff], acts[:, ff:]
    return (gate_act / (1.0 + jnp.exp(-gate_act)) * up_act).astype(jnp.bfloat16)


def weight_of(expert, group, packed):
    lane = lax.broadcasted_iota(jnp.int32, packed.shape, 1)
    chosen = (lane & (group - 1)) == expert
    return jnp.sum(jnp.where(chosen, packed.astype(jnp.float32), 0.0), axis=1, keepdims=True)


def own_kernel(pieces, group, *refs):
    piece_refs, refs = refs[:pieces], refs[pieces:]
    both_a, both_b, down_a, down_b, total_ref, rows_ref = refs
    tok = piece_refs[0].shape[0]
    width = total_ref.shape[1]
    for i, ref in enumerate(piece_refs):
        rows_ref[i * tok : (i + 1) * tok, :] = ref[...]
    place, expert = lax.axis_index("tensor"), lax.axis_index("expert")
    block = 256

    @pl.loop(0, rows_ref.shape[0] // block)
    def _(step):
        begin = pl.multiple_of(step * block, block)
        hidden = hidden_of(place, rows_ref, (both_a, both_b), begin, block)
        weight = weight_of(expert, group, rows_ref[pl.ds(begin, block), width:])
        for which, ref in enumerate((down_a, down_b)):
            half = place if which == 0 else 1 - place
            columns = pl.ds(pl.multiple_of(half * ref.shape[1], ref.shape[1]), ref.shape[1])
            part = jnp.dot(hidden, ref[...], preferred_element_type=jnp.float32)
            total_ref[pl.ds(begin, block), columns] = part * weight


def beside_kernel(pieces, group, *refs):
    piece_refs, refs = refs[:pieces], refs[pieces:]
    both_a, both_b, hidden_ref, weight_ref, rows_ref = refs
    tok = piece_refs[0].shape[0]
    width = rows_ref.shape[1] - PACK
    for i, ref in enumerate(piece_refs):
        rows_ref[i * tok : (i + 1) * tok, :] = ref[...]
    place, expert = lax.axis_index("tensor"), lax.axis_index("expert") ^ Z_LOW
    block = 256

    @pl.loop(0, rows_ref.shape[0] // block)
    def _(step):
        begin = pl.multiple_of(step * block, block)
        hidden_ref[pl.ds(begin, block), :] = hidden_of(
            place, rows_ref, (both_a, both_b), begin, block
        )
        weight = weight_of(expert, group, rows_ref[pl.ds(begin, block), width:])
        weight_ref[pl.ds(begin, block), :] = jnp.broadcast_to(weight, (block, PACK))


def join_kernel(hidden_ref, weight_ref, total_ref, first_a, last_a, first_b, last_b, *outs):
    place = lax.axis_index("tensor")
    inner, width = first_a.shape
    per, count = len(outs) // 2, outs[0].shape[0]
    for part in range(2):
        rows = slice(part * per * count, (part + 1) * per * count)
        weight = weight_ref[rows, :1]
        for which, (first, last) in enumerate(((first_a, last_a), (first_b, last_b))):
            half = place if which == 0 else 1 - place
            columns = pl.ds(pl.multiple_of(half * width, width), width)
            result = jnp.dot(
                hidden_ref[rows, :inner], first[...], preferred_element_type=jnp.float32
            ) + jnp.dot(hidden_ref[rows, inner:], last[...], preferred_element_type=jnp.float32)
            result = result * weight + total_ref[rows, columns]
            for i, out in enumerate(outs[per * part : per * (part + 1)]):
                out[:, columns] = result[i * count : (i + 1) * count].astype(out.dtype)


def part_sum_kernel(keep_ref, got_ref, send_ref):
    send_ref[...] = (keep_ref[...] + got_ref[...].astype(jnp.float32)).astype(jnp.bfloat16)


def three_sum_kernel(keep_a, got_a, far_a, keep_b, got_b, far_b, send_ref, held_ref):
    half = keep_a.shape[0] // 2
    for i, (keep, got, far) in enumerate(((keep_a, got_a, far_a), (keep_b, got_b, far_b))):
        rows = slice(i * half, (i + 1) * half)
        total = keep[...] + got[...].astype(jnp.float32) + far[...].astype(jnp.float32)
        held_ref[rows, :] = total[:half]
        send_ref[rows, :] = total[half:].astype(jnp.bfloat16)


def first_sum_kernel(keep_ref, got_ref, send_ref, held_ref):
    half = held_ref.shape[0]
    held_ref[...] = keep_ref[:half] + got_ref[:half].astype(jnp.float32)
    send_ref[...] = (keep_ref[half:] + got_ref[half:].astype(jnp.float32)).astype(jnp.bfloat16)


def second_sum_kernel(keep_a, got_a, keep_b, got_b, send_ref, held_ref):
    half = keep_a.shape[0] // 2
    for i, (keep, got) in enumerate(((keep_a, got_a), (keep_b, got_b))):
        rows = slice(i * half, (i + 1) * half)
        held_ref[rows, :] = keep[:half] + got[:half].astype(jnp.float32)
        send_ref[rows, :] = (keep[half:] + got[half:].astype(jnp.float32)).astype(jnp.bfloat16)


def last_sum_kernel(keep_ref, got_ref, out_ref):
    out_ref[...] = (keep_ref[...] + got_ref[...].astype(jnp.float32)).astype(jnp.bfloat16)


def swap(block, distance):
    count = lax.axis_size("expert")
    return lax.ppermute(block, "expert", [(i, i ^ distance) for i in range(count)])


def swap_core(block):
    return lax.ppermute(block, "tensor", [(0, 1), (1, 0)])


def halves(own, far):
    half = own.shape[0] // 2
    return [jnp.concatenate([own[i : i + half], far[i : i + half]]) for i in (0, half)]


def spread(a1, b1, a2, b2):
    a3, b3 = swap(a1, Y), swap(b1, X)
    a4, b4 = swap(a2, Y), swap(b2, X)
    return a1, b1, a2, b2, a3, b3, a4, b4


def send_back(one, two):
    send_a, send_b, keep_a, keep_b = one
    a4, b4, a3, b3, a2, b2, a1, b1 = two
    half = jax.ShapeDtypeStruct(a1.shape, jnp.bfloat16)
    held = jax.ShapeDtypeStruct(a1.shape, jnp.float32)
    size = a1.size
    got_a, got_b = swap(send_a, Y), swap(send_b, X)
    got_a4, got_b4 = swap(a4, Y), swap(b4, X)
    next_a, held_a = call(first_sum_kernel, (half, held), (keep_a, got_a), 8, size, 18 * size)
    next_b, held_b = call(first_sum_kernel, (half, held), (keep_b, got_b), 8, size, 18 * size)
    next_a, next_b, a2, b2, a3, b3 = lax.optimization_barrier((next_a, next_b, a2, b2, a3, b3))
    far_a, far_b = swap(next_a, X), swap(next_b, Y)
    next_z, held_z = call(
        second_sum_kernel, (half, held), (held_a, far_a, held_b, far_b), 8, size, 18 * size
    )
    next_a2 = call(part_sum_kernel, half, (a2, got_a4), 4, size, 8 * size)
    next_b2 = call(part_sum_kernel, half, (b2, got_b4), 4, size, 8 * size)
    got_a3, got_b3 = swap(a3, Y), swap(b3, X)
    far_a2, far_b2 = swap(next_a2, X), swap(next_b2, Y)
    got_z = swap(next_z, Z_HIGH)
    got_z, far_a2, far_b2 = lax.optimization_barrier((got_z, far_a2, far_b2))
    next_z2, held_z2 = call(
        three_sum_kernel, (half, held), (a1, got_a3, far_a2, b1, got_b3, far_b2), 8, size, 22 * size
    )
    got_z2 = swap(next_z2, Z_HIGH)
    return (
        call(last_sum_kernel, half, (held_z, got_z), 4, size, 8 * size),
        call(last_sum_kernel, half, (held_z2, got_z2), 4, size, 8 * size),
    )


def local_pairs(
    batch_one,
    batch_two,
    norm_gain,
    slots_one,
    slots_two,
    gates_one,
    gates_two,
    table_old,
    table_new,
    gate_old,
    up_old,
    down_old,
):
    group = table_old.shape[0]
    tok, width = batch_one.shape
    ff = gate_old.shape[2]
    gate, up, down = gate_old[0], up_old[0], down_old[0]
    held = (
        norm_gain, batch_one, batch_two, slots_one.T, slots_two.T, gates_one.T, gates_two.T,
        table_old, table_new,
    )
    hbm = pl.BlockSpec(memory_space=pltpu.HBM)
    own = call(
        prepare_kernel,
        (jax.ShapeDtypeStruct((tok, width + PACK), jnp.bfloat16),) * 2,
        held,
        59,
        10 * tok * width,
        8 * tok * width,
        [(pltpu.SMEM if x.ndim == 1 and x.dtype == jnp.int32 else pltpu.VMEM)(x.shape, x.dtype) for x in held]
        + [pltpu.SemaphoreType.DMA((len(held),))],
        [hbm] * len(held),
    )
    half_down = jax.ShapeDtypeStruct((ff // 2, down.shape[1]), jnp.bfloat16)
    down_first, down_last = call(
        halve_kernel,
        (half_down, half_down),
        (down,),
        59,
        0,
        4 * down.size,
        [pltpu.SemaphoreType.DMA((2,))],
        [hbm],
    )
    own, gate, up = lax.optimization_barrier((own, gate, up))
    both = call(
        pack_kernel,
        jax.ShapeDtypeStruct((gate.shape[0], 2 * ff), jnp.bfloat16),
        (gate, up),
        16,
        0,
        8 * gate.size,
        [pltpu.SemaphoreType.DMA((2,))],
        [hbm] * 2,
    )
    by_first = swap(down_first, Z_LOW)
    twins = (swap_core(both), swap_core(down))
    far = [swap(x, Z_HIGH) for x in own]
    far[0], both_later = lax.optimization_barrier((far[0], both))
    both_by = swap(both_later, Z_LOW)
    first_one = halves(own[0], far[0])
    second_one = swap(first_one[0], X), swap(first_one[1], Y)
    far[1], second_one, twins, by_first = lax.optimization_barrier(
        (far[1], second_one, twins, by_first)
    )
    first_two = halves(own[1], far[1])
    second_two = swap(first_two[0], X), swap(first_two[1], Y)
    a1, b1, a2, b2, a3, b3, a4, b4 = spread(*first_one, *second_one)
    pieces_one = [a3, a4, b3, b4, a1, a2, b1, b2]
    a1, b1, a2, b2, a3, b3, a4, b4 = spread(*first_two, *second_two)
    pieces_one, a3, b3 = lax.optimization_barrier((pieces_one, a3, b3))
    pieces = [pieces_one, [a4, b4, a3, b3, a2, b2, a1, b1]]

    rows = 8 * tok
    scratch = (pltpu.VMEM((rows, width + PACK), jnp.bfloat16),)

    def own_total(p):
        return call(
            functools.partial(own_kernel, 8, group),
            jax.ShapeDtypeStruct((rows, width), jnp.float32),
            (*p, both, twins[0], down, twins[1]),
            20,
            0,
            6 * width * ff + 6 * rows * width,
            scratch,
        )

    def beside_hidden(p):
        return call(
            functools.partial(beside_kernel, 8, group),
            (
                jax.ShapeDtypeStruct((rows, ff), jnp.bfloat16),
                jax.ShapeDtypeStruct((rows, PACK), jnp.float32),
            ),
            (*p, both_by, both_twin),
            16,
            4 * rows * width * ff,
            4 * width * ff + 2 * rows * width,
            scratch,
        )

    def join(total, hid, weight, per):
        count = rows // 2 // per
        return call(
            join_kernel,
            (jax.ShapeDtypeStruct((count, width), jnp.bfloat16),) * per
            + (jax.ShapeDtypeStruct((count, width), jnp.float32),) * per,
            (hid, weight, total, *down_by),
            14,
            2 * rows * width * ff,
            2 * width * ff + 8 * rows * width,
        )

    total_one, total_two = own_total(pieces[0]), own_total(pieces[1])
    down_last, far[1] = lax.optimization_barrier((down_last, far[1]))
    by_last = swap(down_last, Z_LOW)
    both_by, total_one, total_two = lax.optimization_barrier((both_by, total_one, total_two))
    twin_first = swap_core(by_first)
    both_twin = swap_core(both_by)
    hidden_one, hidden_two = beside_hidden(pieces[0]), beside_hidden(pieces[1])
    by_last, twin_first, total_two, hidden_one, hidden_two = lax.optimization_barrier(
        (by_last, twin_first, total_two, hidden_one, hidden_two)
    )
    down_by = (by_first, by_last, twin_first, swap_core(by_last))
    return send_back(join(total_one, *hidden_one, 2), join(total_two, *hidden_two, 4))


def solution(mesh):
    in_specs = (
        P(("expert", "tensor"), None),
        P(("expert", "tensor"), None),
        P(),
        P(("expert", "tensor"), None),
        P(("expert", "tensor"), None),
        P(("expert", "tensor"), None),
        P(("expert", "tensor"), None),
        P(),
        P(),
        P("expert", "tensor", None),
        P("expert", "tensor", None),
        P("expert", None, "tensor"),
    )
    out_specs = (P(("expert", "tensor"), None), P(("expert", "tensor"), None))
    local = local_pairs if (mesh.shape["expert"], mesh.shape["tensor"]) == (16, 2) else local_any
    return jax.shard_map(local, mesh=mesh, in_specs=in_specs, out_specs=out_specs, check_vma=False)
```

```python
import functools

import jax
import jax.numpy as jnp
from jax import lax
from jax.experimental import pallas as pl
from jax.experimental.pallas import tpu as pltpu
from jax.sharding import PartitionSpec as P

EPS = 1e-05
PACK = 128
X, Y, Z_LOW, Z_HIGH = 1, 2, 4, 8


def rms_rows(tokens, norm_gain):
    values = tokens.astype(jnp.float32)
    square = jnp.mean(values * values, axis=-1, keepdims=True)
    return (values * lax.rsqrt(square + EPS) * norm_gain.astype(jnp.float32)).astype(jnp.bfloat16)


def source_slots(table_old, table_new):
    group = table_old.shape[0]
    slot_index = jnp.arange(group, dtype=jnp.int32)
    picked = jnp.where(
        table_new == jnp.roll(table_old, 1), (slot_index - 1) % group, (slot_index + 1) % group
    )
    return jnp.where(table_new == table_old, slot_index, picked).astype(jnp.int32)


def slot_weights(route_slots, route_gates, held_by):
    group = held_by.shape[0]
    hit = route_slots[:, :, None] == jnp.arange(group, dtype=jnp.int32)
    by_slot = jnp.sum(jnp.where(hit, route_gates[:, :, None], 0.0), axis=1)
    moved = held_by[:, None] == jnp.arange(group, dtype=jnp.int32)
    return jnp.sum(jnp.where(moved[None], by_slot[:, :, None], 0.0), axis=1)


def expert_part(rows, weight, gate_full, up_full, down_full):
    gate_act = jnp.dot(rows, gate_full, preferred_element_type=jnp.float32)
    up_act = jnp.dot(rows, up_full, preferred_element_type=jnp.float32)
    hidden = (jax.nn.silu(gate_act) * up_act).astype(jnp.bfloat16)
    result = jnp.dot(hidden, down_full, preferred_element_type=jnp.float32)
    return (result * weight[:, None]).astype(jnp.bfloat16)


def local_any(
    batch_one,
    batch_two,
    norm_gain,
    slots_one,
    slots_two,
    gates_one,
    gates_two,
    table_old,
    table_new,
    gate_old,
    up_old,
    down_old,
):
    group = table_old.shape[0]
    me = lax.axis_index("expert")
    gate_full = lax.all_gather(gate_old[0], "tensor", axis=0, tiled=True)
    up_full = lax.all_gather(up_old[0], "tensor", axis=0, tiled=True)
    down_full = lax.all_gather(down_old[0], "tensor", axis=1, tiled=True)
    rows_one = lax.all_gather(rms_rows(batch_one, norm_gain), "expert", axis=0, tiled=True)
    rows_two = lax.all_gather(rms_rows(batch_two, norm_gain), "expert", axis=0, tiled=True)
    own = jnp.arange(group, dtype=jnp.int32)
    weights = jnp.stack(
        [
            slot_weights(slots_one, gates_one, own),
            slot_weights(slots_two, gates_two, source_slots(table_old, table_new)),
        ]
    )
    all_weights = lax.all_gather(weights, "expert", axis=1, tiled=True)
    mine = lax.dynamic_index_in_dim(all_weights, me, axis=2, keepdims=False)
    outs = []
    for rows, weight in ((rows_one, mine[0]), (rows_two, mine[1])):
        part = expert_part(rows, weight, gate_full, up_full, down_full)
        outs.append(lax.psum_scatter(part, "expert", scatter_dimension=0, tiled=True))
    return tuple(outs)


def call(body, outs, ins, vmem_mb, flops=0, moved=0, scratch=(), specs=None):
    smem = pl.BlockSpec(memory_space=pltpu.SMEM)
    vmem = pl.BlockSpec(memory_space=pltpu.VMEM)
    return pl.pallas_call(
        body,
        out_shape=outs,
        in_specs=specs
        or [smem if x.ndim == 1 and x.dtype == jnp.int32 else vmem for x in ins],
        out_specs=jax.tree.map(lambda _: vmem, outs),
        scratch_shapes=list(scratch),
        compiler_params=pltpu.CompilerParams(vmem_limit_bytes=vmem_mb * 1024 * 1024),
        cost_estimate=pl.CostEstimate(flops=flops, bytes_accessed=moved, transcendentals=0),
    )(*ins)


def prepare_kernel(*refs):
    hbm, outs, held, sems = refs[:9], refs[9:11], refs[11:20], refs[20]
    copies = [pltpu.make_async_copy(a, b, sems.at[i]) for i, (a, b) in enumerate(zip(hbm, held))]
    for copy in copies:
        copy.start()
    for copy in copies:
        copy.wait()
    old_ref, new_ref = held[7:]
    group = old_ref.shape[0]
    sources = []
    for s in range(group):
        left, right = (s - 1) % group, (s + 1) % group
        wanted = new_ref[s]
        other = jnp.where(wanted == old_ref[left], left, right)
        sources.append(jnp.where(wanted == old_ref[s], s, other))
    gain = held[0][...].astype(jnp.float32).reshape(1, -1)
    for b in range(2):
        tokens_ref, slots_ref, gates_ref = held[1 + b], held[3 + b], held[5 + b]
        out_ref = outs[b]
        tok, width = tokens_ref.shape
        values = tokens_ref[...].astype(jnp.float32)
        square = jnp.mean(values * values, axis=-1, keepdims=True)
        out_ref[:, :width] = (values * lax.rsqrt(square + EPS) * gain).astype(jnp.bfloat16)
        slots, gates = slots_ref[...], gates_ref[...]
        if b == 1:
            holder = jnp.zeros_like(slots)
            for s in range(group):
                holder = jnp.where(slots == s, sources[s], holder)
            slots = holder
        expert = lax.broadcasted_iota(jnp.int32, (group, tok), 0)
        total = jnp.zeros((group, tok), jnp.float32)
        for k in range(slots.shape[0]):
            total += jnp.where(expert == slots[k : k + 1, :], gates[k : k + 1, :], 0.0)
        high = total.astype(jnp.bfloat16)
        rest = total - high.astype(jnp.float32)
        middle = rest.astype(jnp.bfloat16)
        low = (rest - middle.astype(jnp.float32)).astype(jnp.bfloat16)
        packed = jnp.concatenate([high, middle, low], axis=0)
        row = lax.broadcasted_iota(jnp.int32, (3 * group, PACK), 0)
        lane = lax.broadcasted_iota(jnp.int32, (3 * group, PACK), 1)
        turned = lax.dot_general(
            packed,
            (row == lane).astype(jnp.bfloat16),
            (((0,), (0,)), ((), ())),
            preferred_element_type=jnp.float32,
        )
        out_ref[:, width:] = turned.astype(jnp.bfloat16)


def pack_kernel(gate_ref, up_ref, down_ref, both_ref, first_ref, last_ref, sems):
    ff, half = gate_ref.shape[1], first_ref.shape[0]
    copies = [
        pltpu.make_async_copy(down_ref.at[:half, :], first_ref, sems.at[0]),
        pltpu.make_async_copy(down_ref.at[half:, :], last_ref, sems.at[1]),
        pltpu.make_async_copy(gate_ref, both_ref.at[:, :ff], sems.at[2]),
        pltpu.make_async_copy(up_ref, both_ref.at[:, ff:], sems.at[3]),
    ]
    for copy in copies:
        copy.start()
    for copy in copies:
        copy.wait()


def hidden_of(place, rows_ref, both_refs, begin, count):
    depth, ff = both_refs[0].shape[0], both_refs[0].shape[1] // 2
    acts = None
    for which, ref in enumerate(both_refs):
        half = place if which == 0 else 1 - place
        columns = pl.ds(pl.multiple_of(half * depth, depth), depth)
        rows = rows_ref[pl.ds(begin, count), columns]
        term = jnp.dot(rows, ref[...], preferred_element_type=jnp.float32)
        acts = term if acts is None else acts + term
    gate_act, up_act = acts[:, :ff], acts[:, ff:]
    return (gate_act / (1.0 + jnp.exp(-gate_act)) * up_act).astype(jnp.bfloat16)


def weight_of(expert, group, packed):
    lane = lax.broadcasted_iota(jnp.int32, packed.shape, 1)
    chosen = (lane & (group - 1)) == expert
    return jnp.sum(jnp.where(chosen, packed.astype(jnp.float32), 0.0), axis=1, keepdims=True)


def own_kernel(pieces, group, *refs):
    piece_refs, refs = refs[:pieces], refs[pieces:]
    both_a, both_b, down_a, down_b, total_ref, rows_ref = refs
    tok = piece_refs[0].shape[0]
    width = total_ref.shape[1]
    for i, ref in enumerate(piece_refs):
        rows_ref[i * tok : (i + 1) * tok, :] = ref[...]
    place, expert = lax.axis_index("tensor"), lax.axis_index("expert")
    block = 256

    @pl.loop(0, rows_ref.shape[0] // block)
    def _(step):
        begin = pl.multiple_of(step * block, block)
        hidden = hidden_of(place, rows_ref, (both_a, both_b), begin, block)
        weight = weight_of(expert, group, rows_ref[pl.ds(begin, block), width:])
        for which, ref in enumerate((down_a, down_b)):
            half = place if which == 0 else 1 - place
            columns = pl.ds(pl.multiple_of(half * ref.shape[1], ref.shape[1]), ref.shape[1])
            part = jnp.dot(hidden, ref[...], preferred_element_type=jnp.float32)
            total_ref[pl.ds(begin, block), columns] = part * weight


def beside_kernel(pieces, group, *refs):
    piece_refs, refs = refs[:pieces], refs[pieces:]
    both_a, both_b, hidden_ref, weight_ref, rows_ref = refs
    tok = piece_refs[0].shape[0]
    width = rows_ref.shape[1] - PACK
    for i, ref in enumerate(piece_refs):
        rows_ref[i * tok : (i + 1) * tok, :] = ref[...]
    place, expert = lax.axis_index("tensor"), lax.axis_index("expert") ^ Z_LOW
    block = 256

    @pl.loop(0, rows_ref.shape[0] // block)
    def _(step):
        begin = pl.multiple_of(step * block, block)
        hidden_ref[pl.ds(begin, block), :] = hidden_of(
            place, rows_ref, (both_a, both_b), begin, block
        )
        weight = weight_of(expert, group, rows_ref[pl.ds(begin, block), width:])
        weight_ref[pl.ds(begin, block), :] = jnp.broadcast_to(weight, (block, PACK))


def join_kernel(hidden_ref, weight_ref, total_ref, first_a, last_a, first_b, last_b, *outs):
    place = lax.axis_index("tensor")
    inner, width = first_a.shape
    per, count = len(outs) // 2, outs[0].shape[0]
    for part in range(2):
        rows = slice(part * per * count, (part + 1) * per * count)
        weight = weight_ref[rows, :1]
        for which, (first, last) in enumerate(((first_a, last_a), (first_b, last_b))):
            half = place if which == 0 else 1 - place
            columns = pl.ds(pl.multiple_of(half * width, width), width)
            result = jnp.dot(
                hidden_ref[rows, :inner], first[...], preferred_element_type=jnp.float32
            ) + jnp.dot(hidden_ref[rows, inner:], last[...], preferred_element_type=jnp.float32)
            result = result * weight + total_ref[rows, columns]
            for i, out in enumerate(outs[per * part : per * (part + 1)]):
                out[:, columns] = result[i * count : (i + 1) * count].astype(out.dtype)


def part_sum_kernel(keep_ref, got_ref, send_ref):
    send_ref[...] = (keep_ref[...] + got_ref[...].astype(jnp.float32)).astype(jnp.bfloat16)


def three_sum_kernel(keep_a, got_a, far_a, keep_b, got_b, far_b, send_ref, held_ref):
    half = keep_a.shape[0] // 2
    for i, (keep, got, far) in enumerate(((keep_a, got_a, far_a), (keep_b, got_b, far_b))):
        rows = slice(i * half, (i + 1) * half)
        total = keep[...] + got[...].astype(jnp.float32) + far[...].astype(jnp.float32)
        held_ref[rows, :] = total[:half]
        send_ref[rows, :] = total[half:].astype(jnp.bfloat16)


def first_sum_kernel(keep_ref, got_ref, send_ref, held_ref):
    half = held_ref.shape[0]
    held_ref[...] = keep_ref[:half] + got_ref[:half].astype(jnp.float32)
    send_ref[...] = (keep_ref[half:] + got_ref[half:].astype(jnp.float32)).astype(jnp.bfloat16)


def second_sum_kernel(keep_a, got_a, keep_b, got_b, send_ref, held_ref):
    half = keep_a.shape[0] // 2
    for i, (keep, got) in enumerate(((keep_a, got_a), (keep_b, got_b))):
        rows = slice(i * half, (i + 1) * half)
        held_ref[rows, :] = keep[:half] + got[:half].astype(jnp.float32)
        send_ref[rows, :] = (keep[half:] + got[half:].astype(jnp.float32)).astype(jnp.bfloat16)


def last_sum_kernel(keep_ref, got_ref, out_ref):
    out_ref[...] = (keep_ref[...] + got_ref[...].astype(jnp.float32)).astype(jnp.bfloat16)


def swap(block, distance):
    count = lax.axis_size("expert")
    return lax.ppermute(block, "expert", [(i, i ^ distance) for i in range(count)])


def swap_core(block):
    return lax.ppermute(block, "tensor", [(0, 1), (1, 0)])


def halves(own, far):
    half = own.shape[0] // 2
    return [jnp.concatenate([own[i : i + half], far[i : i + half]]) for i in (0, half)]


def spread(a1, b1, a2, b2):
    a3, b3 = swap(a1, Y), swap(b1, X)
    a4, b4 = swap(a2, Y), swap(b2, X)
    return a1, b1, a2, b2, a3, b3, a4, b4


def send_back(one, two):
    send_a, send_b, keep_a, keep_b = one
    a4, b4, a3, b3, a2, b2, a1, b1 = two
    half = jax.ShapeDtypeStruct(a1.shape, jnp.bfloat16)
    held = jax.ShapeDtypeStruct(a1.shape, jnp.float32)
    size = a1.size
    got_a, got_b = swap(send_a, Y), swap(send_b, X)
    got_a4, got_b4 = swap(a4, Y), swap(b4, X)
    next_a, held_a = call(first_sum_kernel, (half, held), (keep_a, got_a), 8, size, 18 * size)
    next_b, held_b = call(first_sum_kernel, (half, held), (keep_b, got_b), 8, size, 18 * size)
    next_a, next_b, a2, b2, a3, b3 = lax.optimization_barrier((next_a, next_b, a2, b2, a3, b3))
    far_a, far_b = swap(next_a, X), swap(next_b, Y)
    next_z, held_z = call(
        second_sum_kernel, (half, held), (held_a, far_a, held_b, far_b), 8, size, 18 * size
    )
    next_a2 = call(part_sum_kernel, half, (a2, got_a4), 4, size, 8 * size)
    next_b2 = call(part_sum_kernel, half, (b2, got_b4), 4, size, 8 * size)
    got_a3, got_b3 = swap(a3, Y), swap(b3, X)
    far_a2, far_b2 = swap(next_a2, X), swap(next_b2, Y)
    got_z = swap(next_z, Z_HIGH)
    got_z, far_a2, far_b2 = lax.optimization_barrier((got_z, far_a2, far_b2))
    next_z2, held_z2 = call(
        three_sum_kernel, (half, held), (a1, got_a3, far_a2, b1, got_b3, far_b2), 8, size, 22 * size
    )
    got_z2 = swap(next_z2, Z_HIGH)
    return (
        call(last_sum_kernel, half, (held_z, got_z), 4, size, 8 * size),
        call(last_sum_kernel, half, (held_z2, got_z2), 4, size, 8 * size),
    )


def local_pairs(
    batch_one,
    batch_two,
    norm_gain,
    slots_one,
    slots_two,
    gates_one,
    gates_two,
    table_old,
    table_new,
    gate_old,
    up_old,
    down_old,
):
    group = table_old.shape[0]
    tok, width = batch_one.shape
    ff = gate_old.shape[2]
    gate, up, down = gate_old[0], up_old[0], down_old[0]
    held = (
        norm_gain, batch_one, batch_two, slots_one.T, slots_two.T, gates_one.T, gates_two.T,
        table_old, table_new,
    )
    hbm = pl.BlockSpec(memory_space=pltpu.HBM)
    own = call(
        prepare_kernel,
        (jax.ShapeDtypeStruct((tok, width + PACK), jnp.bfloat16),) * 2,
        held,
        8,
        10 * tok * width,
        8 * tok * width,
        [(pltpu.SMEM if x.ndim == 1 and x.dtype == jnp.int32 else pltpu.VMEM)(x.shape, x.dtype) for x in held]
        + [pltpu.SemaphoreType.DMA((len(held),))],
        [hbm] * len(held),
    )
    half_down = jax.ShapeDtypeStruct((ff // 2, down.shape[1]), jnp.bfloat16)
    both, down_first, down_last = call(
        pack_kernel,
        (jax.ShapeDtypeStruct((gate.shape[0], 2 * ff), jnp.bfloat16), half_down, half_down),
        (gate, up, down),
        59,
        0,
        12 * gate.size,
        [pltpu.SemaphoreType.DMA((4,))],
        [hbm] * 3,
    )
    by_first = swap(down_first, Z_LOW)
    twins = (swap_core(both), swap_core(down))
    far = [swap(x, Z_HIGH) for x in own]
    far[0], twins, both_later = lax.optimization_barrier((far[0], twins, both))
    both_by = swap(both_later, Z_LOW)
    first_one = halves(own[0], far[0])
    second_one = swap(first_one[0], X), swap(first_one[1], Y)
    far[1], second_one, by_first = lax.optimization_barrier((far[1], second_one, by_first))
    first_two = halves(own[1], far[1])
    second_two = swap(first_two[0], X), swap(first_two[1], Y)
    a1, b1, a2, b2, a3, b3, a4, b4 = spread(*first_one, *second_one)
    pieces_one = [a3, a4, b3, b4, a1, a2, b1, b2]
    a1, b1, a2, b2, a3, b3, a4, b4 = spread(*first_two, *second_two)
    pieces_one, a3, b3 = lax.optimization_barrier((pieces_one, a3, b3))
    pieces = [pieces_one, [a4, b4, a3, b3, a2, b2, a1, b1]]

    rows = 8 * tok
    scratch = (pltpu.VMEM((rows, width + PACK), jnp.bfloat16),)

    def own_total(p):
        return call(
            functools.partial(own_kernel, 8, group),
            jax.ShapeDtypeStruct((rows, width), jnp.float32),
            (*p, both, twins[0], down, twins[1]),
            20,
            0,
            6 * width * ff + 6 * rows * width,
            scratch,
        )

    def beside_hidden(p):
        return call(
            functools.partial(beside_kernel, 8, group),
            (
                jax.ShapeDtypeStruct((rows, ff), jnp.bfloat16),
                jax.ShapeDtypeStruct((rows, PACK), jnp.float32),
            ),
            (*p, both_by, both_twin),
            16,
            4 * rows * width * ff,
            4 * width * ff + 2 * rows * width,
            scratch,
        )

    def join(total, hid, weight, per):
        count = rows // 2 // per
        return call(
            join_kernel,
            (jax.ShapeDtypeStruct((count, width), jnp.bfloat16),) * per
            + (jax.ShapeDtypeStruct((count, width), jnp.float32),) * per,
            (hid, weight, total, *down_by),
            14,
            2 * rows * width * ff,
            2 * width * ff + 8 * rows * width,
        )

    total_one, total_two = own_total(pieces[0]), own_total(pieces[1])
    down_last, far[1] = lax.optimization_barrier((down_last, far[1]))
    by_last = swap(down_last, Z_LOW)
    both_by, total_one, total_two = lax.optimization_barrier((both_by, total_one, total_two))
    twin_first = swap_core(by_first)
    both_twin = swap_core(both_by)
    hidden_one, hidden_two = beside_hidden(pieces[0]), beside_hidden(pieces[1])
    by_last, twin_first, total_two, hidden_one, hidden_two = lax.optimization_barrier(
        (by_last, twin_first, total_two, hidden_one, hidden_two)
    )
    down_by = (by_first, by_last, twin_first, swap_core(by_last))
    return send_back(join(total_one, *hidden_one, 2), join(total_two, *hidden_two, 4))


def solution(mesh):
    in_specs = (
        P(("expert", "tensor"), None),
        P(("expert", "tensor"), None),
        P(),
        P(("expert", "tensor"), None),
        P(("expert", "tensor"), None),
        P(("expert", "tensor"), None),
        P(("expert", "tensor"), None),
        P(),
        P(),
        P("expert", "tensor", None),
        P("expert", "tensor", None),
        P("expert", None, "tensor"),
    )
    out_specs = (P(("expert", "tensor"), None), P(("expert", "tensor"), None))
    local = local_pairs if (mesh.shape["expert"], mesh.shape["tensor"]) == (16, 2) else local_any
    return jax.shard_map(local, mesh=mesh, in_specs=in_specs, out_specs=out_specs, check_vma=False)
```
